32 devices in a mesh: cells: 8 (over z, x), chrom: 4 (over y, core).
Axes of the slice: x: 2, y: 2, z: 4, core: 2. Of those that a mesh axis runs over, the one named last changes fastest.
Arguments:
- tokens: bfloat16 [24, 1024, 1280], P('cells', 'chrom'), may hold values from -6 to 6
- cotangent: bfloat16 [24, 1024, 1280], P('cells', 'chrom'), may hold values from -6 to 6
- block_lengths: int32 [24, 8], P('cells'), may hold values from 1 to 128, 768 in all within a row
- group_ids: int32 [24], P('cells'), may hold values from 0 to 3
- group_weights: float32 [4], replicated, may hold values from 0.5 to 2
- first_gain: float32 [1280], replicated, may hold values from 0.5 to 1.5
- first_shift: float32 [1280], replicated, may hold values from -3 to 3
- query_weight: bfloat16 [1280, 1280], replicated, may hold values from -0.15625 to 0.15625
- key_weight: bfloat16 [1280, 1280], replicated, may hold values from -0.15625 to 0.15625
- value_weight: bfloat16 [1280, 1280], replicated, may hold values from -0.15625 to 0.15625
- output_weight: bfloat16 [1280, 1280], replicated, may hold values from -2.5 to 2.5
- second_gain: float32 [1280], replicated, may hold values from 0.5 to 1.5
- second_shift: float32 [1280], replicated, may hold values from -3 to 3
- up_weight: bfloat16 [1280, 5120], replicated, may hold values from -0.15625 to 0.15625
- down_weight: bfloat16 [5120, 1280], replicated, may hold values from -0.078125 to 0.078125
Outputs:
- layer_out: bfloat16 [24, 1024, 1280], P('cells', 'chrom')
- tokens_grad: float32 [24, 1024, 1280], P('cells', 'chrom')
- first_gain_grad: float32 [1280], P(('cells', 'chrom'))
- first_shift_grad: float32 [1280], P(('cells', 'chrom'))
- query_grad: float32 [1280, 1280], P(('cells', 'chrom'))
- key_grad: float32 [1280, 1280], P(('cells', 'chrom'))
- value_grad: float32 [1280, 1280], P(('cells', 'chrom'))
- output_grad: float32 [1280, 1280], P(('cells', 'chrom'))
- second_gain_grad: float32 [1280], P(('cells', 'chrom'))
- second_shift_grad: float32 [1280], P(('cells', 'chrom'))
- up_grad: float32 [1280, 5120], P(('cells', 'chrom'))
- down_grad: float32 [5120, 1280], P(('cells', 'chrom'))
- cls_mean: float32 [1280], replicated
- cls_var: float32 [1280], replicated
The draws below stay inside these ranges and needn't reach their ends.
Inputs may be any that keep to these rules, and one draw needn't show every extreme that they name: `block_lengths`: each row sums to 768 and its largest entry is 128.
All inputs are finite; a program needn't handle non-finite values.
Results may differ from the reference program's by a relative error of at most 0.025.
Values may be sent and summed in bfloat16 or wider, within the bound.
A program may use at most 384 MiB of HBM per device.

```python
import math
import jax
import jax.numpy as jnp
import numpy as np
from jax import lax

D = 1280
HEADS = 20
HEAD_DIM = 64
FF = 5120
SEQ = 1024
NBLK = 8
GROUPS = 4
CELLS = 24
BLOCK = 128
FILLED = 768


def place_ends(drawn, key, smallest, largest):
    spot = [jax.random.randint(jax.random.fold_in(key, axis), (), 0, length) for axis, length in enumerate(drawn.shape)]
    widest = drawn.shape.index(max(drawn.shape))
    beside = spot[:widest] + [(spot[widest] + 1) % drawn.shape[widest]] + spot[widest + 1:]
    return drawn.at[tuple(spot)].set(smallest).at[tuple(beside)].set(largest)


def block_scale(stream_key, shape, split, smallest, high):
    def one(dim, parts):
        heights = jax.random.uniform(jax.random.fold_in(jax.random.fold_in(stream_key, 6), dim), (parts,), jnp.float32, smallest / len(split), high / len(split))
        return jnp.repeat(jnp.exp(heights), shape[dim] // parts).reshape((-1,) + (1,) * (len(shape) - dim - 1))

    factor_of = one(*split[0])
    for cut in split[1:]:
        factor_of = factor_of * one(*cut)
    return factor_of


def split_up(number_of, total, reach, slope):
    weights = [(1 << 20) // math.isqrt(rank ** slope) + 1 for rank in range(2, number_of + 1)]
    spare, given = total - reach - (number_of - 1), [1] * (number_of - 1)
    while spare > 0:
        movable = [i for i in range(number_of - 1) if given[i] < reach]
        mass, left = sum([weights[i] for i in movable]), spare
        for i in movable:
            addition = min(reach - given[i], max(1, left * weights[i] // mass), spare)
            given[i] = given[i] + addition
            spare = spare - addition
    return np.array([reach] + given)


def ragged_sizes(rng, amount, total, most, skew):
    if amount == 2:
        one = jax.random.randint(rng, (), max(1, total - most), min(most, total - 1) + 1)
        return jnp.stack([one, total - one])
    sizes = jnp.asarray(split_up(amount, total, most, skew), jnp.int32)
    twos = (amount - 1) // 2
    source_of, sink = sizes[1:1 + 2 * twos:2], sizes[2:2 + 2 * twos:2]
    room = jnp.minimum(source_of - 1, most - sink)
    moved = jax.random.randint(jax.random.fold_in(rng, 1), (twos,), 0, 1 << 20) % (room + 1)
    sizes = sizes.at[1:1 + 2 * twos:2].set(source_of - moved).at[2:2 + 2 * twos:2].set(sink + moved)
    return sizes[jax.random.permutation(jax.random.fold_in(rng, 2), amount)]


def bell_draw(own_key, dims, scale, bound, split=(), kind=jnp.bfloat16):
    values = scale * jax.random.normal(own_key, dims, jnp.float32)
    if split:
        values = values * block_scale(own_key, dims, split, -0.22, 0.18)
    return jnp.clip(values, -bound, bound).astype(kind)


def setup_inputs(seed: int = 0) -> dict:
    splits = jax.random.split(jax.random.key(seed), 16)
    return {
        "tokens": bell_draw(splits[0], (CELLS, SEQ, D), 1.0, 6.0, ((0, 8), (1, 4))),
        "cotangent": bell_draw(splits[1], (CELLS, SEQ, D), 1.0, 6.0, ((0, 8), (1, 4))),
        "block_lengths": jax.vmap(lambda own: ragged_sizes(own, NBLK, FILLED, BLOCK, 2))(jax.random.split(splits[2], CELLS)).reshape((CELLS, NBLK)).astype(jnp.int32),
        "group_ids": place_ends(jax.random.randint(splits[3], (CELLS,), 0, GROUPS), jax.random.fold_in(splits[3], 1), 0, GROUPS - 1).astype(jnp.int32),
        "group_weights": jnp.clip(jnp.exp(jax.random.uniform(splits[4], (GROUPS,), jnp.float32, math.log(0.5), math.log(2.0))), 0.5, 2.0),
        "first_gain": jnp.clip(1.0 + 0.1 * jax.random.normal(splits[5], (D,), jnp.float32), 0.5, 1.5),
        "first_shift": bell_draw(splits[6], (D,), 0.5, 3.0, (), jnp.float32),
        "query_weight": bell_draw(splits[7], (D, D), D ** -0.5, 0.15625),
        "key_weight": bell_draw(splits[8], (D, D), D ** -0.5, 0.15625),
        "value_weight": bell_draw(splits[9], (D, D), D ** -0.5, 0.15625),
        "output_weight": bell_draw(splits[10], (D, D), (max(D // 256, 1)) ** -0.5, 2.5),
        "second_gain": jnp.clip(1.0 + 0.1 * jax.random.normal(splits[11], (D,), jnp.float32), 0.5, 1.5),
        "second_shift": bell_draw(splits[12], (D,), 0.5, 3.0, (), jnp.float32),
        "up_weight": bell_draw(splits[13], (D, FF), D ** -0.5, 0.15625),
        "down_weight": bell_draw(splits[14], (FF, D), FF ** -0.5, 0.078125),
    }


@jax.custom_vjp
def low(v):
    return lax.optimization_barrier(v.astype(jnp.bfloat16)).astype(jnp.float32)

@jax.custom_vjp
def low_back(v):
    return v

def low_keep(v):
    return (low(v), None)

def low_pass(kept, grad):
    return (grad,)

def back_keep(v):
    return (v, None)

def back_low(kept, grad):
    return (low(grad),)
low.defvjp(low_keep, low_pass)
low_back.defvjp(back_keep, back_low)
EPS = 1e-05

def matmul(left, right):
    return jnp.dot(left, right, precision=lax.Precision.HIGHEST)

def norm_rows(values, gain, shift):
    center = values - lax.optimization_barrier(jnp.mean(values, axis=-1, keepdims=True))
    inverse = lax.rsqrt(lax.optimization_barrier(jnp.mean(center * center, axis=-1, keepdims=True)) + EPS)
    return center * inverse * gain + shift

def cell_forward(cell_in, cell_valid, first_gain, first_shift, query_weight, key_weight, value_weight, output_weight, second_gain, second_shift, up_weight, down_weight):
    first = low(norm_rows(cell_in, first_gain, first_shift))
    query = low_back(low(matmul(first, query_weight))).reshape(SEQ, HEADS, HEAD_DIM)
    keys = low_back(low(matmul(first, key_weight))).reshape(SEQ, HEADS, HEAD_DIM)
    values = low_back(low(matmul(first, value_weight))).reshape(SEQ, HEADS, HEAD_DIM)
    scores = jnp.einsum('qhe,khe->hqk', query, keys, precision=lax.Precision.HIGHEST) * HEAD_DIM ** (-0.5)
    scores = low_back(scores)
    scores = jnp.where(cell_valid[None, None, :], scores, -1e+30)
    probs = low(jax.nn.softmax(scores, axis=-1))
    mixed = jnp.einsum('hqk,khe->qhe', probs, values, precision=lax.Precision.HIGHEST).reshape(SEQ, D)
    mixed = low_back(low(mixed))
    middle = cell_in + low_back(matmul(mixed, output_weight))
    second = low(norm_rows(middle, second_gain, second_shift))
    upper = low_back(matmul(second, up_weight))
    active = low(jax.nn.gelu(upper, approximate=False))
    return middle + low_back(matmul(active, down_weight))

def reference(tokens, cotangent, block_lengths, group_ids, group_weights, first_gain, first_shift, query_weight, key_weight, value_weight, output_weight, second_gain, second_shift, up_weight, down_weight):
    valid = (jnp.arange(BLOCK)[None, None, :] < block_lengths[:, :, None]).reshape(CELLS, SEQ)
    cell_scale = group_weights[group_ids]
    params = tuple((weight_arg.astype(jnp.float32) for weight_arg in (first_gain, first_shift, query_weight, key_weight, value_weight, output_weight, second_gain, second_shift, up_weight, down_weight)))
    inputs_full = tokens.astype(jnp.float32)
    weighted = cotangent.astype(jnp.float32) * cell_scale[:, None, None] * valid.astype(jnp.float32)[:, :, None]

    def step(totals, item):
        cell_tokens, cell_valid, cell_cot = item

        def forward(cell_in, *weights):
            return cell_forward(cell_in, cell_valid, *weights)
        result, pull = jax.vjp(forward, cell_tokens, *params)
        grads = pull(cell_cot)
        summed = tuple((total_now + extra for total_now, extra in zip(totals, grads[1:])))
        return (summed, (result, grads[0]))
    zeros = tuple((jnp.zeros(weight_arg.shape, jnp.float32) for weight_arg in params))
    totals, (results, input_grads) = lax.scan(step, zeros, (inputs_full, valid, weighted))
    heads = results[:, 0, :]
    cls_mean = lax.optimization_barrier(jnp.mean(heads, axis=0))
    cls_var = lax.optimization_barrier(jnp.mean(heads * heads, axis=0)) - cls_mean * cls_mean
    return (results.astype(jnp.bfloat16), input_grads, totals[0], totals[1], totals[2], totals[3], totals[4], totals[5], totals[6], totals[7], totals[8], totals[9], cls_mean, cls_var)
```

```python
import functools
import math

import jax
import jax.numpy as jnp
from jax import lax
from jax.experimental import pallas as pl
from jax.experimental.pallas import tpu as pltpu
from jax.sharding import PartitionSpec as P

HEAD_DIM = 64
FILLED = 768
EPS = 1e-05
ROOT_HALF = 0.7071067811865476
DENSITY_SCALE = 0.3989422804014327
LOG2E = 1.4426950408889634
BF = jnp.bfloat16
F32 = jnp.float32
NT = (((1,), (1,)), ((), ()))
TN = (((0,), (0,)), ((), ()))
VMEM_MAX = 60 * 2**20


def whole(shape):
    return pl.BlockSpec(shape, lambda *_: (0,) * len(shape), pipeline_mode=pl.Buffered(1))


def smem():
    return pl.BlockSpec(memory_space=pltpu.SMEM)


def cost(flops, moved, exps=0):
    return pl.CostEstimate(flops=int(flops), bytes_accessed=int(moved), transcendentals=int(exps))


def shift_rows(shape, dim, shift, length):
    slot = lax.broadcasted_iota(jnp.int32, shape, dim)
    row = lax.broadcasted_iota(jnp.int32, shape, 1 - dim)
    return jnp.where((row == slot + shift) & (slot < length), 1.0, 0.0).astype(BF)


def pack(packed, values, lens, part, block, at):
    per = values.shape[0] // block
    for b in range(per):
        here = lens[part * per + b]
        rows = values[b * block : (b + 1) * block, :]
        shift = at % 8
        base = pl.multiple_of(at - shift, 8) if part + b else 0
        move = shift_rows((block + 8, block), 1, shift, here)
        moved = jnp.dot(move, rows, preferred_element_type=F32)
        if part + b:
            packed[pl.ds(base, 8), :] += moved[:8, :]
            packed[pl.ds(pl.multiple_of(base + 8, 8), block), :] = moved[8:, :]
        else:
            packed[: block + 8, :] = moved
        at = at + here
    return at


def unpack(packed, out, lens, part, block, at):
    per = out.shape[0] // block
    for b in range(per):
        here = lens[part * per + b]
        shift = at % 8
        base = pl.multiple_of(at - shift, 8) if part + b else 0
        rows = packed[pl.ds(base, block + 8), :].astype(BF)
        move = shift_rows((block, block + 8), 0, shift, here)
        out[b * block : (b + 1) * block, :] = jnp.dot(
            move, rows, preferred_element_type=F32
        ).astype(BF)
        at = at + here
    return at


def attend_kernel(block, heads, lens, *refs):
    parts = 4
    firsts, weight = refs[:parts], refs[parts]
    mixed = refs[parts + 1 : 2 * parts + 1]
    qkv_c = refs[2 * parts + 1]
    query, packed = refs[2 * parts + 2 :]
    rows = firsts[0].shape[0]
    wide = heads * HEAD_DIM
    at = 0
    for r in range(parts):
        qkv = jnp.dot(firsts[r][...], weight[...], preferred_element_type=F32)
        query[r * rows : (r + 1) * rows, :] = qkv[:, :wide].astype(BF)
        at = pack(packed, qkv.astype(BF), lens, r, block, at)
    qkv_c[...] = packed[:FILLED, :].astype(BF)
    scale = LOG2E / math.sqrt(HEAD_DIM)
    ones = jnp.ones((FILLED, HEAD_DIM), BF)
    for r in range(parts):
        for h in range(heads):
            lo = h * HEAD_DIM
            q = query[r * rows : (r + 1) * rows, lo : lo + HEAD_DIM]
            k = qkv_c[:, wide + lo : wide + lo + HEAD_DIM]
            v = qkv_c[:, 2 * wide + lo : 2 * wide + lo + HEAD_DIM]
            s = lax.dot_general(q, k, NT, preferred_element_type=F32)
            top = jnp.max(s, axis=1, keepdims=True) * scale
            e = jnp.exp2(s * scale - top).astype(BF)
            o = jnp.dot(e, jnp.concatenate([v, ones], axis=1), preferred_element_type=F32)
            o = o[:, :HEAD_DIM] / o[:, HEAD_DIM:]
            mixed[r][:, lo : lo + HEAD_DIM] = o.astype(BF)


def attend(firsts, lens, weight, block):
    rows, width = firsts[0].shape
    wide3 = weight.shape[1]
    wide = wide3 // 3
    heads = wide // HEAD_DIM
    out = pl.pallas_call(
        functools.partial(attend_kernel, block, heads),
        in_specs=[smem()] + [whole((rows, width))] * 4 + [whole(weight.shape)],
        out_specs=[whole((rows, wide))] * 4 + [whole((FILLED, wide3))],
        out_shape=[jax.ShapeDtypeStruct((rows, wide), BF)] * 4
        + [jax.ShapeDtypeStruct((FILLED, wide3), BF)],
        scratch_shapes=[pltpu.VMEM((4 * rows, wide), BF), pltpu.VMEM((FILLED + block, wide3), F32)],
        compiler_params=pltpu.CompilerParams(vmem_limit_bytes=VMEM_MAX),
        cost_estimate=cost(2 * 4 * rows * width * wide3 + 4 * 4 * rows * FILLED * 256 * heads, 8e6),
        grid=(1,),
        name="attend",
    )(lens, *firsts, weight)
    return out[:4], out[4]


def attend_back_kernel(block, heads, lens, *refs):
    parts = 4
    grads, qkv_c = refs[:parts], refs[parts]
    outs = refs[parts + 1 : 2 * parts + 1]
    packed, back = refs[2 * parts + 1 :]
    wide = heads * HEAD_DIM
    at = 0
    for r in range(parts):
        at = pack(packed, grads[r][...], lens, r, block, at)
    scale = LOG2E / math.sqrt(HEAD_DIM)
    inv_root = 1.0 / math.sqrt(HEAD_DIM)
    chunk = 256
    back[FILLED:, :] = jnp.zeros((block, 3 * wide), F32)
    grad_t = packed[:FILLED, :].T
    query_t = qkv_c[:, :wide].astype(F32).T.astype(BF)
    key_t = qkv_c[:, wide : 2 * wide].astype(F32).T.astype(BF)
    for h in range(heads):
        lo = h * HEAD_DIM
        k = qkv_c[:, wide + lo : wide + lo + HEAD_DIM]
        v = qkv_c[:, 2 * wide + lo : 2 * wide + lo + HEAD_DIM]
        kt = key_t[lo : lo + HEAD_DIM, :]
        dv = jnp.zeros((FILLED, HEAD_DIM), F32)
        dk = jnp.zeros((FILLED, HEAD_DIM), F32)
        for c in range(0, FILLED, chunk):
            qt = query_t[lo : lo + HEAD_DIM, c : c + chunk]
            s = jnp.dot(k, qt, preferred_element_type=F32)
            top = jnp.max(s, axis=0, keepdims=True) * scale
            e = jnp.exp2(s * scale - top)
            inv = 1.0 / jnp.sum(e, axis=0, keepdims=True)
            gt = (grad_t[lo : lo + HEAD_DIM, c : c + chunk] * inv).astype(BF)
            dp = jnp.dot(v, gt, preferred_element_type=F32)
            inner = jnp.sum(e * dp, axis=0, keepdims=True) * inv
            ds = (e * (dp - inner)).astype(BF)
            dv = dv + lax.dot_general(e.astype(BF), gt, NT, preferred_element_type=F32)
            dk = dk + lax.dot_general(ds, qt, NT, preferred_element_type=F32)
            dqt = jnp.dot(kt, ds, preferred_element_type=F32)
            back[c : c + chunk, lo : lo + HEAD_DIM] = dqt.T * inv_root
        back[:FILLED, wide + lo : wide + lo + HEAD_DIM] = dk * inv_root
        back[:FILLED, 2 * wide + lo : 2 * wide + lo + HEAD_DIM] = dv
    at = 0
    for r in range(parts):
        at = unpack(back, outs[r], lens, r, block, at)


def attend_back(grads, lens, qkv_c, block):
    rows, wide = grads[0].shape
    heads = wide // HEAD_DIM
    return pl.pallas_call(
        functools.partial(attend_back_kernel, block, heads),
        in_specs=[smem()] + [whole((rows, wide))] * 4 + [whole(qkv_c.shape)],
        out_specs=[whole((rows, 3 * wide))] * 4,
        out_shape=[jax.ShapeDtypeStruct((rows, 3 * wide), BF)] * 4,
        scratch_shapes=[
            pltpu.VMEM((FILLED + block, wide), F32),
            pltpu.VMEM((FILLED + block, 3 * wide), F32),
        ],
        compiler_params=pltpu.CompilerParams(vmem_limit_bytes=VMEM_MAX),
        cost_estimate=cost(2 * 5 * FILLED * FILLED * 256 * heads, 6e6),
        grid=(1,),
        name="attend_back",
    )(lens, *grads, qkv_c)


FF_TILE = 512
FF_ROWS = 256
FF_GRAD = 256


def feed_kernel(half, second_a, second_b, low_a, low_b, up, down, *refs):
    result, send_result, back, send_back, down_grad, up_grad = refs[:6]
    second_t, active, upper_back, acc_result, acc_back = refs[6:]
    rows, width = second_a.shape
    tile = up.shape[1]
    step = pl.program_id(0)

    @pl.when(step == 0)
    def _():
        result[...] = jnp.zeros_like(result)
        back[...] = jnp.zeros_like(back)
        acc_result[...] = jnp.zeros_like(acc_result)
        acc_back[...] = jnp.zeros_like(acc_back)
        for part, ref in enumerate((second_a, second_b)):
            for lo in range(0, rows, FF_ROWS):
                at = part * rows + lo
                second_t[:, at : at + FF_ROWS] = ref[lo : lo + FF_ROWS, :].astype(F32).T.astype(BF)

    for part, (second, low, to_result, to_back) in enumerate(
        ((second_a, low_a, result, back), (second_b, low_b, acc_result, acc_back))
    ):

        def chunk(i, carry):
            here = pl.ds(pl.multiple_of(i * FF_ROWS, FF_ROWS), FF_ROWS)
            there = pl.ds(pl.multiple_of(part * rows + i * FF_ROWS, FF_ROWS), FF_ROWS)
            upper = jnp.dot(second[here, :], up[...], preferred_element_type=F32)
            grad = lax.dot_general(low[here, :], down[...], NT, preferred_element_type=F32)
            below = 0.5 * (1.0 + lax.erf(upper * ROOT_HALF))
            density = jnp.exp(-0.5 * upper * upper) * DENSITY_SCALE
            act = (upper * below).astype(BF)
            ub = (grad * (below + upper * density)).astype(BF)
            active[there, :] = act
            upper_back[there, :] = ub
            to_result[here, :] += jnp.dot(act, down[...], preferred_element_type=F32)
            to_back[here, :] += lax.dot_general(ub, up[...], NT, preferred_element_type=F32)
            return carry

        lax.fori_loop(0, rows // FF_ROWS, chunk, 0)

    def one_down(i, carry):
        here = pl.ds(pl.multiple_of(i * FF_GRAD, FF_GRAD), FF_GRAD)
        act = active[:, here].astype(F32).T.astype(BF)
        down_grad[here, :] = (
            jnp.dot(act[:, :rows], low_a[...], preferred_element_type=F32)
            + jnp.dot(act[:, rows:], low_b[...], preferred_element_type=F32)
        ).astype(BF)
        return carry

    lax.fori_loop(0, tile // FF_GRAD, one_down, 0)

    def one_up(i, carry):
        here = pl.ds(pl.multiple_of(i * FF_GRAD, FF_GRAD), FF_GRAD)
        up_grad[here, :] = jnp.dot(
            second_t[here, :], upper_back[...], preferred_element_type=F32
        ).astype(BF)
        return carry

    lax.fori_loop(0, width // FF_GRAD, one_up, 0)

    @pl.when(step == pl.num_programs(0) - 1)
    def _():
        send_result[...] = acc_result[...].astype(BF)
        send_back[...] = acc_back[...].astype(BF)


def feed_forward(half, second_a, second_b, low_a, low_b, up, down):
    rows, width = second_a.shape
    units = up.shape[1] // 2
    tiles = units // FF_TILE
    two = 2 * rows
    return pl.pallas_call(
        feed_kernel,
        grid_spec=pltpu.PrefetchScalarGridSpec(
            num_scalar_prefetch=1,
            grid=(tiles,),
            in_specs=[whole((rows, width))] * 4
            + [
                pl.BlockSpec((width, FF_TILE), lambda j, half: (0, half[0] * tiles + j)),
                pl.BlockSpec((FF_TILE, width), lambda j, half: (half[0] * tiles + j, 0)),
            ],
            out_specs=[whole((rows, width))] * 4
            + [
                pl.BlockSpec((FF_TILE, width), lambda j, half: (j, 0)),
                pl.BlockSpec((width, FF_TILE), lambda j, half: (0, j)),
            ],
            scratch_shapes=[
                pltpu.VMEM((width, two), BF),
                pltpu.VMEM((two, FF_TILE), BF),
                pltpu.VMEM((two, FF_TILE), BF),
                pltpu.VMEM((rows, width), F32),
                pltpu.VMEM((rows, width), F32),
            ],
        ),
        out_shape=[
            jax.ShapeDtypeStruct((rows, width), F32),
            jax.ShapeDtypeStruct((rows, width), BF),
            jax.ShapeDtypeStruct((rows, width), F32),
            jax.ShapeDtypeStruct((rows, width), BF),
            jax.ShapeDtypeStruct((units, width), BF),
            jax.ShapeDtypeStruct((width, units), BF),
        ],
        compiler_params=pltpu.CompilerParams(vmem_limit_bytes=VMEM_MAX),
        cost_estimate=cost(2 * 6 * two * width * units, 6e7),
        name="feed_forward",
    )(half, second_a, second_b, low_a, low_b, up, down)


def swap(x, axis, mask):
    size = lax.axis_size(axis)
    return lax.ppermute(x, axis, [(i, i ^ mask) for i in range(size)])


def halve(x, dim, axis, bit):
    mine = (lax.axis_index(axis) >> bit) & 1
    send = lax.dynamic_index_in_dim(x, 1 - mine, dim, keepdims=False)
    keep = lax.dynamic_index_in_dim(x, mine, dim, keepdims=False)
    got = swap(send, axis, 1 << bit)
    return keep.astype(F32) + got.astype(F32)


def log2(n):
    return n.bit_length() - 1


def scatter_rows(x, order, names):
    names = list(names)
    for i, name in enumerate(order):
        x = halve(x.astype(BF), names.index(name), name[0], name[1])
        names.remove(name)
    return x


def sum_all(x):
    for bit in range(log2(lax.axis_size("chrom"))):
        x = x + swap(x, "chrom", 1 << bit)
    for bit in range(log2(lax.axis_size("cells"))):
        x = x + swap(x, "cells", 1 << bit)
    return x


def scatter_columns_split(x, order):
    cell_bits = log2(lax.axis_size("cells"))
    core = lax.axis_index("chrom") & 1
    width = x.shape[1]
    names = [("cells", b) for b in reversed(range(cell_bits))] + [("chrom", 1)]
    x = x.reshape((2,) * (cell_bits + 1) + (-1, width))
    x = scatter_rows(x, order, names)
    x = x.reshape(2, -1, width)
    keep = lax.dynamic_index_in_dim(x, core, 0, keepdims=False)
    got = swap(lax.dynamic_index_in_dim(x, 1 - core, 0, keepdims=False).astype(BF), "chrom", 1).astype(F32)
    left = jnp.where(core == 0, keep, got)
    right = jnp.where(core == 0, got, keep)
    return jnp.concatenate([left, right], axis=1)


def scatter_rows_split(x, order):
    cells = lax.axis_size("cells")
    cell_bits = log2(cells)
    chrom = lax.axis_size("chrom")
    core = lax.axis_index("chrom") & 1
    high = (lax.axis_index("cells") >> (cell_bits - 1)) & 1
    width = x.shape[1]
    names = [("cells", b) for b in reversed(range(cell_bits - 1))] + [("chrom", 1)]
    x = x.reshape((2,) * cell_bits + (-1, width))
    x = scatter_rows(x, order, names)
    top = cells // 2
    pairs = []
    for cell in range(cells):
        for place in range(chrom):
            if (cell // top) != (place & 1):
                pairs.append((cell * chrom + place, (cell ^ top) * chrom + place))
    got = lax.ppermute(x.astype(BF), ("cells", "chrom"), pairs)
    x = (x + got.astype(F32)).reshape(2, -1, width)
    keep = lax.dynamic_index_in_dim(x, core, 0, keepdims=False)
    send = lax.dynamic_index_in_dim(x, 1 - core, 0, keepdims=False).astype(BF)
    back = []
    for cell in range(cells):
        for place in range(chrom):
            if (cell // top) == (place & 1):
                back.append((cell * chrom + place, cell * chrom + (place ^ 1)))
    got = lax.ppermute(send, ("cells", "chrom"), back)
    return jnp.where(core == high, keep, got.astype(F32))


def norm_rows(values, gain, shift):
    center = values - jnp.mean(values, axis=-1, keepdims=True)
    inverse = lax.rsqrt(jnp.mean(center * center, axis=-1, keepdims=True) + EPS)
    normed = center * inverse
    return (normed * gain + shift, normed, inverse)


def norm_back(grad_out, normed, inverse, gain):
    scaled = grad_out * gain
    grad_in = inverse * (
        scaled
        - jnp.mean(scaled, axis=-1, keepdims=True)
        - normed * jnp.mean(scaled * normed, axis=-1, keepdims=True)
    )
    return (grad_in, jnp.sum(grad_out * normed, axis=0), jnp.sum(grad_out, axis=0))


def contract(left, right):
    return lax.dot_general(left, right, TN, preferred_element_type=F32)


def back_through(grad, weight):
    return lax.dot_general(grad, weight, NT, preferred_element_type=F32)


def per_device(
    tokens,
    cotangent,
    block_lengths,
    group_ids,
    group_weights,
    first_gain,
    first_shift,
    query_weight,
    key_weight,
    value_weight,
    output_weight,
    second_gain,
    second_shift,
    up_weight,
    down_weight,
):
    cells_here, seq_here, width = tokens.shape
    rows = cells_here * seq_here
    parts = lax.axis_size("chrom")
    cell_bits = log2(lax.axis_size("cells"))
    seq_full = seq_here * parts
    nblocks = block_lengths.shape[1]
    block = seq_full // nblocks
    per = nblocks // parts
    wide = width // parts
    place = lax.axis_index("chrom")
    core = place & 1
    near = [place ^ r for r in range(parts)]

    valid = (jnp.arange(block)[None, None, :] < block_lengths[:, :, None]).reshape(
        cells_here, seq_full
    )
    local_valid = lax.dynamic_slice_in_dim(valid, place * seq_here, seq_here, 1)
    lens = jnp.concatenate(
        [lax.dynamic_slice_in_dim(block_lengths, n * per, per, 1) for n in near], axis=1
    )
    n_groups = group_weights.shape[0]
    cell_scale = jnp.sum(
        jnp.where(group_ids[:, None] == jnp.arange(n_groups)[None, :], group_weights[None, :], 0.0),
        axis=1,
    )

    def my_heads(weight):
        return lax.dynamic_slice_in_dim(weight, place * wide, wide, 1)

    qkv_weight = jnp.concatenate(
        [my_heads(query_weight), my_heads(key_weight), my_heads(value_weight)], axis=1
    )
    output_near = jnp.concatenate(
        [lax.dynamic_slice_in_dim(output_weight, n * wide, wide, 0) for n in near], axis=0
    )

    flat = tokens.reshape(rows, width).astype(F32)
    first_out, first_norm, first_inv = norm_rows(flat, first_gain, first_shift)
    first_low = first_out.astype(BF).reshape(cells_here, seq_here, width)
    first_all, mixed_near, kept = [], [], []
    for c in range(cells_here):
        mine = first_low[c]
        over = swap(mine, "chrom", 2)
        first_all.append([mine, swap(mine, "chrom", 1), over, swap(over, "chrom", 1)])
    for c in range(cells_here):
        mixed, qkv_c = attend(first_all[c], lens[c], qkv_weight, block)
        kept.append(qkv_c)
        mixed_near.append(
            jnp.concatenate([mixed[0]] + [swap(mixed[r], "chrom", r) for r in range(1, parts)], axis=1)
        )
    mixed_flat = jnp.concatenate(mixed_near, axis=0)

    middle = flat + jnp.dot(mixed_flat, output_near, preferred_element_type=F32)
    second_out, second_norm, second_inv = norm_rows(middle, second_gain, second_shift)
    second_low = second_out.astype(BF)
    result_back = (
        cotangent.astype(F32)
        * cell_scale[:, None, None]
        * local_valid.astype(F32)[:, :, None]
    ).reshape(rows, width)
    down_low = result_back.astype(BF)
    down_low_near = swap(down_low, "chrom", 1)
    second_low_near = swap(second_low, "chrom", 1)

    result_part, result_send, back_part, back_send, down_grad, up_grad = feed_forward(
        core[None].astype(jnp.int32),
        second_low,
        second_low_near,
        down_low,
        down_low_near,
        up_weight,
        down_weight,
    )
    second_back = back_part + swap(back_send, "chrom", 1).astype(F32)
    result = middle + result_part + swap(result_send, "chrom", 1).astype(F32)
    result_cells = result.reshape(cells_here, seq_here, width)
    layer_out = result_cells.astype(BF)
    low_bits = [("cells", b) for b in range(cell_bits - 1)]
    down_out = scatter_rows_split(down_grad, low_bits + [("chrom", 1)])
    up_out = scatter_columns_split(up_grad, [("chrom", 1)] + low_bits[::-1] + [("cells", cell_bits - 1)])

    cls_rows = jnp.where(place == 0, result_cells[:, 0, :], 0.0)
    cls_total = jnp.sum(cls_rows, axis=0)
    cls_square = jnp.sum(cls_rows * cls_rows, axis=0)

    middle_ln, second_gain_grad, second_shift_grad = norm_back(
        second_back, second_norm, second_inv, second_gain
    )
    middle_back = result_back + middle_ln
    attend_low = middle_back.astype(BF)
    mixed_back = back_through(attend_low, output_near).astype(BF)
    output_grad = contract(mixed_flat, attend_low).reshape(parts, wide, width)
    output_grad = jnp.concatenate(
        [lax.dynamic_index_in_dim(output_grad, place ^ j, 0, keepdims=False) for j in range(parts)],
        axis=0,
    )
    half_width = width // 2
    output_half = lax.dynamic_slice_in_dim(output_grad, core * half_width, half_width, 1) + swap(
        lax.dynamic_slice_in_dim(output_grad, (1 - core) * half_width, half_width, 1).astype(BF),
        "chrom",
        1,
    ).astype(F32)
    output_out = scatter_columns_split(
        output_half.astype(BF), low_bits + [("cells", cell_bits - 1), ("chrom", 1)]
    )
    early = sum_all(jnp.stack([cls_total, cls_square, second_gain_grad, second_shift_grad]))

    mixed_back = mixed_back.reshape(cells_here, seq_here, width)
    heads_back = []
    for c in range(cells_here):
        pieces = [mixed_back[c, :, r * wide : (r + 1) * wide] for r in range(parts)]
        heads_back.append(
            [pieces[0]] + [swap(pieces[r], "chrom", r) for r in range(1, parts)]
        )
    qkv_grad = None
    first_back = []
    for c in range(cells_here):
        qkv_back = attend_back(heads_back[c], lens[c], kept[c], block)
        pieces = [back_through(g, qkv_weight) for g in qkv_back]
        sent = swap(jnp.stack([pieces[1].astype(BF), pieces[3].astype(BF)]), "chrom", 1).astype(F32)
        over = swap((pieces[2] + sent[1]).astype(BF), "chrom", 2)
        first_back.append(pieces[0] + sent[0] + over.astype(F32))
        part = contract(
            jnp.concatenate(first_all[c], axis=0), jnp.concatenate(qkv_back, axis=0)
        )
        qkv_grad = part if qkv_grad is None else qkv_grad + part
    first_back = jnp.concatenate(first_back, axis=0)

    names = [("cells", b) for b in reversed(range(cell_bits))]
    qkv_sum = scatter_rows(
        qkv_grad.reshape((2,) * cell_bits + (-1, 3 * wide)),
        [("cells", b) for b in range(cell_bits)],
        names,
    ).reshape(parts, -1, 3 * wide)
    pieces = [lax.dynamic_index_in_dim(qkv_sum, near[0], 0, keepdims=False)]
    for r in range(1, parts):
        piece = lax.dynamic_index_in_dim(qkv_sum, near[r], 0, keepdims=False).astype(BF)
        pieces.append(swap(piece, "chrom", r).astype(F32))
    pieces = jnp.stack(pieces)
    pieces = [lax.dynamic_index_in_dim(pieces, place ^ j, 0, keepdims=False) for j in range(parts)]
    query_out, key_out, value_out = [
        jnp.concatenate([p[:, i * wide : (i + 1) * wide] for p in pieces], axis=1) for i in range(3)
    ]

    first_ln, first_gain_grad, first_shift_grad = norm_back(
        first_back, first_norm, first_inv, first_gain
    )
    tokens_grad = (middle_back + first_ln).reshape(cells_here, seq_here, width)
    late = sum_all(jnp.stack([first_gain_grad, first_shift_grad]))

    count_cells = cells_here * lax.axis_size("cells")
    cls_mean = early[0] / count_cells
    cls_var = early[1] / count_cells - cls_mean * cls_mean
    share = width // (parts * lax.axis_size("cells"))
    start = (lax.axis_index("cells") * parts + place) * share

    def mine(vector):
        return lax.dynamic_slice_in_dim(vector, start, share, 0)

    return (
        layer_out,
        tokens_grad,
        mine(late[0]),
        mine(late[1]),
        query_out,
        key_out,
        value_out,
        output_out,
        mine(early[2]),
        mine(early[3]),
        up_out,
        down_out,
        cls_mean,
        cls_var,
    )


def solution(mesh):
    rows = P("cells", "chrom", None)
    both = ("cells", "chrom")
    in_specs = (rows, rows, P("cells", None), P("cells")) + (P(),) * 11
    out_specs = (
        (rows, rows)
        + (P(both), P(both))
        + (P(both, None),) * 4
        + (P(both), P(both))
        + (P(both, None), P(both, None))
        + (P(), P())
    )
    return jax.shard_map(
        per_device, mesh=mesh, in_specs=in_specs, out_specs=out_specs, check_vma=False
    )
```

```python
import functools
import math

import jax
import jax.numpy as jnp
from jax import lax
from jax.experimental import pallas as pl
from jax.experimental.pallas import tpu as pltpu
from jax.sharding import PartitionSpec as P

HEAD_DIM = 64
FILLED = 768
EPS = 1e-05
ROOT_HALF = 0.7071067811865476
DENSITY_SCALE = 0.3989422804014327
LOG2E = 1.4426950408889634
BF = jnp.bfloat16
F32 = jnp.float32
NT = (((1,), (1,)), ((), ()))
TN = (((0,), (0,)), ((), ()))
VMEM_MAX = 60 * 2**20
VMEM_TOP = 63 * 2**20


def whole(shape):
    return pl.BlockSpec(shape, lambda *_: (0,) * len(shape), pipeline_mode=pl.Buffered(1))


def smem():
    return pl.BlockSpec(memory_space=pltpu.SMEM)


def cost(flops, moved, exps=0):
    return pl.CostEstimate(flops=int(flops), bytes_accessed=int(moved), transcendentals=int(exps))


def shift_rows(shape, dim, shift, length):
    slot = lax.broadcasted_iota(jnp.int32, shape, dim)
    row = lax.broadcasted_iota(jnp.int32, shape, 1 - dim)
    return jnp.where((row == slot + shift) & (slot < length), 1.0, 0.0).astype(BF)


def pack(packed, values, lens, part, block, at):
    per = values.shape[0] // block
    for b in range(per):
        here = lens[part * per + b]
        rows = values[b * block : (b + 1) * block, :]
        shift = at % 8
        base = pl.multiple_of(at - shift, 8) if part + b else 0
        move = shift_rows((block + 8, block), 1, shift, here)
        moved = jnp.dot(move, rows, preferred_element_type=F32)
        if part + b:
            packed[pl.ds(base, 8), :] += moved[:8, :]
            packed[pl.ds(pl.multiple_of(base + 8, 8), block), :] = moved[8:, :]
        else:
            packed[: block + 8, :] = moved
        at = at + here
    return at


def unpack(packed, out, lens, part, block, at):
    per = out.shape[0] // block
    for b in range(per):
        here = lens[part * per + b]
        shift = at % 8
        base = pl.multiple_of(at - shift, 8) if part + b else 0
        rows = packed[pl.ds(base, block + 8), :].astype(BF)
        move = shift_rows((block, block + 8), 0, shift, here)
        out[b * block : (b + 1) * block, :] = jnp.dot(
            move, rows, preferred_element_type=F32
        ).astype(BF)
        at = at + here
    return at


def attend_kernel(block, heads, lens, *refs):
    parts = 4
    firsts, weight = refs[:parts], refs[parts]
    mixed = refs[parts + 1 : 2 * parts + 1]
    qkv_c = refs[2 * parts + 1]
    query, packed = refs[2 * parts + 2 :]
    rows = firsts[0].shape[0]
    wide = heads * HEAD_DIM
    at = 0
    for r in range(parts):
        qkv = jnp.dot(firsts[r][...], weight[...], preferred_element_type=F32)
        query[r * rows : (r + 1) * rows, :] = qkv[:, :wide].astype(BF)
        at = pack(packed, qkv.astype(BF), lens, r, block, at)
    qkv_c[...] = packed[:FILLED, :].astype(BF)
    scale = LOG2E / math.sqrt(HEAD_DIM)
    ones = jnp.ones((FILLED, HEAD_DIM), BF)
    for r in range(parts):
        for h in range(heads):
            lo = h * HEAD_DIM
            q = query[r * rows : (r + 1) * rows, lo : lo + HEAD_DIM]
            k = qkv_c[:, wide + lo : wide + lo + HEAD_DIM]
            v = qkv_c[:, 2 * wide + lo : 2 * wide + lo + HEAD_DIM]
            s = lax.dot_general(q, k, NT, preferred_element_type=F32)
            top = jnp.max(s, axis=1, keepdims=True) * scale
            e = jnp.exp2(s * scale - top).astype(BF)
            o = jnp.dot(e, jnp.concatenate([v, ones], axis=1), preferred_element_type=F32)
            o = o[:, :HEAD_DIM] / o[:, HEAD_DIM:]
            mixed[r][:, lo : lo + HEAD_DIM] = o.astype(BF)


def attend(firsts, lens, weight, block):
    rows, width = firsts[0].shape
    wide3 = weight.shape[1]
    wide = wide3 // 3
    heads = wide // HEAD_DIM
    out = pl.pallas_call(
        functools.partial(attend_kernel, block, heads),
        in_specs=[smem()] + [whole((rows, width))] * 4 + [whole(weight.shape)],
        out_specs=[whole((rows, wide))] * 4 + [whole((FILLED, wide3))],
        out_shape=[jax.ShapeDtypeStruct((rows, wide), BF)] * 4
        + [jax.ShapeDtypeStruct((FILLED, wide3), BF)],
        scratch_shapes=[pltpu.VMEM((4 * rows, wide), BF), pltpu.VMEM((FILLED + block, wide3), F32)],
        compiler_params=pltpu.CompilerParams(vmem_limit_bytes=VMEM_MAX),
        cost_estimate=cost(2 * 4 * rows * width * wide3 + 4 * 4 * rows * FILLED * 256 * heads, 8e6),
        grid=(1,),
        name="attend",
    )(lens, *firsts, weight)
    return out[:4], out[4]


def attend_back_kernel(block, heads, lens, *refs):
    parts = 4
    grads, qkv_c = refs[:parts], refs[parts]
    outs = refs[parts + 1 : 2 * parts + 1]
    packed, back = refs[2 * parts + 1 :]
    wide = heads * HEAD_DIM
    at = 0
    for r in range(parts):
        at = pack(packed, grads[r][...], lens, r, block, at)
    scale = LOG2E / math.sqrt(HEAD_DIM)
    inv_root = 1.0 / math.sqrt(HEAD_DIM)
    chunk = 256
    back[FILLED:, :] = jnp.zeros((block, 3 * wide), F32)
    grad_t = packed[:FILLED, :].T
    query_t = qkv_c[:, :wide].astype(F32).T.astype(BF)
    key_t = qkv_c[:, wide : 2 * wide].astype(F32).T.astype(BF)
    for h in range(heads):
        lo = h * HEAD_DIM
        k = qkv_c[:, wide + lo : wide + lo + HEAD_DIM]
        v = qkv_c[:, 2 * wide + lo : 2 * wide + lo + HEAD_DIM]
        kt = key_t[lo : lo + HEAD_DIM, :]
        dv = jnp.zeros((FILLED, HEAD_DIM), F32)
        dk = jnp.zeros((FILLED, HEAD_DIM), F32)
        for c in range(0, FILLED, chunk):
            qt = query_t[lo : lo + HEAD_DIM, c : c + chunk]
            s = jnp.dot(k, qt, preferred_element_type=F32)
            top = jnp.max(s, axis=0, keepdims=True) * scale
            e = jnp.exp2(s * scale - top)
            inv = 1.0 / jnp.sum(e, axis=0, keepdims=True)
            gt = (grad_t[lo : lo + HEAD_DIM, c : c + chunk] * inv).astype(BF)
            dp = jnp.dot(v, gt, preferred_element_type=F32)
            inner = jnp.sum(e * dp, axis=0, keepdims=True) * inv
            ds = (e * (dp - inner)).astype(BF)
            dv = dv + lax.dot_general(e.astype(BF), gt, NT, preferred_element_type=F32)
            dk = dk + lax.dot_general(ds, qt, NT, preferred_element_type=F32)
            dqt = jnp.dot(kt, ds, preferred_element_type=F32)
            back[c : c + chunk, lo : lo + HEAD_DIM] = dqt.T * inv_root
        back[:FILLED, wide + lo : wide + lo + HEAD_DIM] = dk * inv_root
        back[:FILLED, 2 * wide + lo : 2 * wide + lo + HEAD_DIM] = dv
    at = 0
    for r in range(parts):
        at = unpack(back, outs[r], lens, r, block, at)


def attend_back(grads, lens, qkv_c, block):
    rows, wide = grads[0].shape
    heads = wide // HEAD_DIM
    return pl.pallas_call(
        functools.partial(attend_back_kernel, block, heads),
        in_specs=[smem()] + [whole((rows, wide))] * 4 + [whole(qkv_c.shape)],
        out_specs=[whole((rows, 3 * wide))] * 4,
        out_shape=[jax.ShapeDtypeStruct((rows, 3 * wide), BF)] * 4,
        scratch_shapes=[
            pltpu.VMEM((FILLED + block, wide), F32),
            pltpu.VMEM((FILLED + block, 3 * wide), F32),
        ],
        compiler_params=pltpu.CompilerParams(vmem_limit_bytes=VMEM_MAX),
        cost_estimate=cost(2 * 5 * FILLED * FILLED * 256 * heads, 6e6),
        grid=(1,),
        name="attend_back",
    )(lens, *grads, qkv_c)


FF_TILE = 512
FF_ROWS = 256
FF_GRAD = 256


def feed_kernel(half, second_a, second_b, low_a, low_b, up, down, *refs):
    result, send_result, back, send_back, down_grad, up_grad = refs[:6]
    second_t, active, upper_back, acc_result, acc_back = refs[6:]
    rows, width = second_a.shape
    tile = up.shape[1]
    step = pl.program_id(0)

    @pl.when(step == 0)
    def _():
        result[...] = jnp.zeros_like(result)
        back[...] = jnp.zeros_like(back)
        acc_result[...] = jnp.zeros_like(acc_result)
        acc_back[...] = jnp.zeros_like(acc_back)
        for part, ref in enumerate((second_a, second_b)):
            for lo in range(0, rows, FF_ROWS):
                at = part * rows + lo
                second_t[:, at : at + FF_ROWS] = ref[lo : lo + FF_ROWS, :].astype(F32).T.astype(BF)

    for part, (second, low, to_result, to_back) in enumerate(
        ((second_a, low_a, result, back), (second_b, low_b, acc_result, acc_back))
    ):

        def chunk(i, carry):
            here = pl.ds(pl.multiple_of(i * FF_ROWS, FF_ROWS), FF_ROWS)
            there = pl.ds(pl.multiple_of(part * rows + i * FF_ROWS, FF_ROWS), FF_ROWS)
            upper = jnp.dot(second[here, :], up[...], preferred_element_type=F32)
            grad = lax.dot_general(low[here, :], down[...], NT, preferred_element_type=F32)
            below = 0.5 * (1.0 + lax.erf(upper * ROOT_HALF))
            density = jnp.exp(-0.5 * upper * upper) * DENSITY_SCALE
            act = (upper * below).astype(BF)
            ub = (grad * (below + upper * density)).astype(BF)
            active[there, :] = act
            upper_back[there, :] = ub
            to_result[here, :] += jnp.dot(act, down[...], preferred_element_type=F32)
            to_back[here, :] += lax.dot_general(ub, up[...], NT, preferred_element_type=F32)
            return carry

        lax.fori_loop(0, rows // FF_ROWS, chunk, 0)

    def one_down(i, carry):
        here = pl.ds(pl.multiple_of(i * FF_GRAD, FF_GRAD), FF_GRAD)
        act = active[:, here].astype(F32).T.astype(BF)
        down_grad[here, :] = (
            jnp.dot(act[:, :rows], low_a[...], preferred_element_type=F32)
            + jnp.dot(act[:, rows:], low_b[...], preferred_element_type=F32)
        ).astype(BF)
        return carry

    lax.fori_loop(0, tile // FF_GRAD, one_down, 0)

    def one_up(i, carry):
        here = pl.ds(pl.multiple_of(i * FF_GRAD, FF_GRAD), FF_GRAD)
        up_grad[here, :] = jnp.dot(
            second_t[here, :], upper_back[...], preferred_element_type=F32
        ).astype(BF)
        return carry

    lax.fori_loop(0, width // FF_GRAD, one_up, 0)

    @pl.when(step == pl.num_programs(0) - 1)
    def _():
        send_result[...] = acc_result[...].astype(BF)
        send_back[...] = acc_back[...].astype(BF)


def feed_forward(half, second_a, second_b, low_a, low_b, up, down):
    rows, width = second_a.shape
    units = up.shape[1] // 2
    tiles = units // FF_TILE
    two = 2 * rows
    return pl.pallas_call(
        feed_kernel,
        grid_spec=pltpu.PrefetchScalarGridSpec(
            num_scalar_prefetch=1,
            grid=(tiles,),
            in_specs=[whole((rows, width))] * 4
            + [
                pl.BlockSpec((width, FF_TILE), lambda j, half: (0, half[0] * tiles + j)),
                pl.BlockSpec((FF_TILE, width), lambda j, half: (half[0] * tiles + j, 0)),
            ],
            out_specs=[whole((rows, width))] * 4
            + [
                pl.BlockSpec((FF_TILE, width), lambda j, half: (j, 0)),
                pl.BlockSpec((width, FF_TILE), lambda j, half: (0, j)),
            ],
            scratch_shapes=[
                pltpu.VMEM((width, two), BF),
                pltpu.VMEM((two, FF_TILE), BF),
                pltpu.VMEM((two, FF_TILE), BF),
                pltpu.VMEM((rows, width), F32),
                pltpu.VMEM((rows, width), F32),
            ],
        ),
        out_shape=[
            jax.ShapeDtypeStruct((rows, width), F32),
            jax.ShapeDtypeStruct((rows, width), BF),
            jax.ShapeDtypeStruct((rows, width), F32),
            jax.ShapeDtypeStruct((rows, width), BF),
            jax.ShapeDtypeStruct((units, width), BF),
            jax.ShapeDtypeStruct((width, units), BF),
        ],
        compiler_params=pltpu.CompilerParams(vmem_limit_bytes=VMEM_MAX),
        cost_estimate=cost(2 * 6 * two * width * units, 6e7),
        name="feed_forward",
    )(half, second_a, second_b, low_a, low_b, up, down)


MESH = pl.DeviceIdType.MESH
TILE = 512
SPAN = 256
CHUNK = 256
DOWN_ITEMS = ((0, 512, "xyz"), (512, 1024, "yzx"), (1024, 1280, "zxy"))
UP_ORDERS = ("xyz", "yzx", "xyz", "zxy", "zxy")
UP_WHOLE = 3


def add_pieces(total, view, got):
    lead = len(total.shape) - 2
    tail = view[lead:] + (slice(None),) * (len(total.shape) - max(len(view), lead))
    free = [i for i in range(lead) if isinstance(view[i], slice)]
    for n in range(2 ** len(free)):
        pick = [(n >> i) & 1 for i in range(len(free))]
        index = list(view[:lead])
        for i, bit in zip(free, pick):
            index[i] = bit
        here = tuple(index) + tail
        total[here] = (total[here].astype(F32) + got[tuple(pick)].astype(F32)).astype(BF)


def feed_sum_kernel(
    second_in, low_in, up, down,
    back_out, result_out, down_out, up_out, up_rest,
    second, low, second_t, active, slope, down_part, up_part,
    wide_buf, tall_buf, flat_buf, thin_buf, stage,
    ra1, ra2, ra3, rb1, rb2, rb3, rc1, rc2, rc3, ru1, ru2, ru3,
    load_sem, weight_sem, out_sem, end_sem, swap_send, swap_recv, sum_send, sum_recv,
    ready_second, ready_low,
):
    rows = low_in.shape[0]
    width = low_in.shape[1]
    two = 2 * rows
    units = active.shape[1]
    tiles = units // TILE
    spans = width // SPAN
    cell = lax.axis_index("cells")
    place = lax.axis_index("chrom")
    core = place % 2
    mine = {"y": place // 2, "x": cell % 2, "z": (cell // 2) % 2}
    sibling = (cell, place + 1 - 2 * core)
    near = {
        "y": (cell, place + 2 - 4 * mine["y"]),
        "x": (cell + 1 - 2 * mine["x"], place),
        "z": (cell + 2 - 4 * mine["z"], place),
    }

    barrier = pltpu.get_barrier_semaphore()
    for other in (sibling, near["x"], near["y"], near["z"]):
        pl.semaphore_signal(barrier, inc=1, device_id=other, device_id_type=MESH)
    loads = [
        pltpu.make_async_copy(second_in, second.at[:rows], load_sem.at[0]),
        pltpu.make_async_copy(low_in, low.at[:rows], load_sem.at[1]),
    ]
    for copy in loads:
        copy.start()
    base = core * units

    def weight_copy(kind, j, slot):
        if kind == "wide":
            src = up.at[:, pl.ds(pl.multiple_of(base + j * TILE, 128), TILE)]
            return pltpu.make_async_copy(src, wide_buf.at[slot], weight_sem.at[slot])
        if kind == "tall":
            src = down.at[pl.ds(pl.multiple_of(base + j * TILE, 128), TILE), :]
            return pltpu.make_async_copy(src, tall_buf.at[slot], weight_sem.at[2 + slot])
        if kind == "flat":
            src = up.at[j * SPAN : (j + 1) * SPAN, pl.ds(pl.multiple_of(base, 128), units)]
            return pltpu.make_async_copy(src, flat_buf, weight_sem.at[4])
        src = down.at[pl.ds(pl.multiple_of(base, 128), units), j * SPAN : (j + 1) * SPAN]
        return pltpu.make_async_copy(src, thin_buf, weight_sem.at[5])

    plan = (
        [("wide", j) for j in range(tiles)]
        + [("tall", j) for j in range(tiles)]
        + [(kind, j) for j in range(spans) for kind in ("flat", "thin")]
    )
    copies = {}

    def fetch(i):
        if i < len(plan):
            kind, j = plan[i]
            copies[i] = weight_copy(kind, j, j % 2)
            copies[i].start()

    fetch(0)
    pl.semaphore_wait(barrier, 4)

    def remote(src, dst, send, recv, device):
        copy = pltpu.make_async_remote_copy(
            src_ref=src, dst_ref=dst, send_sem=send, recv_sem=recv,
            device_id=device, device_id_type=MESH,
        )
        copy.start()
        return copy

    sent = []
    swaps = [
        remote(second_in, second.at[rows:], swap_send.at[0], swap_recv.at[0], sibling),
        remote(low_in, low.at[rows:], swap_send.at[1], swap_recv.at[1], sibling),
    ]
    sent += swaps

    flight = {}

    def down_view(order, stage_no, lo, hi, other, fix_z=None):
        index = {"z": slice(None), "x": slice(None), "y": slice(None)}
        for s, axis in enumerate(order[: stage_no + 1]):
            index[axis] = 1 - mine[axis] if (s == stage_no and other) else mine[axis]
        if fix_z is not None:
            index["z"] = fix_z
        return (index["z"], index["x"], index["y"], slice(None), slice(lo, hi))

    def up_view(order, stage_no, other):
        index = {"z": slice(None), "x": slice(None), "y": slice(None)}
        for s, axis in enumerate(order[: stage_no + 1]):
            index[axis] = 1 - mine[axis] if (s == stage_no and other) else mine[axis]
        return (slice(None), index["z"], index["x"], index["y"])

    down_recv = ((ra1, ra2, ra3), (rb1, rb2, rb3), (rc1, rc2, rc3))
    up_recv = (ru1, ru2, ru3)

    def go_down(item, stage_no, fix_z=None):
        lo, hi, order = DOWN_ITEMS[item]
        src = down_part.at[down_view(order, stage_no, lo, hi, True, fix_z)]
        dst = down_recv[item][stage_no]
        sem = item * 4 + stage_no
        if fix_z is not None:
            dst = dst.at[fix_z]
            sem = item * 4 + (3 if fix_z else 0)
        copy = remote(src, dst, sum_send.at[sem], sum_recv.at[sem], near[order[stage_no]])
        flight.setdefault(("d", item, stage_no), []).append(copy)
        sent.append(copy)

    def end_down(item, stage_no):
        lo, hi, order = DOWN_ITEMS[item]
        for copy in flight[("d", item, stage_no)]:
            copy.wait_recv()
        add_pieces(down_part, down_view(order, stage_no, lo, hi, False), down_recv[item][stage_no])
        if stage_no < 2:
            go_down(item, stage_no + 1)

    def go_up(j, stage_no):
        order = UP_ORDERS[j]
        src = up_part.at[j].at[up_view(order, stage_no, True)]
        sem = 12 + 3 * j + stage_no
        copy = remote(
            src, up_recv[stage_no].at[j], sum_send.at[sem], sum_recv.at[sem], near[order[stage_no]]
        )
        flight[("u", j, stage_no)] = [copy]
        sent.append(copy)

    def end_up(j, stage_no):
        flight[("u", j, stage_no)][0].wait_recv()
        view = (j,) + up_view(UP_ORDERS[j], stage_no, False)
        add_pieces(up_part, view, up_recv[stage_no].at[j])
        if stage_no < 2 and j < UP_WHOLE:
            go_up(j, stage_no + 1)

    def down_rows(row):
        block = row // 320
        return (block // 4, (block // 2) % 2, block % 2, row % 320)

    def transpose_rows(at):
        second_t[:, at : at + CHUNK] = second[at : at + CHUNK, :].T

    def hidden(j, lo):
        here, cols = slice(lo, lo + rows), slice(j * TILE, (j + 1) * TILE)
        upper = jnp.dot(second[here, :], wide_buf[j % 2], preferred_element_type=F32)
        below = 0.5 * (1.0 + lax.erf(upper * ROOT_HALF))
        density = jnp.exp(-0.5 * upper * upper) * DENSITY_SCALE
        active[here, cols] = (upper * below).astype(BF)
        slope[here, cols] = (below + upper * density).astype(BF)

    def down_grad(lo):
        act = active[:, lo : lo + CHUNK].T
        grad = jnp.dot(act, low[...], preferred_element_type=F32).astype(BF)
        for s in range(0, CHUNK, 64):
            z, x, y, row = down_rows(lo + s)
            down_part[z, x, y, row : row + 64, :] = grad[s : s + 64, :]

    loads[0].wait()
    for j in range(tiles + 1):
        if j < tiles:
            fetch(j + 1)
            copies[j].wait()
        for part in range(2):
            if j < tiles:
                hidden(j, part * rows)
            if j:
                down_grad((j - 1) * TILE + part * CHUNK)
            if j == 0 and part == 0:
                loads[1].wait()
                for copy in swaps:
                    copy.wait_recv()
        if j < tiles:
            transpose_rows(j * CHUNK)
        else:
            transpose_rows(two - CHUNK)
        if j == 3:
            go_down(0, 0, 0)
            go_down(1, 0, 0)
    go_down(0, 0, 1)
    go_down(1, 0, 1)
    go_down(2, 0)
    for copy in swaps:
        copy.wait_send()
        sent.remove(copy)
    pl.semaphore_signal(ready_second, inc=1, device_id=sibling, device_id_type=MESH)

    for j in range(tiles):
        fetch(tiles + j + 1)
        copies[tiles + j].wait()
        cols = slice(j * TILE, (j + 1) * TILE)

        def hidden_back(i, carry, j=j, cols=cols):
            here = pl.ds(pl.multiple_of(i * CHUNK, CHUNK), CHUNK)
            grad = lax.dot_general(low[here, :], tall_buf[j % 2], NT, preferred_element_type=F32)
            slope[here, cols] = (grad * slope[here, cols].astype(F32)).astype(BF)
            return carry

        lax.fori_loop(0, two // CHUNK, hidden_back, 0)
        for m in range(4):
            grad = jnp.dot(
                second_t[m * 320 : (m + 1) * 320, :], slope[:, cols], preferred_element_type=F32
            ).astype(BF)
            for s in range(4):
                k = 4 * m + s
                up_part[j, k // 8, (k // 4) % 2, (k // 2) % 2, k % 2] = grad[s * 80 : (s + 1) * 80]
        go_up(j, 0)
        if j == 3:
            end_down(2, 0)
        if j == 4:
            end_down(0, 0)
            end_down(1, 0)
    pl.semaphore_signal(ready_low, inc=1, device_id=sibling, device_id_type=MESH)

    events = {
        0: [(end_down, 2, 1), (end_up, 0, 0)],
        2: [(end_up, 1, 0), (end_down, 0, 1)],
        4: [(end_down, 1, 1), (end_down, 2, 2)],
        5: [(end_up, 2, 0), (end_up, 0, 1)],
        6: [(end_up, 1, 1)],
        8: [(end_up, 2, 1), (end_up, 3, 0)],
        9: [
            (end_down, 0, 2), (end_down, 1, 2), (end_up, 0, 2), (end_up, 1, 2), (end_up, 2, 2),
            (end_up, 4, 0),
        ],
    }
    pending = []
    writes = {}

    def finish(step, buf, out, n, copy):
        copy.wait_recv()
        cols = slice(n * SPAN, (n + 1) * SPAN)
        stage[step % 2] = stage[step % 2] + buf[rows:, cols].astype(F32)
        writes[step] = pltpu.make_async_copy(stage.at[step % 2], out.at[:, cols], out_sem.at[step % 2])
        writes[step].start()

    for step in range(2 * spans):
        n = step // 2
        backward = step % 2 == 0
        buf, out = (second, back_out) if backward else (low, result_out)
        fetch(2 * tiles + step + 1)
        copies[2 * tiles + step].wait()
        cols = slice(n * SPAN, (n + 1) * SPAN)

        def product(lo, n=n, backward=backward):
            if backward:
                return lax.dot_general(
                    slope[lo : lo + rows, :], flat_buf[...], NT, preferred_element_type=F32
                )
            return jnp.dot(active[lo : lo + rows, :], thin_buf[...], preferred_element_type=F32)

        buf[:rows, cols] = product(rows).astype(BF)
        own = product(0)
        if n == 0:
            pl.semaphore_wait(ready_second if backward else ready_low, 1)
        copy = remote(
            buf.at[:rows, cols], buf.at[rows:, cols],
            swap_send.at[2 + step], swap_recv.at[2 + step], sibling,
        )
        sent.append(copy)
        if step >= 2:
            writes[step - 2].wait()
        stage[step % 2] = own
        if pending:
            finish(*pending.pop())
        pending.append((step, buf, out, n, copy))
        for event, item, stage_no in events.get(step, ()):
            event(item, stage_no)
    finish(*pending.pop())
    ends = [
        pltpu.make_async_copy(
            down_part.at[mine["z"], mine["x"], mine["y"]], down_out, end_sem.at[0]
        ),
        pltpu.make_async_copy(
            up_part.at[:UP_WHOLE, :, mine["z"], mine["x"], mine["y"]], up_out, end_sem.at[1]
        ),
        pltpu.make_async_copy(up_part.at[UP_WHOLE:, :, mine["z"]], up_rest, end_sem.at[2]),
    ]
    for copy in ends:
        copy.start()
    writes[2 * spans - 2].wait()
    writes[2 * spans - 1].wait()
    for copy in ends:
        copy.wait()
    for copy in sent:
        copy.wait_send()


def feed_forward_sum(second, low, up, down):
    rows, width = second.shape
    units = up.shape[1] // 2
    tiles = units // TILE
    two = 2 * rows
    anywhere = pl.BlockSpec(memory_space=pl.ANY)
    recv = []
    for lo, hi, _ in DOWN_ITEMS:
        recv += [
            pltpu.VMEM((2, 2, 320, hi - lo), BF),
            pltpu.VMEM((2, 320, hi - lo), BF),
            pltpu.VMEM((320, hi - lo), BF),
        ]
    recv += [
        pltpu.VMEM((tiles, 2, 2, 2, 80, TILE), BF),
        pltpu.VMEM((UP_WHOLE, 2, 2, 80, TILE), BF),
        pltpu.VMEM((UP_WHOLE, 2, 80, TILE), BF),
    ]
    dma = pltpu.SemaphoreType.DMA
    return pl.pallas_call(
        feed_sum_kernel,
        in_specs=[anywhere] * 4,
        out_specs=[anywhere] * 5,
        out_shape=[
            jax.ShapeDtypeStruct((rows, width), F32),
            jax.ShapeDtypeStruct((rows, width), F32),
            jax.ShapeDtypeStruct((320, width), BF),
            jax.ShapeDtypeStruct((UP_WHOLE, 2, 80, TILE), BF),
            jax.ShapeDtypeStruct((tiles - UP_WHOLE, 2, 2, 2, 80, TILE), BF),
        ],
        scratch_shapes=[
            pltpu.VMEM((two, width), BF),
            pltpu.VMEM((two, width), BF),
            pltpu.VMEM((width, two), BF),
            pltpu.VMEM((two, units), BF),
            pltpu.VMEM((two, units), BF),
            pltpu.VMEM((2, 2, 2, 320, width), BF),
            pltpu.VMEM((tiles, 2, 2, 2, 2, 80, TILE), BF),
            pltpu.VMEM((2, width, TILE), BF),
            pltpu.VMEM((2, TILE, width), BF),
            pltpu.VMEM((SPAN, units), BF),
            pltpu.VMEM((units, SPAN), BF),
            pltpu.VMEM((2, rows, SPAN), F32),
        ]
        + recv
        + [
            dma((2,)), dma((6,)), dma((2,)), dma((3,)), dma((12,)), dma((12,)), dma((27,)), dma((27,)),
            pltpu.SemaphoreType.REGULAR, pltpu.SemaphoreType.REGULAR,
        ],
        compiler_params=pltpu.CompilerParams(
            vmem_limit_bytes=VMEM_TOP, collective_id=0, has_side_effects=True
        ),
        cost_estimate=cost(2 * 6 * two * width * units, 6e7),
        name="feed_sum",
    )(second, low, up, down)


def swap(x, axis, mask):
    size = lax.axis_size(axis)
    return lax.ppermute(x, axis, [(i, i ^ mask) for i in range(size)])


def halve(x, dim, axis, bit):
    mine = (lax.axis_index(axis) >> bit) & 1
    send = lax.dynamic_index_in_dim(x, 1 - mine, dim, keepdims=False)
    keep = lax.dynamic_index_in_dim(x, mine, dim, keepdims=False)
    got = swap(send, axis, 1 << bit)
    return keep.astype(F32) + got.astype(F32)


def log2(n):
    return n.bit_length() - 1


def scatter_rows(x, order, names):
    names = list(names)
    for i, name in enumerate(order):
        x = halve(x.astype(BF), names.index(name), name[0], name[1])
        names.remove(name)
    return x


def sum_all(x):
    for bit in range(log2(lax.axis_size("chrom"))):
        x = x + swap(x, "chrom", 1 << bit)
    for bit in range(log2(lax.axis_size("cells"))):
        x = x + swap(x, "cells", 1 << bit)
    return x


def scatter_columns_split(x, order):
    cell_bits = log2(lax.axis_size("cells"))
    width = x.shape[1]
    names = [("cells", b) for b in reversed(range(cell_bits))] + [("chrom", 1)]
    x = x.reshape((2,) * (cell_bits + 1) + (-1, width))
    return place_columns(scatter_rows(x, order, names))


def place_columns(x):
    core = lax.axis_index("chrom") & 1
    x = x.reshape(2, -1, x.shape[-1])
    keep = lax.dynamic_index_in_dim(x, core, 0, keepdims=False)
    got = swap(lax.dynamic_index_in_dim(x, 1 - core, 0, keepdims=False).astype(BF), "chrom", 1).astype(F32)
    left = jnp.where(core == 0, keep, got)
    right = jnp.where(core == 0, got, keep)
    return jnp.concatenate([left, right], axis=1)


def scatter_rows_split(x, order):
    cell_bits = log2(lax.axis_size("cells"))
    width = x.shape[1]
    names = [("cells", b) for b in reversed(range(cell_bits - 1))] + [("chrom", 1)]
    x = x.reshape((2,) * cell_bits + (-1, width))
    return place_rows(scatter_rows(x, order, names))


def place_rows(x):
    cells = lax.axis_size("cells")
    chrom = lax.axis_size("chrom")
    core = lax.axis_index("chrom") & 1
    top = cells // 2
    high = lax.axis_index("cells") // top
    width = x.shape[1]
    pairs = []
    for cell in range(cells):
        for place in range(chrom):
            if (cell // top) != (place & 1):
                pairs.append((cell * chrom + place, (cell ^ top) * chrom + place))
    got = lax.ppermute(x.astype(BF), ("cells", "chrom"), pairs)
    x = (x.astype(F32) + got.astype(F32)).reshape(2, -1, width)
    keep = lax.dynamic_index_in_dim(x, core, 0, keepdims=False)
    send = lax.dynamic_index_in_dim(x, 1 - core, 0, keepdims=False).astype(BF)
    back = []
    for cell in range(cells):
        for place in range(chrom):
            if (cell // top) == (place & 1):
                back.append((cell * chrom + place, cell * chrom + (place ^ 1)))
    got = lax.ppermute(send, ("cells", "chrom"), back)
    return jnp.where(core == high, keep, got.astype(F32))


def feed_forward_plain(second_low, down_low, up_weight, down_weight):
    cell_bits = log2(lax.axis_size("cells"))
    core = lax.axis_index("chrom") & 1
    result_part, result_send, back_part, back_send, down_grad, up_grad = feed_forward(
        core[None].astype(jnp.int32),
        second_low,
        swap(second_low, "chrom", 1),
        down_low,
        swap(down_low, "chrom", 1),
        up_weight,
        down_weight,
    )
    second_back = back_part + swap(back_send, "chrom", 1).astype(F32)
    result_part = result_part + swap(result_send, "chrom", 1).astype(F32)
    low_bits = [("cells", b) for b in range(cell_bits - 1)]
    down_out = scatter_rows_split(down_grad, low_bits + [("chrom", 1)])
    up_out = scatter_columns_split(
        up_grad, [("chrom", 1)] + low_bits[::-1] + [("cells", cell_bits - 1)]
    )
    return second_back, result_part, down_out, up_out


def norm_rows(values, gain, shift):
    center = values - jnp.mean(values, axis=-1, keepdims=True)
    inverse = lax.rsqrt(jnp.mean(center * center, axis=-1, keepdims=True) + EPS)
    normed = center * inverse
    return (normed * gain + shift, normed, inverse)


def norm_back(grad_out, normed, inverse, gain):
    scaled = grad_out * gain
    grad_in = inverse * (
        scaled
        - jnp.mean(scaled, axis=-1, keepdims=True)
        - normed * jnp.mean(scaled * normed, axis=-1, keepdims=True)
    )
    return (grad_in, jnp.sum(grad_out * normed, axis=0), jnp.sum(grad_out, axis=0))


def contract(left, right):
    return lax.dot_general(left, right, TN, preferred_element_type=F32)


def back_through(grad, weight):
    return lax.dot_general(grad, weight, NT, preferred_element_type=F32)


def per_device(
    tokens,
    cotangent,
    block_lengths,
    group_ids,
    group_weights,
    first_gain,
    first_shift,
    query_weight,
    key_weight,
    value_weight,
    output_weight,
    second_gain,
    second_shift,
    up_weight,
    down_weight,
):
    cells_here, seq_here, width = tokens.shape
    rows = cells_here * seq_here
    parts = lax.axis_size("chrom")
    cell_bits = log2(lax.axis_size("cells"))
    seq_full = seq_here * parts
    nblocks = block_lengths.shape[1]
    block = seq_full // nblocks
    per = nblocks // parts
    wide = width // parts
    place = lax.axis_index("chrom")
    core = place & 1
    near = [place ^ r for r in range(parts)]

    valid = (jnp.arange(block)[None, None, :] < block_lengths[:, :, None]).reshape(
        cells_here, seq_full
    )
    local_valid = lax.dynamic_slice_in_dim(valid, place * seq_here, seq_here, 1)
    lens = jnp.concatenate(
        [lax.dynamic_slice_in_dim(block_lengths, n * per, per, 1) for n in near], axis=1
    )
    n_groups = group_weights.shape[0]
    cell_scale = jnp.sum(
        jnp.where(group_ids[:, None] == jnp.arange(n_groups)[None, :], group_weights[None, :], 0.0),
        axis=1,
    )

    def my_heads(weight):
        return lax.dynamic_slice_in_dim(weight, place * wide, wide, 1)

    qkv_weight = jnp.concatenate(
        [my_heads(query_weight), my_heads(key_weight), my_heads(value_weight)], axis=1
    )
    output_near = jnp.concatenate(
        [lax.dynamic_slice_in_dim(output_weight, n * wide, wide, 0) for n in near], axis=0
    )

    flat = tokens.reshape(rows, width).astype(F32)
    first_out, first_norm, first_inv = norm_rows(flat, first_gain, first_shift)
    first_low = first_out.astype(BF).reshape(cells_here, seq_here, width)
    first_all, mixed_near, kept = [], [], []
    for c in range(cells_here):
        mine = first_low[c]
        over = swap(mine, "chrom", 2)
        first_all.append([mine, swap(mine, "chrom", 1), over, swap(over, "chrom", 1)])
    for c in range(cells_here):
        mixed, qkv_c = attend(first_all[c], lens[c], qkv_weight, block)
        kept.append(qkv_c)
        mixed_near.append(
            jnp.concatenate([mixed[0]] + [swap(mixed[r], "chrom", r) for r in range(1, parts)], axis=1)
        )
    mixed_flat = jnp.concatenate(mixed_near, axis=0)

    middle = flat + jnp.dot(mixed_flat, output_near, preferred_element_type=F32)
    second_out, second_norm, second_inv = norm_rows(middle, second_gain, second_shift)
    second_low = second_out.astype(BF)
    result_back = (
        cotangent.astype(F32)
        * cell_scale[:, None, None]
        * local_valid.astype(F32)[:, :, None]
    ).reshape(rows, width)
    down_low = result_back.astype(BF)
    low_bits = [("cells", b) for b in range(cell_bits - 1)]
    if lax.axis_size("cells") == 8 and parts == 4:
        second_back, result_part, down_grad, up_grad, up_rest = feed_forward_sum(
            second_low, down_low, up_weight, down_weight
        )
        result = middle + result_part
        down_out = place_rows(down_grad)
        up_rest = halve(halve(up_rest, 2, "cells", 0).astype(BF), 2, "chrom", 1).astype(BF)
        up_grad = jnp.concatenate([up_grad, up_rest], axis=0)
        up_grad = up_grad.transpose(1, 2, 0, 3).reshape(2, 80, -1)
        up_out = place_columns(halve(up_grad, 0, "cells", 2))
    else:
        second_back, result_part, down_out, up_out = feed_forward_plain(
            second_low, down_low, up_weight, down_weight
        )
        result = middle + result_part
    result_cells = result.reshape(cells_here, seq_here, width)
    layer_out = result_cells.astype(BF)

    cls_rows = jnp.where(place == 0, result_cells[:, 0, :], 0.0)
    cls_total = jnp.sum(cls_rows, axis=0)
    cls_square = jnp.sum(cls_rows * cls_rows, axis=0)

    middle_ln, second_gain_grad, second_shift_grad = norm_back(
        second_back, second_norm, second_inv, second_gain
    )
    middle_back = result_back + middle_ln
    attend_low = middle_back.astype(BF)
    mixed_back = back_through(attend_low, output_near).astype(BF)
    output_grad = contract(mixed_flat, attend_low).reshape(parts, wide, width)
    output_grad = jnp.concatenate(
        [lax.dynamic_index_in_dim(output_grad, place ^ j, 0, keepdims=False) for j in range(parts)],
        axis=0,
    )
    half_width = width // 2
    output_half = lax.dynamic_slice_in_dim(output_grad, core * half_width, half_width, 1) + swap(
        lax.dynamic_slice_in_dim(output_grad, (1 - core) * half_width, half_width, 1).astype(BF),
        "chrom",
        1,
    ).astype(F32)
    output_out = scatter_columns_split(
        output_half.astype(BF), low_bits + [("cells", cell_bits - 1), ("chrom", 1)]
    )
    early = sum_all(jnp.stack([cls_total, cls_square, second_gain_grad, second_shift_grad]))

    mixed_back = mixed_back.reshape(cells_here, seq_here, width)
    heads_back = []
    for c in range(cells_here):
        pieces = [mixed_back[c, :, r * wide : (r + 1) * wide] for r in range(parts)]
        heads_back.append(
            [pieces[0]] + [swap(pieces[r], "chrom", r) for r in range(1, parts)]
        )
    qkv_grad = None
    first_back = []
    for c in range(cells_here):
        qkv_back = attend_back(heads_back[c], lens[c], kept[c], block)
        pieces = [back_through(g, qkv_weight) for g in qkv_back]
        sent = swap(jnp.stack([pieces[1].astype(BF), pieces[3].astype(BF)]), "chrom", 1).astype(F32)
        over = swap((pieces[2] + sent[1]).astype(BF), "chrom", 2)
        first_back.append(pieces[0] + sent[0] + over.astype(F32))
        part = contract(
            jnp.concatenate(first_all[c], axis=0), jnp.concatenate(qkv_back, axis=0)
        )
        qkv_grad = part if qkv_grad is None else qkv_grad + part
    first_back = jnp.concatenate(first_back, axis=0)

    names = [("cells", b) for b in reversed(range(cell_bits))]
    qkv_sum = scatter_rows(
        qkv_grad.reshape((2,) * cell_bits + (-1, 3 * wide)),
        [("cells", b) for b in range(cell_bits)],
        names,
    ).reshape(parts, -1, 3 * wide)
    pieces = [lax.dynamic_index_in_dim(qkv_sum, near[0], 0, keepdims=False)]
    for r in range(1, parts):
        piece = lax.dynamic_index_in_dim(qkv_sum, near[r], 0, keepdims=False).astype(BF)
        pieces.append(swap(piece, "chrom", r).astype(F32))
    pieces = jnp.stack(pieces)
    pieces = [lax.dynamic_index_in_dim(pieces, place ^ j, 0, keepdims=False) for j in range(parts)]
    query_out, key_out, value_out = [
        jnp.concatenate([p[:, i * wide : (i + 1) * wide] for p in pieces], axis=1) for i in range(3)
    ]

    first_ln, first_gain_grad, first_shift_grad = norm_back(
        first_back, first_norm, first_inv, first_gain
    )
    tokens_grad = (middle_back + first_ln).reshape(cells_here, seq_here, width)
    late = sum_all(jnp.stack([first_gain_grad, first_shift_grad]))

    count_cells = cells_here * lax.axis_size("cells")
    cls_mean = early[0] / count_cells
    cls_var = early[1] / count_cells - cls_mean * cls_mean
    share = width // (parts * lax.axis_size("cells"))
    start = (lax.axis_index("cells") * parts + place) * share

    def mine(vector):
        return lax.dynamic_slice_in_dim(vector, start, share, 0)

    return (
        layer_out,
        tokens_grad,
        mine(late[0]),
        mine(late[1]),
        query_out,
        key_out,
        value_out,
        output_out,
        mine(early[2]),
        mine(early[3]),
        up_out,
        down_out,
        cls_mean,
        cls_var,
    )


def solution(mesh):
    rows = P("cells", "chrom", None)
    both = ("cells", "chrom")
    in_specs = (rows, rows, P("cells", None), P("cells")) + (P(),) * 11
    out_specs = (
        (rows, rows)
        + (P(both), P(both))
        + (P(both, None),) * 4
        + (P(both), P(both))
        + (P(both, None), P(both, None))
        + (P(), P())
    )
    return jax.shard_map(
        per_device, mesh=mesh, in_specs=in_specs, out_specs=out_specs, check_vma=False
    )
```

```python
import functools
import itertools
import math

import jax
import jax.numpy as jnp
from jax import lax
from jax.experimental import pallas as pl
from jax.experimental.pallas import tpu as pltpu
from jax.sharding import PartitionSpec as P

HEAD_DIM = 64
FILLED = 768
EPS = 1e-05
ROOT_HALF = 0.7071067811865476
DENSITY_SCALE = 0.3989422804014327
LOG2E = 1.4426950408889634
BF = jnp.bfloat16
F32 = jnp.float32
NT = (((1,), (1,)), ((), ()))
TN = (((0,), (0,)), ((), ()))
VMEM_MAX = 60 * 2**20
VMEM_TOP = 63 * 2**20


def whole(shape):
    return pl.BlockSpec(shape, lambda *_: (0,) * len(shape), pipeline_mode=pl.Buffered(1))


def smem():
    return pl.BlockSpec(memory_space=pltpu.SMEM)


def cost(flops, moved, exps=0):
    return pl.CostEstimate(flops=int(flops), bytes_accessed=int(moved), transcendentals=int(exps))


def shift_rows(shape, dim, shift, length):
    slot = lax.broadcasted_iota(jnp.int32, shape, dim)
    row = lax.broadcasted_iota(jnp.int32, shape, 1 - dim)
    return jnp.where((row == slot + shift) & (slot < length), 1.0, 0.0).astype(BF)


def pack(packed, values, lens, part, block, at):
    per = values.shape[0] // block
    for b in range(per):
        here = lens[part * per + b]
        rows = values[b * block : (b + 1) * block, :]
        shift = at % 8
        base = pl.multiple_of(at - shift, 8) if part + b else 0
        move = shift_rows((block + 8, block), 1, shift, here)
        moved = jnp.dot(move, rows, preferred_element_type=F32)
        if part + b:
            packed[pl.ds(base, 8), :] += moved[:8, :]
            packed[pl.ds(pl.multiple_of(base + 8, 8), block), :] = moved[8:, :]
        else:
            packed[: block + 8, :] = moved
        at = at + here
    return at


def unpack(packed, out, lens, part, block, at):
    per = out.shape[0] // block
    for b in range(per):
        here = lens[part * per + b]
        shift = at % 8
        base = pl.multiple_of(at - shift, 8) if part + b else 0
        rows = packed[pl.ds(base, block + 8), :].astype(BF)
        move = shift_rows((block, block + 8), 0, shift, here)
        out[b * block : (b + 1) * block, :] = jnp.dot(
            move, rows, preferred_element_type=F32
        ).astype(BF)
        at = at + here
    return at


def attend_kernel(block, heads, lens, *refs):
    parts = 4
    firsts, weight = refs[:parts], refs[parts]
    mixed = refs[parts + 1 : 2 * parts + 1]
    qkv_c = refs[2 * parts + 1]
    query, packed = refs[2 * parts + 2 :]
    rows = firsts[0].shape[0]
    wide = heads * HEAD_DIM
    at = 0
    for r in range(parts):
        qkv = jnp.dot(firsts[r][...], weight[...], preferred_element_type=F32)
        query[r * rows : (r + 1) * rows, :] = qkv[:, :wide].astype(BF)
        at = pack(packed, qkv.astype(BF), lens, r, block, at)
    qkv_c[...] = packed[:FILLED, :].astype(BF)
    scale = LOG2E / math.sqrt(HEAD_DIM)
    ones = jnp.ones((FILLED, HEAD_DIM), BF)
    for r in range(parts):
        for h in range(heads):
            lo = h * HEAD_DIM
            q = query[r * rows : (r + 1) * rows, lo : lo + HEAD_DIM]
            k = qkv_c[:, wide + lo : wide + lo + HEAD_DIM]
            v = qkv_c[:, 2 * wide + lo : 2 * wide + lo + HEAD_DIM]
            s = lax.dot_general(q, k, NT, preferred_element_type=F32)
            top = jnp.max(s, axis=1, keepdims=True) * scale
            e = jnp.exp2(s * scale - top).astype(BF)
            o = jnp.dot(e, jnp.concatenate([v, ones], axis=1), preferred_element_type=F32)
            o = o[:, :HEAD_DIM] / o[:, HEAD_DIM:]
            mixed[r][:, lo : lo + HEAD_DIM] = o.astype(BF)


def attend(firsts, lens, weight, block):
    rows, width = firsts[0].shape
    wide3 = weight.shape[1]
    wide = wide3 // 3
    heads = wide // HEAD_DIM
    out = pl.pallas_call(
        functools.partial(attend_kernel, block, heads),
        in_specs=[smem()] + [whole((rows, width))] * 4 + [whole(weight.shape)],
        out_specs=[whole((rows, wide))] * 4 + [whole((FILLED, wide3))],
        out_shape=[jax.ShapeDtypeStruct((rows, wide), BF)] * 4
        + [jax.ShapeDtypeStruct((FILLED, wide3), BF)],
        scratch_shapes=[pltpu.VMEM((4 * rows, wide), BF), pltpu.VMEM((FILLED + block, wide3), F32)],
        compiler_params=pltpu.CompilerParams(vmem_limit_bytes=VMEM_MAX),
        cost_estimate=cost(2 * 4 * rows * width * wide3 + 4 * 4 * rows * FILLED * 256 * heads, 8e6),
        grid=(1,),
        name="attend",
    )(lens, *firsts, weight)
    return out[:4], out[4]


def attend_back_kernel(block, heads, lens, *refs):
    parts = 4
    grads, qkv_c = refs[:parts], refs[parts]
    outs = refs[parts + 1 : 2 * parts + 1]
    packed, back = refs[2 * parts + 1 :]
    wide = heads * HEAD_DIM
    at = 0
    for r in range(parts):
        at = pack(packed, grads[r][...], lens, r, block, at)
    scale = LOG2E / math.sqrt(HEAD_DIM)
    inv_root = 1.0 / math.sqrt(HEAD_DIM)
    chunk = 256
    back[FILLED:, :] = jnp.zeros((block, 3 * wide), F32)
    grad_t = packed[:FILLED, :].T
    query_t = qkv_c[:, :wide].astype(F32).T.astype(BF)
    key_t = qkv_c[:, wide : 2 * wide].astype(F32).T.astype(BF)
    for h in range(heads):
        lo = h * HEAD_DIM
        k = qkv_c[:, wide + lo : wide + lo + HEAD_DIM]
        v = qkv_c[:, 2 * wide + lo : 2 * wide + lo + HEAD_DIM]
        kt = key_t[lo : lo + HEAD_DIM, :]
        dv = jnp.zeros((FILLED, HEAD_DIM), F32)
        dk = jnp.zeros((FILLED, HEAD_DIM), F32)
        for c in range(0, FILLED, chunk):
            qt = query_t[lo : lo + HEAD_DIM, c : c + chunk]
            s = jnp.dot(k, qt, preferred_element_type=F32)
            top = jnp.max(s, axis=0, keepdims=True) * scale
            e = jnp.exp2(s * scale - top)
            inv = 1.0 / jnp.sum(e, axis=0, keepdims=True)
            gt = (grad_t[lo : lo + HEAD_DIM, c : c + chunk] * inv).astype(BF)
            dp = jnp.dot(v, gt, preferred_element_type=F32)
            inner = jnp.sum(e * dp, axis=0, keepdims=True) * inv
            ds = (e * (dp - inner)).astype(BF)
            dv = dv + lax.dot_general(e.astype(BF), gt, NT, preferred_element_type=F32)
            dk = dk + lax.dot_general(ds, qt, NT, preferred_element_type=F32)
            dqt = jnp.dot(kt, ds, preferred_element_type=F32)
            back[c : c + chunk, lo : lo + HEAD_DIM] = dqt.T * inv_root
        back[:FILLED, wide + lo : wide + lo + HEAD_DIM] = dk * inv_root
        back[:FILLED, 2 * wide + lo : 2 * wide + lo + HEAD_DIM] = dv
    at = 0
    for r in range(parts):
        at = unpack(back, outs[r], lens, r, block, at)


def attend_back(grads, lens, qkv_c, block):
    rows, wide = grads[0].shape
    heads = wide // HEAD_DIM
    return pl.pallas_call(
        functools.partial(attend_back_kernel, block, heads),
        in_specs=[smem()] + [whole((rows, wide))] * 4 + [whole(qkv_c.shape)],
        out_specs=[whole((rows, 3 * wide))] * 4,
        out_shape=[jax.ShapeDtypeStruct((rows, 3 * wide), BF)] * 4,
        scratch_shapes=[
            pltpu.VMEM((FILLED + block, wide), F32),
            pltpu.VMEM((FILLED + block, 3 * wide), F32),
        ],
        compiler_params=pltpu.CompilerParams(vmem_limit_bytes=VMEM_MAX),
        cost_estimate=cost(2 * 5 * FILLED * FILLED * 256 * heads, 6e6),
        grid=(1,),
        name="attend_back",
    )(lens, *grads, qkv_c)


FF_TILE = 512
FF_ROWS = 256
FF_GRAD = 256


def feed_kernel(half, second_a, second_b, low_a, low_b, up, down, *refs):
    result, send_result, back, send_back, down_grad, up_grad = refs[:6]
    second_t, active, upper_back, acc_result, acc_back = refs[6:]
    rows, width = second_a.shape
    tile = up.shape[1]
    step = pl.program_id(0)

    @pl.when(step == 0)
    def _():
        result[...] = jnp.zeros_like(result)
        back[...] = jnp.zeros_like(back)
        acc_result[...] = jnp.zeros_like(acc_result)
        acc_back[...] = jnp.zeros_like(acc_back)
        for part, ref in enumerate((second_a, second_b)):
            for lo in range(0, rows, FF_ROWS):
                at = part * rows + lo
                second_t[:, at : at + FF_ROWS] = ref[lo : lo + FF_ROWS, :].astype(F32).T.astype(BF)

    for part, (second, low, to_result, to_back) in enumerate(
        ((second_a, low_a, result, back), (second_b, low_b, acc_result, acc_back))
    ):

        def chunk(i, carry):
            here = pl.ds(pl.multiple_of(i * FF_ROWS, FF_ROWS), FF_ROWS)
            there = pl.ds(pl.multiple_of(part * rows + i * FF_ROWS, FF_ROWS), FF_ROWS)
            upper = jnp.dot(second[here, :], up[...], preferred_element_type=F32)
            grad = lax.dot_general(low[here, :], down[...], NT, preferred_element_type=F32)
            below = 0.5 * (1.0 + lax.erf(upper * ROOT_HALF))
            density = jnp.exp(-0.5 * upper * upper) * DENSITY_SCALE
            act = (upper * below).astype(BF)
            ub = (grad * (below + upper * density)).astype(BF)
            active[there, :] = act
            upper_back[there, :] = ub
            to_result[here, :] += jnp.dot(act, down[...], preferred_element_type=F32)
            to_back[here, :] += lax.dot_general(ub, up[...], NT, preferred_element_type=F32)
            return carry

        lax.fori_loop(0, rows // FF_ROWS, chunk, 0)

    def one_down(i, carry):
        here = pl.ds(pl.multiple_of(i * FF_GRAD, FF_GRAD), FF_GRAD)
        act = active[:, here].astype(F32).T.astype(BF)
        down_grad[here, :] = (
            jnp.dot(act[:, :rows], low_a[...], preferred_element_type=F32)
            + jnp.dot(act[:, rows:], low_b[...], preferred_element_type=F32)
        ).astype(BF)
        return carry

    lax.fori_loop(0, tile // FF_GRAD, one_down, 0)

    def one_up(i, carry):
        here = pl.ds(pl.multiple_of(i * FF_GRAD, FF_GRAD), FF_GRAD)
        up_grad[here, :] = jnp.dot(
            second_t[here, :], upper_back[...], preferred_element_type=F32
        ).astype(BF)
        return carry

    lax.fori_loop(0, width // FF_GRAD, one_up, 0)

    @pl.when(step == pl.num_programs(0) - 1)
    def _():
        send_result[...] = acc_result[...].astype(BF)
        send_back[...] = acc_back[...].astype(BF)


def feed_forward(half, second_a, second_b, low_a, low_b, up, down):
    rows, width = second_a.shape
    units = up.shape[1] // 2
    tiles = units // FF_TILE
    two = 2 * rows
    return pl.pallas_call(
        feed_kernel,
        grid_spec=pltpu.PrefetchScalarGridSpec(
            num_scalar_prefetch=1,
            grid=(tiles,),
            in_specs=[whole((rows, width))] * 4
            + [
                pl.BlockSpec((width, FF_TILE), lambda j, half: (0, half[0] * tiles + j)),
                pl.BlockSpec((FF_TILE, width), lambda j, half: (half[0] * tiles + j, 0)),
            ],
            out_specs=[whole((rows, width))] * 4
            + [
                pl.BlockSpec((FF_TILE, width), lambda j, half: (j, 0)),
                pl.BlockSpec((width, FF_TILE), lambda j, half: (0, j)),
            ],
            scratch_shapes=[
                pltpu.VMEM((width, two), BF),
                pltpu.VMEM((two, FF_TILE), BF),
                pltpu.VMEM((two, FF_TILE), BF),
                pltpu.VMEM((rows, width), F32),
                pltpu.VMEM((rows, width), F32),
            ],
        ),
        out_shape=[
            jax.ShapeDtypeStruct((rows, width), F32),
            jax.ShapeDtypeStruct((rows, width), BF),
            jax.ShapeDtypeStruct((rows, width), F32),
            jax.ShapeDtypeStruct((rows, width), BF),
            jax.ShapeDtypeStruct((units, width), BF),
            jax.ShapeDtypeStruct((width, units), BF),
        ],
        compiler_params=pltpu.CompilerParams(vmem_limit_bytes=VMEM_MAX),
        cost_estimate=cost(2 * 6 * two * width * units, 6e7),
        name="feed_forward",
    )(half, second_a, second_b, low_a, low_b, up, down)


MESH = pl.DeviceIdType.MESH
TILE = 512
SPAN = 256
CHUNK = 256
DOWN_ITEMS = ((0, 512, "xyz"), (512, 1024, "yxz"), (1024, 1280, "zxy"))
DOWN_CUT = 1024
UP_ORDERS = ("zxy", "zxy", "yxz", "zxy", "yxz")
UP_SLOT = (0, 1, 3, 2, 4)


def add_pieces(total, view, got):
    lead = len(total.shape) - 2
    tail = tuple(view[lead:]) + (slice(None),) * (len(total.shape) - max(len(view), lead))
    free = [i for i in range(lead) if isinstance(view[i], slice)]
    for pick in itertools.product(*[range(total.shape[i]) for i in free]):
        index = list(view[:lead])
        for i, n in zip(free, pick):
            index[i] = n
        here = tuple(index) + tail
        add = got[pick] if pick else got[...]
        total[here] = (total[here].astype(F32) + add.astype(F32)).astype(BF)


def feed_sum_kernel(
    second_in, low_in, up, down,
    back_out, result_out, down_ab, down_c, up_z, up_y,
    second, low, second_t, active, slope, down_part, up_part,
    wide_buf, tall_buf, flat_buf, thin_buf, stage,
    ra1, ra2, rb1, rb2, rc1, rc2, up_recv,
    load_sem, weight_sem, out_sem, end_sem, swap_send, swap_recv, sum_send, sum_recv,
    ready_second, ready_low,
):
    rows = low_in.shape[0]
    width = low_in.shape[1]
    two = 2 * rows
    units = active.shape[1]
    tiles = units // TILE
    spans = width // SPAN
    cell = lax.axis_index("cells")
    place = lax.axis_index("chrom")
    core = place % 2
    mine = {"y": place // 2, "x": cell % 2, "z": (cell // 2) % 2}
    sibling = (cell, place + 1 - 2 * core)
    near = {
        "y": (cell, place + 2 - 4 * mine["y"]),
        "x": (cell + 1 - 2 * mine["x"], place),
        "z": (cell + 2 - 4 * mine["z"], place),
    }

    barrier = pltpu.get_barrier_semaphore()
    for other in (sibling, near["x"], near["y"], near["z"]):
        pl.semaphore_signal(barrier, inc=1, device_id=other, device_id_type=MESH)
    loads = [
        pltpu.make_async_copy(second_in, second.at[:rows], load_sem.at[0]),
        pltpu.make_async_copy(low_in, low.at[:rows], load_sem.at[1]),
    ]
    for copy in loads:
        copy.start()
    base = core * units

    def weight_copy(kind, j, slot):
        if kind == "wide":
            src = up.at[:, pl.ds(pl.multiple_of(base + j * TILE, 128), TILE)]
            return pltpu.make_async_copy(src, wide_buf.at[slot], weight_sem.at[slot])
        if kind == "tall":
            src = down.at[pl.ds(pl.multiple_of(base + j * TILE, 128), TILE), :]
            return pltpu.make_async_copy(src, tall_buf.at[slot], weight_sem.at[2 + slot])
        if kind == "flat":
            src = up.at[j * SPAN : (j + 1) * SPAN, pl.ds(pl.multiple_of(base, 128), units)]
            return pltpu.make_async_copy(src, flat_buf, weight_sem.at[4])
        src = down.at[pl.ds(pl.multiple_of(base, 128), units), j * SPAN : (j + 1) * SPAN]
        return pltpu.make_async_copy(src, thin_buf, weight_sem.at[5])

    plan = (
        [("wide", j) for j in range(tiles)]
        + [("tall", j) for j in range(tiles)]
        + [(kind, j) for j in range(spans) for kind in ("flat", "thin")]
    )
    copies = {}

    def fetch(i):
        if i < len(plan):
            kind, j = plan[i]
            copies[i] = weight_copy(kind, j, j % 2)
            copies[i].start()

    fetch(0)
    pl.semaphore_wait(barrier, 4)

    def remote(src, dst, send, recv, device):
        copy = pltpu.make_async_remote_copy(
            src_ref=src, dst_ref=dst, send_sem=send, recv_sem=recv,
            device_id=device, device_id_type=MESH,
        )
        copy.start()
        return copy

    sent = []
    swaps = [
        remote(second_in, second.at[rows:], swap_send.at[0], swap_recv.at[0], sibling),
        remote(low_in, low.at[rows:], swap_send.at[1], swap_recv.at[1], sibling),
    ]
    sent += swaps

    flight = {}

    def down_view(order, stage_no, lo, hi, other, fix_z=None):
        index = {"z": slice(None), "x": slice(None), "y": slice(None)}
        for s, axis in enumerate(order[: stage_no + 1]):
            index[axis] = 1 - mine[axis] if (s == stage_no and other) else mine[axis]
        if fix_z is not None:
            index["z"] = fix_z
        return (index["z"], index["x"], index["y"], slice(None), slice(lo, hi))

    def up_view(order, stage_no, other):
        index = {"z": slice(None), "x": slice(None), "y": slice(None)}
        for s, axis in enumerate(order[: stage_no + 1]):
            index[axis] = 1 - mine[axis] if (s == stage_no and other) else mine[axis]
        return (slice(None), index["z"], index["x"], index["y"])

    down_recv = ((ra1, ra2), (rb1, rb2), (rc1, rc2))

    def go_down(item, stage_no, fix_z=None):
        lo, hi, order = DOWN_ITEMS[item]
        src = down_part.at[down_view(order, stage_no, lo, hi, True, fix_z)]
        dst = down_recv[item][stage_no]
        sem = item * 3 + stage_no
        if fix_z is not None:
            dst = dst.at[fix_z]
            sem = item * 3 + (2 if fix_z else 0)
        copy = remote(src, dst, sum_send.at[sem], sum_recv.at[sem], near[order[stage_no]])
        flight.setdefault(("d", item, stage_no), []).append(copy)
        sent.append(copy)

    def end_down(item, stage_no):
        lo, hi, order = DOWN_ITEMS[item]
        for copy in flight[("d", item, stage_no)]:
            copy.wait_recv()
        add_pieces(down_part, down_view(order, stage_no, lo, hi, False), down_recv[item][stage_no])
        if stage_no < 1:
            go_down(item, stage_no + 1)

    def go_up(j):
        order = UP_ORDERS[j]
        slot = UP_SLOT[j]
        copy = remote(
            up_part.at[slot].at[up_view(order, 0, True)], up_recv.at[slot],
            sum_send.at[9 + j], sum_recv.at[9 + j], near[order[0]],
        )
        flight[("u", j)] = copy
        sent.append(copy)

    def end_up(j, _):
        flight[("u", j)].wait_recv()
        slot = UP_SLOT[j]
        add_pieces(up_part, (slot,) + up_view(UP_ORDERS[j], 0, False), up_recv.at[slot])

    def down_rows(row):
        block = row // 320
        return (block // 4, (block // 2) % 2, block % 2, row % 320)

    def transpose_rows(at):
        second_t[:, at : at + CHUNK] = second[at : at + CHUNK, :].T

    def hidden(j, lo):
        here, cols = slice(lo, lo + rows), slice(j * TILE, (j + 1) * TILE)
        upper = jnp.dot(second[here, :], wide_buf[j % 2], preferred_element_type=F32)
        below = 0.5 * (1.0 + lax.erf(upper * ROOT_HALF))
        density = jnp.exp(-0.5 * upper * upper) * DENSITY_SCALE
        active[here, cols] = (upper * below).astype(BF)
        slope[here, cols] = (below + upper * density).astype(BF)

    def down_grad(lo):
        act = active[:, lo : lo + CHUNK].T
        grad = jnp.dot(act, low[...], preferred_element_type=F32).astype(BF)
        for s in range(0, CHUNK, 64):
            z, x, y, row = down_rows(lo + s)
            down_part[z, x, y, row : row + 64, :] = grad[s : s + 64, :]

    loads[0].wait()
    for j in range(tiles + 1):
        if j < tiles:
            fetch(j + 1)
            copies[j].wait()
        for part in range(2):
            if j < tiles:
                hidden(j, part * rows)
            if j:
                down_grad((j - 1) * TILE + part * CHUNK)
            if j == 0 and part == 0:
                loads[1].wait()
                for copy in swaps:
                    copy.wait_recv()
        if j < tiles:
            transpose_rows(j * CHUNK)
        else:
            transpose_rows(two - CHUNK)
        if j == 3:
            go_down(0, 0, 0)
            go_down(1, 0, 0)
    go_down(0, 0, 1)
    go_down(1, 0, 1)
    go_down(2, 0)
    for copy in swaps:
        copy.wait_send()
        sent[:] = [other for other in sent if other is not copy]
    pl.semaphore_signal(ready_second, inc=1, device_id=sibling, device_id_type=MESH)

    for j in range(tiles):
        fetch(tiles + j + 1)
        copies[tiles + j].wait()
        cols = slice(j * TILE, (j + 1) * TILE)

        def hidden_back(i, carry, j=j, cols=cols):
            here = pl.ds(pl.multiple_of(i * CHUNK, CHUNK), CHUNK)
            grad = lax.dot_general(low[here, :], tall_buf[j % 2], NT, preferred_element_type=F32)
            slope[here, cols] = (grad * slope[here, cols].astype(F32)).astype(BF)
            return carry

        lax.fori_loop(0, two // CHUNK, hidden_back, 0)
        for m in range(4):
            grad = jnp.dot(
                second_t[m * 320 : (m + 1) * 320, :], slope[:, cols], preferred_element_type=F32
            ).astype(BF)
            for s in range(4):
                k = 4 * m + s
                up_part[UP_SLOT[j], k // 8, (k // 4) % 2, (k // 2) % 2, k % 2] = grad[s * 80 : (s + 1) * 80]
        go_up(j)
    end_down(0, 0)
    pl.semaphore_signal(ready_low, inc=1, device_id=sibling, device_id_type=MESH)

    events = {
        0: [(end_down, 1, 0)],
        2: [(end_down, 2, 0)],
        8: [(end_up, 0, 0)],
        9: [
            (end_up, 2, 0), (end_down, 1, 1), (end_down, 2, 1), (end_up, 1, 0), (end_up, 3, 0),
            (end_up, 4, 0), (end_down, 0, 1),
        ],
    }
    pending = []
    writes = {}

    def finish(step, buf, out, n, copy):
        copy.wait_recv()
        cols = slice(n * SPAN, (n + 1) * SPAN)
        stage[step % 2] = stage[step % 2] + buf[rows:, cols].astype(F32)
        writes[step] = pltpu.make_async_copy(stage.at[step % 2], out.at[:, cols], out_sem.at[step % 2])
        writes[step].start()

    for step in range(2 * spans):
        n = step // 2
        backward = step % 2 == 0
        buf, out = (second, back_out) if backward else (low, result_out)
        fetch(2 * tiles + step + 1)
        copies[2 * tiles + step].wait()
        cols = slice(n * SPAN, (n + 1) * SPAN)

        def product(lo, n=n, backward=backward):
            if backward:
                return lax.dot_general(
                    slope[lo : lo + rows, :], flat_buf[...], NT, preferred_element_type=F32
                )
            return jnp.dot(active[lo : lo + rows, :], thin_buf[...], preferred_element_type=F32)

        buf[:rows, cols] = product(rows).astype(BF)
        own = product(0)
        if n == 0:
            pl.semaphore_wait(ready_second if backward else ready_low, 1)
        copy = remote(
            buf.at[:rows, cols], buf.at[rows:, cols],
            swap_send.at[2 + step], swap_recv.at[2 + step], sibling,
        )
        sent.append(copy)
        if step >= 2:
            writes[step - 2].wait()
        stage[step % 2] = own
        if pending:
            finish(*pending.pop())
        pending.append((step, buf, out, n, copy))
        for event, item, stage_no in events.get(step, ()):
            event(item, stage_no)
    finish(*pending.pop())
    views = (
        (down_part.at[:, mine["x"], mine["y"], :, :DOWN_CUT], down_ab),
        (down_part.at[mine["z"], mine["x"], :, :, DOWN_CUT:], down_c),
        (up_part.at[:3, :, mine["z"]], up_z),
        (up_part.at[3:, :, :, :, mine["y"]], up_y),
    )
    ends = [
        pltpu.make_async_copy(src, dst, end_sem.at[i]) for i, (src, dst) in enumerate(views)
    ]
    for copy in ends:
        copy.start()
    writes[2 * spans - 2].wait()
    writes[2 * spans - 1].wait()
    for copy in ends:
        copy.wait()
    for copy in sent:
        copy.wait_send()


def feed_forward_sum(second, low, up, down):
    rows, width = second.shape
    units = up.shape[1] // 2
    tiles = units // TILE
    two = 2 * rows
    anywhere = pl.BlockSpec(memory_space=pl.ANY)
    recv = []
    for lo, hi, _ in DOWN_ITEMS:
        recv += [
            pltpu.VMEM((2, 2, 320, hi - lo), BF),
            pltpu.VMEM((2, 320, hi - lo), BF),
        ]
    recv += [pltpu.VMEM((tiles, 2, 2, 2, 80, TILE), BF)]
    dma = pltpu.SemaphoreType.DMA
    return pl.pallas_call(
        feed_sum_kernel,
        in_specs=[anywhere] * 4,
        out_specs=[anywhere] * 6,
        out_shape=[
            jax.ShapeDtypeStruct((rows, width), F32),
            jax.ShapeDtypeStruct((rows, width), F32),
            jax.ShapeDtypeStruct((2, 320, DOWN_CUT), BF),
            jax.ShapeDtypeStruct((2, 320, width - DOWN_CUT), BF),
            jax.ShapeDtypeStruct((3, 2, 2, 2, 80, TILE), BF),
            jax.ShapeDtypeStruct((tiles - 3, 2, 2, 2, 80, TILE), BF),
        ],
        scratch_shapes=[
            pltpu.VMEM((two, width), BF),
            pltpu.VMEM((two, width), BF),
            pltpu.VMEM((width, two), BF),
            pltpu.VMEM((two, units), BF),
            pltpu.VMEM((two, units), BF),
            pltpu.VMEM((2, 2, 2, 320, width), BF),
            pltpu.VMEM((tiles, 2, 2, 2, 2, 80, TILE), BF),
            pltpu.VMEM((2, width, TILE), BF),
            pltpu.VMEM((2, TILE, width), BF),
            pltpu.VMEM((SPAN, units), BF),
            pltpu.VMEM((units, SPAN), BF),
            pltpu.VMEM((2, rows, SPAN), F32),
        ]
        + recv
        + [
            dma((2,)), dma((6,)), dma((2,)), dma((4,)), dma((12,)), dma((12,)), dma((14,)), dma((14,)),
            pltpu.SemaphoreType.REGULAR, pltpu.SemaphoreType.REGULAR,
        ],
        compiler_params=pltpu.CompilerParams(
            vmem_limit_bytes=VMEM_TOP, collective_id=0, has_side_effects=True
        ),
        cost_estimate=cost(2 * 6 * two * width * units, 6e7),
        name="feed_sum",
    )(second, low, up, down)


QUERY_ITEMS = ((0, 512, "xzh"), (512, 960, "zxh"))


def row_dot(left, right, exact_left):
    wide = right if exact_left else left
    high = wide.astype(BF)
    low = (wide - high.astype(F32)).astype(BF)
    pairs = ((left, high), (left, low)) if exact_left else ((high, right), (low, right))
    return sum(lax.dot_general(a, b, NT, preferred_element_type=F32) for a, b in pairs)


def attend_sum_kernel(
    block, heads,
    lens, g0, g1, g2, g3, kept, *refs
):
    firsts = refs[:12]
    (
        weight, up_z_in, up_y_in, out_in, down_ab_in, down_c_in, early_in, tokens_in, through_in, gain,
        tokens_out, query_out, up_z_out, up_y_out, out_out, down_out, early_out, late_out,
        grads, qkv_c, first, weights, back, moved, total, query_part,
        up_z, up_y, out_part, down_ab, down_c, down_part, got_ab, got_c,
        keep_back, got_near, got_far, got_over,
        qa1, qa2, qa3, qb1, qb2, qb3, query_last, query_got,
        uz1, uz2, uz3, up_z_last, up_z_got, uy1, uy2, uy3, up_y_last, up_y_got,
        oc1, oc2, oc3, oc4, oc5, out_last, out_got, down_got, down_last, early, early_got, late, late_got, column_sum, norm_in,
        load_sem, first_sem, turn_send, turn_recv, back_send, back_recv, sum_send, sum_recv, end_sem, norm_sem,
    ) = refs[12:]
    sources = (g0, g1, g2, g3)
    cells = kept.shape[0]
    rows = g0.shape[1]
    wide = heads * HEAD_DIM
    cell = lax.axis_index("cells")
    place = lax.axis_index("chrom")
    core = place % 2
    mine = {"c": core, "y": place // 2, "x": cell % 2, "z": (cell // 2) % 2, "h": cell // 4}

    def chrom_near(r):
        return (place // 2 + r // 2) % 2 * 2 + (core + r % 2) % 2

    near = {
        "c": (cell, chrom_near(1)),
        "y": (cell, chrom_near(2)),
        "x": (cell + 1 - 2 * mine["x"], place),
        "z": (cell + 2 - 4 * mine["z"], place),
        "h": (cell + 4 - 8 * mine["h"], place),
    }
    far = (cell, chrom_near(3))
    by_part = (None, near["c"], near["y"], far)

    barrier = pltpu.get_barrier_semaphore()
    for other in (*near.values(), far):
        pl.semaphore_signal(barrier, inc=1, device_id=other, device_id_type=MESH)

    def load(src, dst, sem):
        copy = pltpu.make_async_copy(src, dst, sem)
        copy.start()
        return copy

    def load_own(c):
        return [
            load(g0.at[c], grads.at[c, 0], load_sem.at[2 * c]),
            load(kept.at[c], qkv_c.at[c % 2], load_sem.at[2 * c + 1]),
        ]

    own_loads = {c: load_own(c) for c in range(2)}
    extra = [
        load(down_ab_in, down_ab, load_sem.at[6]),
        load(down_c_in, down_c, load_sem.at[11]),
        load(up_z_in, up_z, load_sem.at[7]),
        load(up_y_in, up_y, load_sem.at[8]),
        load(out_in, out_part, load_sem.at[9]),
        load(weight, weights, load_sem.at[10]),
    ]

    def load_first(c):
        return [
            load(
                firsts[4 * c + r],
                first.at[c % 2, r * rows : (r + 1) * rows],
                first_sem.at[4 * c + r],
            )
            for r in range(4)
        ]

    first_loads = {c: load_first(c) for c in range(2)}
    early_load = load(early_in, early.at[0], load_sem.at[12])
    pl.semaphore_wait(barrier, 6)

    def remote(src, dst, send, recv, device, start=True):
        copy = pltpu.make_async_remote_copy(
            src_ref=src, dst_ref=dst, send_sem=send, recv_sem=recv,
            device_id=device, device_id_type=MESH,
        )
        if start:
            copy.start()
        return copy

    sent = []

    def turn(c):
        line = []
        for r in (2, 3, 1):
            n = 3 * c + r - 1
            line.append(
                remote(sources[r].at[c], grads.at[c, r], turn_send.at[n], turn_recv.at[n], by_part[r])
            )
        sent.extend(line)
        return line

    turns = {0: turn(0)}

    sems = iter(range(64))
    items = {}

    def item(name, part, dims, stages, recvs, cols=slice(None)):
        items[name] = (part, dims, stages, recvs, cols, [next(sems) for _ in stages], {})

    item("uz", up_z, "*hxy", "xyh", (uz1, uz2, uz3))
    item("uy", up_y, "*hzx", "zxh", (uy1, uy2, uy3))
    item("o", out_part, "chzxy", "czxyh", (oc1, oc2, oc3, oc4, oc5))
    item("da", down_ab, "z", "z", (got_ab,))
    item("dc", down_c, "y", "y", (got_c,))
    for n, (lo, hi, stages) in enumerate(QUERY_ITEMS):
        item("q%d" % n, query_part, "hzx", stages, ((qa1, qa2, qa3), (qb1, qb2, qb3))[n], slice(lo, hi))

    def view(name, s, other):
        _, dims, stages, _, cols, _, _ = items[name]
        index = [slice(None)] * len(dims)
        for t, axis in enumerate(stages[: s + 1]):
            index[dims.index(axis)] = 1 - mine[axis] if (t == s and other) else mine[axis]
        return tuple(index) + (slice(None), cols)

    def go(name, s):
        part, _, stages, recvs, _, ids, flight = items[name]
        copy = remote(
            part.at[view(name, s, True)], recvs[s],
            sum_send.at[ids[s]], sum_recv.at[ids[s]], near[stages[s]],
        )
        flight[s] = copy
        sent.append(copy)

    def end(name, s):
        part, _, stages, recvs, _, _, flight = items[name]
        flight[s].wait_recv()
        add_pieces(part, view(name, s, False), recvs[s])
        if s + 1 < len(stages):
            go(name, s + 1)

    lasts = {
        "uz": (up_z, up_z_last, up_z_got, next(sems)),
        "uy": (up_y, up_y_last, up_y_got, next(sems)),
        "o": (out_part, out_last, out_got, next(sems)),
    }

    def swap_last(name, _):
        part, last, got, sem = lasts[name]
        at = view(name, len(items[name][2]) - 1, False)
        half = part.shape[-2] // 2
        tiles = part.shape[0] if name != "o" else 1
        for t in range(tiles):
            here = (t,) + at[1:] if name != "o" else at
            values = part[here]
            for k in range(2):
                last[k, t] = values[k * half : (k + 1) * half]
        copy = remote(last.at[1 - core], got, sum_send.at[sem], sum_recv.at[sem], near["c"])
        sent.append(copy)
        items[name][6]["last"] = copy

    down_sems = (next(sems), next(sems))

    def down_far():
        return remote(
            down_part, down_got, sum_send.at[down_sems[0]], sum_recv.at[down_sems[0]], near["h"], False
        )

    def down_near():
        return remote(
            down_part.at[1 - core], down_last, sum_send.at[down_sems[1]], sum_recv.at[down_sems[1]],
            near["c"], False,
        )

    def down_start(*_):
        for k in range(2):
            half = slice(k * 160, (k + 1) * 160)
            down_part[k, :, :DOWN_CUT] = down_ab[mine["z"], half, :]
            down_part[k, :, DOWN_CUT:] = down_c[mine["y"], half, :]

        @pl.when(core != mine["h"])
        def _():
            down_far().start()

    def down_add(*_):
        @pl.when(core == mine["h"])
        def _():
            down_far().wait_recv()
            for k in range(2):
                down_part[k] = (down_part[k].astype(F32) + down_got[k].astype(F32)).astype(BF)
            down_near().start()
            down_last[...] = down_part[core]

    def down_end(*_):
        @pl.when(core != mine["h"])
        def _():
            down_far().wait_send()
            down_near().wait_recv()

        @pl.when(core == mine["h"])
        def _():
            down_near().wait_send()

    vectors = {"early": (early, early_got, 26), "late": (late, late_got, 31)}

    def vector_go(name, s):
        stack, got, sem = vectors[name]
        copy = remote(
            stack.at[s], got.at[s], sum_send.at[sem + s], sum_recv.at[sem + s], near["cyxzh"[s]]
        )
        flights[name, s] = copy
        sent.append(copy)

    def vector_end(name, s):
        stack, got, _ = vectors[name]
        flights[name, s].wait_recv()
        stack[s + 1] = stack[s] + got[s]
        if s < 4:
            vector_go(name, s + 1)

    flights = {}

    for copy in extra:
        copy.wait()
    go("da", 0)
    go("dc", 0)
    go("uz", 0)
    go("uy", 0)
    go("o", 0)
    early_load.wait()
    vector_go("early", 0)

    near_copies, over_copies, norm_loads = {}, {}, {}

    def back_sum(c, _):
        near_copies[c][1].wait_recv()
        mid = slice(512, 768)
        first[c % 2, mid] = (first[c % 2, mid].astype(F32) + got_far[c].astype(F32)).astype(BF)
        over_copies[c] = remote(
            first.at[c % 2, mid], got_over.at[c], back_send.at[3 * c + 2], back_recv.at[3 * c + 2], near["y"]
        )
        sent.append(over_copies[c])
        norm_loads[c] = [
            load(tokens_in.at[c], norm_in, norm_sem.at[2 * c]),
            load(through_in.at[c], got_far.at[c], norm_sem.at[2 * c + 1]),
        ]

    def back_end(c, _):
        near_copies[c][0].wait_recv()
        over_copies[c].wait_recv()
        for copy in norm_loads[c]:
            copy.wait()

        def some(i, carry):
            here = pl.ds(pl.multiple_of(i * 64, 64), 64)
            values = norm_in[here, :].astype(F32)
            center = values - jnp.mean(values, axis=1, keepdims=True)
            inverse = lax.rsqrt(jnp.mean(center * center, axis=1, keepdims=True) + EPS)
            normed = center * inverse
            scaled = keep_back[c, here, :] + got_near[c, here, :].astype(F32)
            scaled = (scaled + got_over[c, here, :].astype(F32)) * gain[...]
            keep_back[c, here, :] = got_far[c, here, :].astype(F32) + inverse * (
                scaled
                - jnp.mean(scaled, axis=1, keepdims=True)
                - normed * jnp.mean(scaled * normed, axis=1, keepdims=True)
            )
            return carry

        lax.fori_loop(0, rows // 64, some, 0)
        ends.append(load(keep_back.at[c], tokens_out.at[c], end_sem.at[c]))
        if c + 2 < cells:
            for copy in (*near_copies[c], over_copies[c]):
                copy.wait_send()
                sent[:] = [other for other in sent if other is not copy]
            first_loads[c + 2] = load_first(c + 2)

    ends = []
    events = {
        (0, 0): [(end, "o", 0), (vector_end, "early", 0)],
        (0, 1): [(vector_end, "early", 1)],
        (0, 2): [(end, "dc", 0), (vector_end, "early", 2)],
        (0, 3): [(end, "uz", 0), (vector_end, "early", 3)],
        (0, 4): [(end, "uy", 0), (end, "da", 0), (down_start, 0, 0), (vector_end, "early", 4)],
        (0, 6): [(end, "uy", 1)],
        (1, 0): [(end, "uz", 1), (back_sum, 0, 0)],
        (1, 1): [(end, "o", 1)],
        (1, 2): [(end, "uy", 2), (swap_last, "uy", 0), (down_add, 0, 0)],
        (1, 3): [(end, "o", 2)],
        (1, 4): [(end, "uz", 2), (swap_last, "uz", 0), (down_end, 0, 0)],
        (1, 5): [(end, "o", 3)],
        (1, 6): [(back_end, 0, 0)],
        (2, 0): [(end, "o", 4), (swap_last, "o", 0), (back_sum, 1, 0)],
        (2, 4): [(back_end, 1, 0)],
    }

    def run(key):
        for event, a, b in events.get(key, ()):
            event(a, b)

    scale = LOG2E / math.sqrt(HEAD_DIM)
    inv_root = 1.0 / math.sqrt(HEAD_DIM)
    chunk = 256
    per = rows // block
    for c in range(cells):
        own_loads[c][0].wait()
        own_loads[c][1].wait()
        for copy in turns[c]:
            copy.wait_recv()
        if c + 1 < cells:
            turns[c + 1] = turn(c + 1)
        ranks, columns = [], []
        at = 0
        for b in range(4 * per):
            slot = lax.broadcasted_iota(jnp.int32, (1, block), 1)
            ranks.append(jnp.where(slot < lens[c, b], slot + at, -1))
            slot = lax.broadcasted_iota(jnp.int32, (block, 1), 0)
            columns.append(jnp.where(slot < lens[c, b], slot + at, -1))
            at = at + lens[c, b]
        packed = jnp.zeros((wide, FILLED), F32)
        for r in range(4):
            rank = jnp.concatenate(ranks[r * per : (r + 1) * per], axis=1)
            line = lax.broadcasted_iota(jnp.int32, (FILLED, rows), 0)
            move = jnp.where(line == rank, 1.0, 0.0).astype(BF)
            grad = grads[c, r].astype(F32).T.astype(BF)
            packed = packed + lax.dot_general(grad, move, NT, preferred_element_type=F32)
        query_t = qkv_c[c % 2, :, :wide].astype(F32).T.astype(BF)
        key_t = qkv_c[c % 2, :, wide : 2 * wide].astype(F32).T.astype(BF)
        for h in range(heads):
            lo = h * HEAD_DIM
            k = qkv_c[c % 2, :, wide + lo : wide + lo + HEAD_DIM]
            v = qkv_c[c % 2, :, 2 * wide + lo : 2 * wide + lo + HEAD_DIM]
            kt = key_t[lo : lo + HEAD_DIM, :]
            dv = jnp.zeros((FILLED, HEAD_DIM), F32)
            dk = jnp.zeros((FILLED, HEAD_DIM), F32)
            for w in range(0, FILLED, chunk):
                qt = query_t[lo : lo + HEAD_DIM, w : w + chunk]
                s = jnp.dot(k, qt, preferred_element_type=F32)
                top = jnp.max(s, axis=0, keepdims=True) * scale
                e = jnp.exp2(s * scale - top)
                inv = 1.0 / jnp.sum(e, axis=0, keepdims=True)
                gt = (packed[lo : lo + HEAD_DIM, w : w + chunk] * inv).astype(BF)
                dp = jnp.dot(v, gt, preferred_element_type=F32)
                inner = jnp.sum(e * dp, axis=0, keepdims=True) * inv
                ds = (e * (dp - inner)).astype(BF)
                dv = dv + lax.dot_general(e.astype(BF), gt, NT, preferred_element_type=F32)
                dk = dk + lax.dot_general(ds, qt, NT, preferred_element_type=F32)
                dqt = jnp.dot(kt, ds, preferred_element_type=F32)
                back[w : w + chunk, lo : lo + HEAD_DIM] = (dqt.T * inv_root).astype(BF)
            back[:, wide + lo : wide + lo + HEAD_DIM] = (dk * inv_root).astype(BF)
            back[:, 2 * wide + lo : 2 * wide + lo + HEAD_DIM] = dv.astype(BF)
            run((c, h))
        if c + 2 < cells:
            own_loads[c + 2] = load_own(c + 2)
        for r in range(4):
            rank = jnp.concatenate(columns[r * per : (r + 1) * per], axis=0)
            line = lax.broadcasted_iota(jnp.int32, (rows, FILLED), 1)
            move = jnp.where(line == rank, 1.0, 0.0).astype(BF)
            moved[r * rows : (r + 1) * rows, :] = jnp.dot(
                move, back[...], preferred_element_type=F32
            ).astype(BF)
        for copy in first_loads[c]:
            copy.wait()
        ones = jnp.ones((8, 4 * rows), BF)
        part = jnp.dot(ones, moved[...], preferred_element_type=F32)
        column_sum[...] = part + column_sum[...] if c else part
        for m in range(first.shape[2] // CHUNK):
            cols = slice(m * CHUNK, (m + 1) * CHUNK)
            part = jnp.dot(first[c % 2, :, cols].T, moved[...], preferred_element_type=F32)
            if c:
                part = part + total[cols, :]
            if c < cells - 1:
                total[cols, :] = part
            else:
                product = part * weights[cols, :].astype(F32)
                late[0, :, cols] = row_dot(ones[:, : 3 * wide], product, True)
                low = part.astype(BF)
                for s in range(0, CHUNK, 32):
                    row = m * CHUNK + s
                    n = row // 160
                    query_part[n // 4, (n // 2) % 2, n % 2, row % 160 : row % 160 + 32, :] = low[s : s + 32, :]
        if c == cells - 1:
            go("q0", 0)
            go("q1", 0)
            line = lax.broadcasted_iota(jnp.int32, late.shape[1:], 0)
            late[0] = jnp.where(line == 0, late[0], row_dot(column_sum[...], weights[...], False))
            vector_go("late", 0)
        run((c, 5))
        lines = []
        for r in (3, 1, 2, 0):
            part = lax.dot_general(
                moved[r * rows : (r + 1) * rows, :], weights[...], NT, preferred_element_type=F32
            )
            if r == 0:
                keep_back[c] = part
                continue
            spot = {1: slice(0, 256), 2: slice(512, 768), 3: slice(256, 512)}[r]
            first[c % 2, spot] = part.astype(BF)
            if r != 2:
                n = 3 * c + (1 if r == 3 else 0)
                copy = remote(
                    first.at[c % 2, spot], (got_far if r == 3 else got_near).at[c],
                    back_send.at[n], back_recv.at[n], near["c"],
                )
                lines.insert(0, copy)
                sent.append(copy)
        near_copies[c] = lines
        run((c, 6))
    back_sum(cells - 1, 0)
    vector_end("late", 0)
    end("q0", 0)
    end("q1", 0)
    vector_end("late", 1)
    end("q1", 1)
    end("q0", 1)
    vector_end("late", 2)
    back_end(cells - 1, 0)
    vector_end("late", 3)
    end("q0", 2)
    end("q1", 2)
    vector_end("late", 4)
    values = query_part[mine["h"], mine["z"], mine["x"]]
    for j in range(4):
        query_last[j] = values[j * 40 : (j + 1) * 40]
    last_query = []
    for r in range(1, 4):
        sem = next(sems)
        copy = remote(
            query_last.at[chrom_near(r)], query_got.at[r], sum_send.at[sem], sum_recv.at[sem], by_part[r]
        )
        last_query.append(copy)
        sent.append(copy)
    query_got[0] = query_last[place]
    n = cells
    for name, out in (("uz", up_z_out), ("uy", up_y_out), ("o", out_out)):
        _, last, got, _ = lasts[name]
        items[name][6]["last"].wait_recv()
        ends.append(load(last.at[core], out.at[0], end_sem.at[n]))
        ends.append(load(got, out.at[1], end_sem.at[n + 1]))
        n += 2
    ends.append(load(down_last, down_out, end_sem.at[n]))
    ends.append(load(early.at[5], early_out, end_sem.at[n + 2]))
    ends.append(load(late.at[5], late_out, end_sem.at[n + 3]))
    for copy in last_query:
        copy.wait_recv()
    ends.append(load(query_got, query_out, end_sem.at[n + 1]))
    for copy in ends:
        copy.wait()
    for copy in sent:
        copy.wait_send()


def attend_sum(
    lens, grads, kept, firsts, weight, up_z, up_y, out_part, down_ab, down_c, early, tokens, through, gain, block
):
    cells, rows, wide = grads[0].shape
    width = firsts[0].shape[1]
    heads = wide // HEAD_DIM
    seq = 4 * rows
    anywhere = pl.BlockSpec(memory_space=pl.ANY)
    dma = pltpu.SemaphoreType.DMA
    vmem = lambda *shape: pltpu.VMEM(shape, BF)
    qa, qb = [hi - lo for lo, hi, _ in QUERY_ITEMS]
    return pl.pallas_call(
        functools.partial(attend_sum_kernel, block, heads),
        in_specs=[smem()] + [anywhere] * (5 + 12 + 9) + [pl.BlockSpec(memory_space=pltpu.VMEM)],
        out_specs=[anywhere] * 8,
        out_shape=[
            jax.ShapeDtypeStruct((cells, rows, width), F32),
            jax.ShapeDtypeStruct((4, 40, 3 * wide), BF),
            jax.ShapeDtypeStruct((2, 3, 40, TILE), BF),
            jax.ShapeDtypeStruct((2, 2, 40, TILE), BF),
            jax.ShapeDtypeStruct((2, 1, 40, width // 2), BF),
            jax.ShapeDtypeStruct((160, width), BF),
            jax.ShapeDtypeStruct((8, width), F32),
            jax.ShapeDtypeStruct((8, width), F32),
        ],
        scratch_shapes=[
            vmem(cells, 4, rows, wide),
            vmem(2, FILLED, 3 * wide),
            vmem(2, seq, width),
            vmem(width, 3 * wide),
            vmem(FILLED, 3 * wide),
            vmem(seq, 3 * wide),
            pltpu.VMEM((width, 3 * wide), F32),
            vmem(2, 2, 2, 160, 3 * wide),
            vmem(*up_z.shape), vmem(*up_y.shape), vmem(*out_part.shape), vmem(*down_ab.shape), vmem(*down_c.shape),
            vmem(2, 160, width), vmem(*down_ab.shape[1:]), vmem(*down_c.shape[1:]),
            pltpu.VMEM((cells, rows, width), F32),
            vmem(cells, rows, width), vmem(cells, rows, width), vmem(cells, rows, width),
            vmem(2, 2, 160, qa), vmem(2, 160, qa), vmem(160, qa),
            vmem(2, 2, 160, qb), vmem(2, 160, qb), vmem(160, qb),
            vmem(4, 40, 3 * wide), vmem(4, 40, 3 * wide),
            vmem(3, 2, 2, 80, TILE), vmem(3, 2, 80, TILE), vmem(3, 80, TILE),
            vmem(2, 3, 40, TILE), vmem(3, 40, TILE),
            vmem(2, 2, 2, 80, TILE), vmem(2, 2, 80, TILE), vmem(2, 80, TILE),
            vmem(2, 2, 40, TILE), vmem(2, 40, TILE),
            vmem(2, 2, 2, 2, 80, width // 2), vmem(2, 2, 2, 80, width // 2), vmem(2, 2, 80, width // 2),
            vmem(2, 80, width // 2), vmem(80, width // 2),
            vmem(2, 1, 40, width // 2), vmem(1, 40, width // 2),
            vmem(2, 160, width), vmem(160, width),
            pltpu.VMEM((6, 8, width), F32), pltpu.VMEM((5, 8, width), F32),
            pltpu.VMEM((6, 8, width), F32), pltpu.VMEM((5, 8, width), F32),
            pltpu.VMEM((8, 3 * wide), F32), vmem(rows, width),
            dma((13,)), dma((12,)), dma((9,)), dma((9,)), dma((9,)), dma((9,)), dma((36,)), dma((36,)),
            dma((16,)), dma((2 * cells,)),
        ],
        compiler_params=pltpu.CompilerParams(
            vmem_limit_bytes=VMEM_TOP, collective_id=1, has_side_effects=True
        ),
        cost_estimate=cost(8e10, 6e7),
        name="attend_sum",
    )(
        lens, *grads, kept, *firsts, weight, up_z, up_y, out_part, down_ab, down_c, early, tokens, through, gain
    )


def swap(x, axis, mask):
    size = lax.axis_size(axis)
    return lax.ppermute(x, axis, [(i, i ^ mask) for i in range(size)])


def halve(x, dim, axis, bit):
    mine = (lax.axis_index(axis) >> bit) & 1
    send = lax.dynamic_index_in_dim(x, 1 - mine, dim, keepdims=False)
    keep = lax.dynamic_index_in_dim(x, mine, dim, keepdims=False)
    got = swap(send, axis, 1 << bit)
    return keep.astype(F32) + got.astype(F32)


def log2(n):
    return n.bit_length() - 1


def scatter_rows(x, order, names):
    names = list(names)
    for i, name in enumerate(order):
        x = halve(x.astype(BF), names.index(name), name[0], name[1])
        names.remove(name)
    return x


def sum_all(x):
    for bit in range(log2(lax.axis_size("chrom"))):
        x = x + swap(x, "chrom", 1 << bit)
    for bit in range(log2(lax.axis_size("cells"))):
        x = x + swap(x, "cells", 1 << bit)
    return x


def scatter_columns_split(x, order):
    cell_bits = log2(lax.axis_size("cells"))
    width = x.shape[1]
    names = [("cells", b) for b in reversed(range(cell_bits))] + [("chrom", 1)]
    x = x.reshape((2,) * (cell_bits + 1) + (-1, width))
    return place_columns(scatter_rows(x, order, names))


def place_columns(x):
    core = lax.axis_index("chrom") & 1
    x = x.reshape(2, -1, x.shape[-1])
    keep = lax.dynamic_index_in_dim(x, core, 0, keepdims=False)
    got = swap(lax.dynamic_index_in_dim(x, 1 - core, 0, keepdims=False).astype(BF), "chrom", 1).astype(F32)
    left = jnp.where(core == 0, keep, got)
    right = jnp.where(core == 0, got, keep)
    return jnp.concatenate([left, right], axis=1)


def scatter_rows_split(x, order):
    cell_bits = log2(lax.axis_size("cells"))
    width = x.shape[1]
    names = [("cells", b) for b in reversed(range(cell_bits - 1))] + [("chrom", 1)]
    x = x.reshape((2,) * cell_bits + (-1, width))
    return place_rows(scatter_rows(x, order, names))


def place_rows(x):
    cells = lax.axis_size("cells")
    chrom = lax.axis_size("chrom")
    core = lax.axis_index("chrom") & 1
    top = cells // 2
    high = lax.axis_index("cells") // top
    width = x.shape[1]
    pairs = []
    for cell in range(cells):
        for place in range(chrom):
            if (cell // top) != (place & 1):
                pairs.append((cell * chrom + place, (cell ^ top) * chrom + place))
    got = lax.ppermute(x.astype(BF), ("cells", "chrom"), pairs)
    x = (x.astype(F32) + got.astype(F32)).reshape(2, -1, width)
    keep = lax.dynamic_index_in_dim(x, core, 0, keepdims=False)
    send = lax.dynamic_index_in_dim(x, 1 - core, 0, keepdims=False).astype(BF)
    back = []
    for cell in range(cells):
        for place in range(chrom):
            if (cell // top) == (place & 1):
                back.append((cell * chrom + place, cell * chrom + (place ^ 1)))
    got = lax.ppermute(send, ("cells", "chrom"), back)
    return jnp.where(core == high, keep, got.astype(F32))


def feed_forward_plain(second_low, down_low, up_weight, down_weight):
    cell_bits = log2(lax.axis_size("cells"))
    core = lax.axis_index("chrom") & 1
    result_part, result_send, back_part, back_send, down_grad, up_grad = feed_forward(
        core[None].astype(jnp.int32),
        second_low,
        swap(second_low, "chrom", 1),
        down_low,
        swap(down_low, "chrom", 1),
        up_weight,
        down_weight,
    )
    second_back = back_part + swap(back_send, "chrom", 1).astype(F32)
    result_part = result_part + swap(result_send, "chrom", 1).astype(F32)
    low_bits = [("cells", b) for b in range(cell_bits - 1)]
    down_out = scatter_rows_split(down_grad, low_bits + [("chrom", 1)])
    up_out = scatter_columns_split(
        up_grad, [("chrom", 1)] + low_bits[::-1] + [("cells", cell_bits - 1)]
    )
    return second_back, result_part, down_out, up_out


def norm_rows(values, gain, shift):
    center = values - jnp.mean(values, axis=-1, keepdims=True)
    inverse = lax.rsqrt(jnp.mean(center * center, axis=-1, keepdims=True) + EPS)
    normed = center * inverse
    return (normed * gain + shift, normed, inverse)


def norm_back(grad_out, normed, inverse, gain):
    scaled = grad_out * gain
    grad_in = inverse * (
        scaled
        - jnp.mean(scaled, axis=-1, keepdims=True)
        - normed * jnp.mean(scaled * normed, axis=-1, keepdims=True)
    )
    return (grad_in, jnp.sum(grad_out * normed, axis=0), jnp.sum(grad_out, axis=0))


def contract(left, right):
    return lax.dot_general(left, right, TN, preferred_element_type=F32)


def back_through(grad, weight):
    return lax.dot_general(grad, weight, NT, preferred_element_type=F32)


def per_device(
    tokens,
    cotangent,
    block_lengths,
    group_ids,
    group_weights,
    first_gain,
    first_shift,
    query_weight,
    key_weight,
    value_weight,
    output_weight,
    second_gain,
    second_shift,
    up_weight,
    down_weight,
):
    cells_here, seq_here, width = tokens.shape
    rows = cells_here * seq_here
    parts = lax.axis_size("chrom")
    cell_bits = log2(lax.axis_size("cells"))
    seq_full = seq_here * parts
    nblocks = block_lengths.shape[1]
    block = seq_full // nblocks
    per = nblocks // parts
    wide = width // parts
    place = lax.axis_index("chrom")
    core = place & 1
    near = [place ^ r for r in range(parts)]

    valid = (jnp.arange(block)[None, None, :] < block_lengths[:, :, None]).reshape(
        cells_here, seq_full
    )
    local_valid = lax.dynamic_slice_in_dim(valid, place * seq_here, seq_here, 1)
    lens = jnp.concatenate(
        [lax.dynamic_slice_in_dim(block_lengths, n * per, per, 1) for n in near], axis=1
    )
    n_groups = group_weights.shape[0]
    cell_scale = jnp.sum(
        jnp.where(group_ids[:, None] == jnp.arange(n_groups)[None, :], group_weights[None, :], 0.0),
        axis=1,
    )

    def my_heads(weight):
        return lax.dynamic_slice_in_dim(weight, place * wide, wide, 1)

    qkv_weight = jnp.concatenate(
        [my_heads(query_weight), my_heads(key_weight), my_heads(value_weight)], axis=1
    )
    output_near = jnp.concatenate(
        [lax.dynamic_slice_in_dim(output_weight, n * wide, wide, 0) for n in near], axis=0
    )

    flat = tokens.reshape(rows, width).astype(F32)
    first_out, first_norm, first_inv = norm_rows(flat, first_gain, first_shift)
    first_low = first_out.astype(BF).reshape(cells_here, seq_here, width)
    first_all, mixed_near, kept = [], [], []
    for c in range(cells_here):
        mine = first_low[c]
        over = swap(mine, "chrom", 2)
        first_all.append([mine, swap(mine, "chrom", 1), over, swap(over, "chrom", 1)])
    for c in range(cells_here):
        if c:
            first_all[c], mixed_near[-1] = lax.optimization_barrier((first_all[c], mixed_near[-1]))
        mixed, qkv_c = attend(first_all[c], lens[c], qkv_weight, block)
        kept.append(qkv_c)
        mixed_near.append(
            jnp.concatenate([mixed[0]] + [swap(mixed[r], "chrom", r) for r in range(1, parts)], axis=1)
        )
    mixed_flat = jnp.concatenate(mixed_near, axis=0)

    middle = flat + jnp.dot(mixed_flat, output_near, preferred_element_type=F32)
    second_out, second_norm, second_inv = norm_rows(middle, second_gain, second_shift)
    second_low = second_out.astype(BF)
    result_back = (
        cotangent.astype(F32)
        * cell_scale[:, None, None]
        * local_valid.astype(F32)[:, :, None]
    ).reshape(rows, width)
    down_low = result_back.astype(BF)
    low_bits = [("cells", b) for b in range(cell_bits - 1)]
    fused = lax.axis_size("cells") == 8 and parts == 4
    if fused:
        second_back, result_part, down_ab, down_c, up_z, up_y = feed_forward_sum(
            second_low, down_low, up_weight, down_weight
        )
    else:
        second_back, result_part, down_out, up_out = feed_forward_plain(
            second_low, down_low, up_weight, down_weight
        )
    result = middle + result_part
    result_cells = result.reshape(cells_here, seq_here, width)
    layer_out = result_cells.astype(BF)

    cls_rows = jnp.where(place == 0, result_cells[:, 0, :], 0.0)
    cls_total = jnp.sum(cls_rows, axis=0)
    cls_square = jnp.sum(cls_rows * cls_rows, axis=0)

    middle_ln, second_gain_grad, second_shift_grad = norm_back(
        second_back, second_norm, second_inv, second_gain
    )
    middle_back = result_back + middle_ln
    attend_low = middle_back.astype(BF)
    output_grad = contract(mixed_flat, attend_low).reshape(parts, wide, width)
    output_grad = jnp.concatenate(
        [lax.dynamic_index_in_dim(output_grad, place ^ j, 0, keepdims=False) for j in range(parts)],
        axis=0,
    )
    early = jnp.stack([cls_total, cls_square, second_gain_grad, second_shift_grad])

    if fused:
        grads_near = [
            back_through(attend_low, output_near[r * wide : (r + 1) * wide])
            .astype(BF)
            .reshape(cells_here, seq_here, wide)
            for r in range(parts)
        ]
        output_part = output_grad.astype(BF).reshape(2, 2, 2, 2, 80, 2, width // 2)
        tokens_grad, qkv_got, up_z, up_y, out_two, down_grad, early, late = attend_sum(
            lens,
            grads_near,
            jnp.stack(kept),
            [piece for line in first_all for piece in line],
            qkv_weight,
            up_z,
            up_y,
            output_part.transpose(5, 0, 1, 2, 3, 4, 6),
            down_ab,
            down_c,
            jnp.concatenate([early, jnp.zeros_like(early)], axis=0),
            tokens,
            attend_low.reshape(cells_here, seq_here, width),
            first_gain[None, :],
            block,
        )
        late = jnp.stack([(late[0] - first_shift * late[1]) / first_gain, late[1]])
        down_out = down_grad.astype(F32)

        def both_cores(two):
            two = two.transpose(0, 2, 1, 3).reshape(2, two.shape[2], -1)
            swapped = jnp.where(core == 0, two, two[::-1])
            return jnp.concatenate([swapped[0], swapped[1]], axis=1).astype(F32)

        up_two = jnp.stack([up_z[:, 0], up_z[:, 1], up_y[:, 0], up_z[:, 2], up_y[:, 1]], axis=1)
        up_out = both_cores(up_two)
        output_out = both_cores(out_two)
        pieces = [
            lax.dynamic_index_in_dim(qkv_got, place ^ j, 0, keepdims=False).astype(F32)
            for j in range(parts)
        ]
    else:
        half_width = width // 2
        output_half = lax.dynamic_slice_in_dim(output_grad, core * half_width, half_width, 1) + swap(
            lax.dynamic_slice_in_dim(output_grad, (1 - core) * half_width, half_width, 1).astype(BF),
            "chrom",
            1,
        ).astype(F32)
        output_out = scatter_columns_split(
            output_half.astype(BF), low_bits + [("cells", cell_bits - 1), ("chrom", 1)]
        )
        mixed_back = back_through(attend_low, output_near).astype(BF)
        mixed_back = mixed_back.reshape(cells_here, seq_here, width)
        heads_back = []
        for c in range(cells_here):
            pieces = [mixed_back[c, :, r * wide : (r + 1) * wide] for r in range(parts)]
            heads_back.append(
                [pieces[0]] + [swap(pieces[r], "chrom", r) for r in range(1, parts)]
            )
        qkv_grad = None
        first_back = []
        for c in range(cells_here):
            qkv_back = attend_back(heads_back[c], lens[c], kept[c], block)
            pieces = [back_through(g, qkv_weight) for g in qkv_back]
            sent = swap(jnp.stack([pieces[1].astype(BF), pieces[3].astype(BF)]), "chrom", 1).astype(F32)
            over = swap((pieces[2] + sent[1]).astype(BF), "chrom", 2)
            first_back.append(pieces[0] + sent[0] + over.astype(F32))
            part = contract(
                jnp.concatenate(first_all[c], axis=0), jnp.concatenate(qkv_back, axis=0)
            )
            qkv_grad = part if qkv_grad is None else qkv_grad + part
        first_back = jnp.concatenate(first_back, axis=0)

        names = [("cells", b) for b in reversed(range(cell_bits))]
        qkv_sum = scatter_rows(
            qkv_grad.reshape((2,) * cell_bits + (-1, 3 * wide)),
            [("cells", b) for b in range(cell_bits)],
            names,
        ).reshape(parts, -1, 3 * wide)
        pieces = [lax.dynamic_index_in_dim(qkv_sum, near[0], 0, keepdims=False)]
        for r in range(1, parts):
            piece = lax.dynamic_index_in_dim(qkv_sum, near[r], 0, keepdims=False).astype(BF)
            pieces.append(swap(piece, "chrom", r).astype(F32))
        pieces = jnp.stack(pieces)
        pieces = [lax.dynamic_index_in_dim(pieces, place ^ j, 0, keepdims=False) for j in range(parts)]
        first_ln, first_gain_grad, first_shift_grad = norm_back(
            first_back, first_norm, first_inv, first_gain
        )
        tokens_grad = (middle_back + first_ln).reshape(cells_here, seq_here, width)
        early = sum_all(early)
        late = sum_all(jnp.stack([first_gain_grad, first_shift_grad]))
    query_out, key_out, value_out = [
        jnp.concatenate([p[:, i * wide : (i + 1) * wide] for p in pieces], axis=1) for i in range(3)
    ]

    count_cells = cells_here * lax.axis_size("cells")
    cls_mean = early[0] / count_cells
    cls_var = early[1] / count_cells - cls_mean * cls_mean
    share = width // (parts * lax.axis_size("cells"))
    start = (lax.axis_index("cells") * parts + place) * share

    def mine(vector):
        return lax.dynamic_slice_in_dim(vector, start, share, 0)

    return (
        layer_out,
        tokens_grad,
        mine(late[0]),
        mine(late[1]),
        query_out,
        key_out,
        value_out,
        output_out,
        mine(early[2]),
        mine(early[3]),
        up_out,
        down_out,
        cls_mean,
        cls_var,
    )


def solution(mesh):
    rows = P("cells", "chrom", None)
    both = ("cells", "chrom")
    in_specs = (rows, rows, P("cells", None), P("cells")) + (P(),) * 11
    out_specs = (
        (rows, rows)
        + (P(both), P(both))
        + (P(both, None),) * 4
        + (P(both), P(both))
        + (P(both, None), P(both, None))
        + (P(), P())
    )
    return jax.shard_map(
        per_device, mesh=mesh, in_specs=in_specs, out_specs=out_specs, check_vma=False
    )
```

```python
import functools
import itertools
import math

import jax
import jax.numpy as jnp
from jax import lax
from jax.experimental import pallas as pl
from jax.experimental.pallas import tpu as pltpu
from jax.sharding import PartitionSpec as P

HEAD_DIM = 64
FILLED = 768
EPS = 1e-05
ROOT_HALF = 0.7071067811865476
DENSITY_SCALE = 0.3989422804014327
LOG2E = 1.4426950408889634
BF = jnp.bfloat16
F32 = jnp.float32
NT = (((1,), (1,)), ((), ()))
TN = (((0,), (0,)), ((), ()))
VMEM_MAX = 60 * 2**20
VMEM_TOP = 63 * 2**20


def whole(shape):
    return pl.BlockSpec(shape, lambda *_: (0,) * len(shape), pipeline_mode=pl.Buffered(1))


def smem():
    return pl.BlockSpec(memory_space=pltpu.SMEM)


def cost(flops, moved, exps=0):
    return pl.CostEstimate(flops=int(flops), bytes_accessed=int(moved), transcendentals=int(exps))


def shift_rows(shape, dim, shift, length):
    slot = lax.broadcasted_iota(jnp.int32, shape, dim)
    row = lax.broadcasted_iota(jnp.int32, shape, 1 - dim)
    return jnp.where((row == slot + shift) & (slot < length), 1.0, 0.0).astype(BF)


def pack(packed, values, lens, part, block, at):
    per = values.shape[0] // block
    for b in range(per):
        here = lens[part * per + b]
        rows = values[b * block : (b + 1) * block, :]
        shift = at % 8
        base = pl.multiple_of(at - shift, 8) if part + b else 0
        move = shift_rows((block + 8, block), 1, shift, here)
        moved = jnp.dot(move, rows, preferred_element_type=F32)
        if part + b:
            packed[pl.ds(base, 8), :] += moved[:8, :]
            packed[pl.ds(pl.multiple_of(base + 8, 8), block), :] = moved[8:, :]
        else:
            packed[: block + 8, :] = moved
        at = at + here
    return at


def unpack(packed, out, lens, part, block, at):
    per = out.shape[0] // block
    for b in range(per):
        here = lens[part * per + b]
        shift = at % 8
        base = pl.multiple_of(at - shift, 8) if part + b else 0
        rows = packed[pl.ds(base, block + 8), :].astype(BF)
        move = shift_rows((block, block + 8), 0, shift, here)
        out[b * block : (b + 1) * block, :] = jnp.dot(
            move, rows, preferred_element_type=F32
        ).astype(BF)
        at = at + here
    return at


def attend_kernel(block, heads, lens, *refs):
    parts = 4
    firsts, weight = refs[:parts], refs[parts]
    mixed = refs[parts + 1 : 2 * parts + 1]
    qkv_c = refs[2 * parts + 1]
    query, packed = refs[2 * parts + 2 :]
    rows = firsts[0].shape[0]
    wide = heads * HEAD_DIM
    at = 0
    for r in range(parts):
        qkv = jnp.dot(firsts[r][...], weight[...], preferred_element_type=F32)
        query[r * rows : (r + 1) * rows, :] = qkv[:, :wide].astype(BF)
        at = pack(packed, qkv.astype(BF), lens, r, block, at)
    qkv_c[...] = packed[:FILLED, :].astype(BF)
    scale = LOG2E / math.sqrt(HEAD_DIM)
    ones = jnp.ones((FILLED, HEAD_DIM), BF)
    for r in range(parts):
        for h in range(heads):
            lo = h * HEAD_DIM
            q = query[r * rows : (r + 1) * rows, lo : lo + HEAD_DIM]
            k = qkv_c[:, wide + lo : wide + lo + HEAD_DIM]
            v = qkv_c[:, 2 * wide + lo : 2 * wide + lo + HEAD_DIM]
            s = lax.dot_general(q, k, NT, preferred_element_type=F32)
            top = jnp.max(s, axis=1, keepdims=True) * scale
            e = jnp.exp2(s * scale - top).astype(BF)
            o = jnp.dot(e, jnp.concatenate([v, ones], axis=1), preferred_element_type=F32)
            o = o[:, :HEAD_DIM] / o[:, HEAD_DIM:]
            mixed[r][:, lo : lo + HEAD_DIM] = o.astype(BF)


def attend(firsts, lens, weight, block):
    rows, width = firsts[0].shape
    wide3 = weight.shape[1]
    wide = wide3 // 3
    heads = wide // HEAD_DIM
    out = pl.pallas_call(
        functools.partial(attend_kernel, block, heads),
        in_specs=[smem()] + [whole((rows, width))] * 4 + [whole(weight.shape)],
        out_specs=[whole((rows, wide))] * 4 + [whole((FILLED, wide3))],
        out_shape=[jax.ShapeDtypeStruct((rows, wide), BF)] * 4
        + [jax.ShapeDtypeStruct((FILLED, wide3), BF)],
        scratch_shapes=[pltpu.VMEM((4 * rows, wide), BF), pltpu.VMEM((FILLED + block, wide3), F32)],
        compiler_params=pltpu.CompilerParams(vmem_limit_bytes=VMEM_MAX),
        cost_estimate=cost(2 * 4 * rows * width * wide3 + 4 * 4 * rows * FILLED * 256 * heads, 8e6),
        grid=(1,),
        name="attend",
    )(lens, *firsts, weight)
    return out[:4], out[4]


def attend_back_kernel(block, heads, lens, *refs):
    parts = 4
    grads, qkv_c = refs[:parts], refs[parts]
    outs = refs[parts + 1 : 2 * parts + 1]
    packed, back = refs[2 * parts + 1 :]
    wide = heads * HEAD_DIM
    at = 0
    for r in range(parts):
        at = pack(packed, grads[r][...], lens, r, block, at)
    scale = LOG2E / math.sqrt(HEAD_DIM)
    inv_root = 1.0 / math.sqrt(HEAD_DIM)
    chunk = 256
    back[FILLED:, :] = jnp.zeros((block, 3 * wide), F32)
    grad_t = packed[:FILLED, :].T
    query_t = qkv_c[:, :wide].astype(F32).T.astype(BF)
    key_t = qkv_c[:, wide : 2 * wide].astype(F32).T.astype(BF)
    for h in range(heads):
        lo = h * HEAD_DIM
        k = qkv_c[:, wide + lo : wide + lo + HEAD_DIM]
        v = qkv_c[:, 2 * wide + lo : 2 * wide + lo + HEAD_DIM]
        kt = key_t[lo : lo + HEAD_DIM, :]
        dv = jnp.zeros((FILLED, HEAD_DIM), F32)
        dk = jnp.zeros((FILLED, HEAD_DIM), F32)
        for c in range(0, FILLED, chunk):
            qt = query_t[lo : lo + HEAD_DIM, c : c + chunk]
            s = jnp.dot(k, qt, preferred_element_type=F32)
            top = jnp.max(s, axis=0, keepdims=True) * scale
            e = jnp.exp2(s * scale - top)
            inv = 1.0 / jnp.sum(e, axis=0, keepdims=True)
            gt = (grad_t[lo : lo + HEAD_DIM, c : c + chunk] * inv).astype(BF)
            dp = jnp.dot(v, gt, preferred_element_type=F32)
            inner = jnp.sum(e * dp, axis=0, keepdims=True) * inv
            ds = (e * (dp - inner)).astype(BF)
            dv = dv + lax.dot_general(e.astype(BF), gt, NT, preferred_element_type=F32)
            dk = dk + lax.dot_general(ds, qt, NT, preferred_element_type=F32)
            dqt = jnp.dot(kt, ds, preferred_element_type=F32)
            back[c : c + chunk, lo : lo + HEAD_DIM] = dqt.T * inv_root
        back[:FILLED, wide + lo : wide + lo + HEAD_DIM] = dk * inv_root
        back[:FILLED, 2 * wide + lo : 2 * wide + lo + HEAD_DIM] = dv
    at = 0
    for r in range(parts):
        at = unpack(back, outs[r], lens, r, block, at)


def attend_back(grads, lens, qkv_c, block):
    rows, wide = grads[0].shape
    heads = wide // HEAD_DIM
    return pl.pallas_call(
        functools.partial(attend_back_kernel, block, heads),
        in_specs=[smem()] + [whole((rows, wide))] * 4 + [whole(qkv_c.shape)],
        out_specs=[whole((rows, 3 * wide))] * 4,
        out_shape=[jax.ShapeDtypeStruct((rows, 3 * wide), BF)] * 4,
        scratch_shapes=[
            pltpu.VMEM((FILLED + block, wide), F32),
            pltpu.VMEM((FILLED + block, 3 * wide), F32),
        ],
        compiler_params=pltpu.CompilerParams(vmem_limit_bytes=VMEM_MAX),
        cost_estimate=cost(2 * 5 * FILLED * FILLED * 256 * heads, 6e6),
        grid=(1,),
        name="attend_back",
    )(lens, *grads, qkv_c)


FF_TILE = 512
FF_ROWS = 256
FF_GRAD = 256


def feed_kernel(half, second_a, second_b, low_a, low_b, up, down, *refs):
    result, send_result, back, send_back, down_grad, up_grad = refs[:6]
    second_t, active, upper_back, acc_result, acc_back = refs[6:]
    rows, width = second_a.shape
    tile = up.shape[1]
    step = pl.program_id(0)

    @pl.when(step == 0)
    def _():
        result[...] = jnp.zeros_like(result)
        back[...] = jnp.zeros_like(back)
        acc_result[...] = jnp.zeros_like(acc_result)
        acc_back[...] = jnp.zeros_like(acc_back)
        for part, ref in enumerate((second_a, second_b)):
            for lo in range(0, rows, FF_ROWS):
                at = part * rows + lo
                second_t[:, at : at + FF_ROWS] = ref[lo : lo + FF_ROWS, :].astype(F32).T.astype(BF)

    for part, (second, low, to_result, to_back) in enumerate(
        ((second_a, low_a, result, back), (second_b, low_b, acc_result, acc_back))
    ):

        def chunk(i, carry):
            here = pl.ds(pl.multiple_of(i * FF_ROWS, FF_ROWS), FF_ROWS)
            there = pl.ds(pl.multiple_of(part * rows + i * FF_ROWS, FF_ROWS), FF_ROWS)
            upper = jnp.dot(second[here, :], up[...], preferred_element_type=F32)
            grad = lax.dot_general(low[here, :], down[...], NT, preferred_element_type=F32)
            below = 0.5 * (1.0 + lax.erf(upper * ROOT_HALF))
            density = jnp.exp(-0.5 * upper * upper) * DENSITY_SCALE
            act = (upper * below).astype(BF)
            ub = (grad * (below + upper * density)).astype(BF)
            active[there, :] = act
            upper_back[there, :] = ub
            to_result[here, :] += jnp.dot(act, down[...], preferred_element_type=F32)
            to_back[here, :] += lax.dot_general(ub, up[...], NT, preferred_element_type=F32)
            return carry

        lax.fori_loop(0, rows // FF_ROWS, chunk, 0)

    def one_down(i, carry):
        here = pl.ds(pl.multiple_of(i * FF_GRAD, FF_GRAD), FF_GRAD)
        act = active[:, here].astype(F32).T.astype(BF)
        down_grad[here, :] = (
            jnp.dot(act[:, :rows], low_a[...], preferred_element_type=F32)
            + jnp.dot(act[:, rows:], low_b[...], preferred_element_type=F32)
        ).astype(BF)
        return carry

    lax.fori_loop(0, tile // FF_GRAD, one_down, 0)

    def one_up(i, carry):
        here = pl.ds(pl.multiple_of(i * FF_GRAD, FF_GRAD), FF_GRAD)
        up_grad[here, :] = jnp.dot(
            second_t[here, :], upper_back[...], preferred_element_type=F32
        ).astype(BF)
        return carry

    lax.fori_loop(0, width // FF_GRAD, one_up, 0)

    @pl.when(step == pl.num_programs(0) - 1)
    def _():
        send_result[...] = acc_result[...].astype(BF)
        send_back[...] = acc_back[...].astype(BF)


def feed_forward(half, second_a, second_b, low_a, low_b, up, down):
    rows, width = second_a.shape
    units = up.shape[1] // 2
    tiles = units // FF_TILE
    two = 2 * rows
    return pl.pallas_call(
        feed_kernel,
        grid_spec=pltpu.PrefetchScalarGridSpec(
            num_scalar_prefetch=1,
            grid=(tiles,),
            in_specs=[whole((rows, width))] * 4
            + [
                pl.BlockSpec((width, FF_TILE), lambda j, half: (0, half[0] * tiles + j)),
                pl.BlockSpec((FF_TILE, width), lambda j, half: (half[0] * tiles + j, 0)),
            ],
            out_specs=[whole((rows, width))] * 4
            + [
                pl.BlockSpec((FF_TILE, width), lambda j, half: (j, 0)),
                pl.BlockSpec((width, FF_TILE), lambda j, half: (0, j)),
            ],
            scratch_shapes=[
                pltpu.VMEM((width, two), BF),
                pltpu.VMEM((two, FF_TILE), BF),
                pltpu.VMEM((two, FF_TILE), BF),
                pltpu.VMEM((rows, width), F32),
                pltpu.VMEM((rows, width), F32),
            ],
        ),
        out_shape=[
            jax.ShapeDtypeStruct((rows, width), F32),
            jax.ShapeDtypeStruct((rows, width), BF),
            jax.ShapeDtypeStruct((rows, width), F32),
            jax.ShapeDtypeStruct((rows, width), BF),
            jax.ShapeDtypeStruct((units, width), BF),
            jax.ShapeDtypeStruct((width, units), BF),
        ],
        compiler_params=pltpu.CompilerParams(vmem_limit_bytes=VMEM_MAX),
        cost_estimate=cost(2 * 6 * two * width * units, 6e7),
        name="feed_forward",
    )(half, second_a, second_b, low_a, low_b, up, down)


MESH = pl.DeviceIdType.MESH
TILE = 512
SPAN = 256
CHUNK = 256
DOWN_ITEMS = ((0, 512, "xyz"), (512, 1024, "yxz"), (1024, 1280, "zxy"))
DOWN_CUT = 1024
UP_ORDERS = ("zxy", "zxy", "yxz", "zxy", "yxz")
UP_SLOT = (0, 1, 3, 2, 4)


def add_pieces(total, view, got):
    lead = len(total.shape) - 2
    tail = tuple(view[lead:]) + (slice(None),) * (len(total.shape) - max(len(view), lead))
    free = [i for i in range(lead) if isinstance(view[i], slice)]
    for pick in itertools.product(*[range(total.shape[i]) for i in free]):
        index = list(view[:lead])
        for i, n in zip(free, pick):
            index[i] = n
        here = tuple(index) + tail
        add = got[pick] if pick else got[...]
        total[here] = (total[here].astype(F32) + add.astype(F32)).astype(BF)


def feed_sum_kernel(
    second_in, low_in, up, down,
    back_out, result_out, down_ab, down_c, up_z, up_y,
    second, low, second_t, active, slope, down_part, up_part,
    wide_buf, tall_buf, flat_buf, thin_buf, stage,
    ra1, ra2, rb1, rb2, rc1, rc2, up_recv,
    load_sem, weight_sem, out_sem, end_sem, swap_send, swap_recv, sum_send, sum_recv,
    ready_second, ready_low,
):
    rows = low_in.shape[0]
    width = low_in.shape[1]
    two = 2 * rows
    units = active.shape[1]
    tiles = units // TILE
    spans = width // SPAN
    cell = lax.axis_index("cells")
    place = lax.axis_index("chrom")
    core = place % 2
    mine = {"y": place // 2, "x": cell % 2, "z": (cell // 2) % 2}
    sibling = (cell, place + 1 - 2 * core)
    near = {
        "y": (cell, place + 2 - 4 * mine["y"]),
        "x": (cell + 1 - 2 * mine["x"], place),
        "z": (cell + 2 - 4 * mine["z"], place),
    }

    barrier = pltpu.get_barrier_semaphore()
    for other in (sibling, near["x"], near["y"], near["z"]):
        pl.semaphore_signal(barrier, inc=1, device_id=other, device_id_type=MESH)
    loads = [
        pltpu.make_async_copy(second_in, second.at[:rows], load_sem.at[0]),
        pltpu.make_async_copy(low_in, low.at[:rows], load_sem.at[1]),
    ]
    for copy in loads:
        copy.start()
    base = core * units

    def weight_copy(kind, j, slot):
        if kind == "wide":
            src = up.at[:, pl.ds(pl.multiple_of(base + j * TILE, 128), TILE)]
            return pltpu.make_async_copy(src, wide_buf.at[slot], weight_sem.at[slot])
        if kind == "tall":
            src = down.at[pl.ds(pl.multiple_of(base + j * TILE, 128), TILE), :]
            return pltpu.make_async_copy(src, tall_buf.at[slot], weight_sem.at[2 + slot])
        if kind == "flat":
            src = up.at[j * SPAN : (j + 1) * SPAN, pl.ds(pl.multiple_of(base, 128), units)]
            return pltpu.make_async_copy(src, flat_buf, weight_sem.at[4])
        src = down.at[pl.ds(pl.multiple_of(base, 128), units), j * SPAN : (j + 1) * SPAN]
        return pltpu.make_async_copy(src, thin_buf, weight_sem.at[5])

    plan = (
        [("wide", j) for j in range(tiles)]
        + [("tall", j) for j in range(tiles)]
        + [(kind, j) for j in range(spans) for kind in ("flat", "thin")]
    )
    copies = {}

    def fetch(i):
        if i < len(plan):
            kind, j = plan[i]
            copies[i] = weight_copy(kind, j, j % 2)
            copies[i].start()

    fetch(0)
    pl.semaphore_wait(barrier, 4)

    def remote(src, dst, send, recv, device):
        copy = pltpu.make_async_remote_copy(
            src_ref=src, dst_ref=dst, send_sem=send, recv_sem=recv,
            device_id=device, device_id_type=MESH,
        )
        copy.start()
        return copy

    sent = []
    swaps = [
        remote(second_in, second.at[rows:], swap_send.at[0], swap_recv.at[0], sibling),
        remote(low_in, low.at[rows:], swap_send.at[1], swap_recv.at[1], sibling),
    ]
    sent += swaps

    flight = {}

    def down_view(order, stage_no, lo, hi, other, fix_z=None):
        index = {"z": slice(None), "x": slice(None), "y": slice(None)}
        for s, axis in enumerate(order[: stage_no + 1]):
            index[axis] = 1 - mine[axis] if (s == stage_no and other) else mine[axis]
        if fix_z is not None:
            index["z"] = fix_z
        return (index["z"], index["x"], index["y"], slice(None), slice(lo, hi))

    def up_view(order, stage_no, other):
        index = {"z": slice(None), "x": slice(None), "y": slice(None)}
        for s, axis in enumerate(order[: stage_no + 1]):
            index[axis] = 1 - mine[axis] if (s == stage_no and other) else mine[axis]
        return (slice(None), index["z"], index["x"], index["y"])

    down_recv = ((ra1, ra2), (rb1, rb2), (rc1, rc2))

    def go_down(item, stage_no, fix_z=None):
        lo, hi, order = DOWN_ITEMS[item]
        src = down_part.at[down_view(order, stage_no, lo, hi, True, fix_z)]
        dst = down_recv[item][stage_no]
        sem = item * 3 + stage_no
        if fix_z is not None:
            dst = dst.at[fix_z]
            sem = item * 3 + (2 if fix_z else 0)
        copy = remote(src, dst, sum_send.at[sem], sum_recv.at[sem], near[order[stage_no]])
        flight.setdefault(("d", item, stage_no), []).append(copy)
        sent.append(copy)

    def end_down(item, stage_no):
        lo, hi, order = DOWN_ITEMS[item]
        for copy in flight[("d", item, stage_no)]:
            copy.wait_recv()
        add_pieces(down_part, down_view(order, stage_no, lo, hi, False), down_recv[item][stage_no])
        if stage_no < 1:
            go_down(item, stage_no + 1)

    def go_up(j):
        order = UP_ORDERS[j]
        slot = UP_SLOT[j]
        copy = remote(
            up_part.at[slot].at[up_view(order, 0, True)], up_recv.at[slot],
            sum_send.at[9 + j], sum_recv.at[9 + j], near[order[0]],
        )
        flight[("u", j)] = copy
        sent.append(copy)

    def end_up(j, _):
        flight[("u", j)].wait_recv()
        slot = UP_SLOT[j]
        add_pieces(up_part, (slot,) + up_view(UP_ORDERS[j], 0, False), up_recv.at[slot])

    def down_rows(row):
        block = row // 320
        return (block // 4, (block // 2) % 2, block % 2, row % 320)

    def transpose_rows(at):
        second_t[:, at : at + CHUNK] = second[at : at + CHUNK, :].T

    def hidden(j, lo):
        here, cols = slice(lo, lo + rows), slice(j * TILE, (j + 1) * TILE)
        upper = jnp.dot(second[here, :], wide_buf[j % 2], preferred_element_type=F32)
        below = 0.5 * (1.0 + lax.erf(upper * ROOT_HALF))
        density = jnp.exp(-0.5 * upper * upper) * DENSITY_SCALE
        active[here, cols] = (upper * below).astype(BF)
        slope[here, cols] = (below + upper * density).astype(BF)

    def down_grad(lo):
        act = active[:, lo : lo + CHUNK].T
        grad = jnp.dot(act, low[...], preferred_element_type=F32).astype(BF)
        for s in range(0, CHUNK, 64):
            z, x, y, row = down_rows(lo + s)
            down_part[z, x, y, row : row + 64, :] = grad[s : s + 64, :]

    loads[0].wait()
    for j in range(tiles + 1):
        if j < tiles:
            fetch(j + 1)
            copies[j].wait()
        for part in range(2):
            if j < tiles:
                hidden(j, part * rows)
            if j:
                down_grad((j - 1) * TILE + part * CHUNK)
            if j == 0 and part == 0:
                loads[1].wait()
                for copy in swaps:
                    copy.wait_recv()
        if j < tiles:
            transpose_rows(j * CHUNK)
        else:
            transpose_rows(two - CHUNK)
        if j == 3:
            go_down(0, 0, 0)
            go_down(1, 0, 0)
    go_down(0, 0, 1)
    go_down(1, 0, 1)
    go_down(2, 0)
    for copy in swaps:
        copy.wait_send()
        sent[:] = [other for other in sent if other is not copy]
    pl.semaphore_signal(ready_second, inc=1, device_id=sibling, device_id_type=MESH)

    for j in range(tiles):
        fetch(tiles + j + 1)
        copies[tiles + j].wait()
        cols = slice(j * TILE, (j + 1) * TILE)

        def hidden_back(i, carry, j=j, cols=cols):
            here = pl.ds(pl.multiple_of(i * CHUNK, CHUNK), CHUNK)
            grad = lax.dot_general(low[here, :], tall_buf[j % 2], NT, preferred_element_type=F32)
            slope[here, cols] = (grad * slope[here, cols].astype(F32)).astype(BF)
            return carry

        lax.fori_loop(0, two // CHUNK, hidden_back, 0)
        for m in range(4):
            grad = jnp.dot(
                second_t[m * 320 : (m + 1) * 320, :], slope[:, cols], preferred_element_type=F32
            ).astype(BF)
            for s in range(4):
                k = 4 * m + s
                up_part[UP_SLOT[j], k // 8, (k // 4) % 2, (k // 2) % 2, k % 2] = grad[s * 80 : (s + 1) * 80]
        go_up(j)
    end_down(0, 0)
    pl.semaphore_signal(ready_low, inc=1, device_id=sibling, device_id_type=MESH)

    events = {
        0: [(end_down, 1, 0)],
        2: [(end_down, 2, 0)],
        8: [(end_up, 0, 0)],
        9: [
            (end_up, 2, 0), (end_down, 1, 1), (end_down, 2, 1), (end_up, 1, 0), (end_up, 3, 0),
            (end_up, 4, 0), (end_down, 0, 1),
        ],
    }
    pending = []
    writes = {}

    def finish(step, buf, out, n, copy):
        copy.wait_recv()
        cols = slice(n * SPAN, (n + 1) * SPAN)
        stage[step % 2] = stage[step % 2] + buf[rows:, cols].astype(F32)
        writes[step] = pltpu.make_async_copy(stage.at[step % 2], out.at[:, cols], out_sem.at[step % 2])
        writes[step].start()

    for step in range(2 * spans):
        n = step // 2
        backward = step % 2 == 0
        buf, out = (second, back_out) if backward else (low, result_out)
        fetch(2 * tiles + step + 1)
        copies[2 * tiles + step].wait()
        cols = slice(n * SPAN, (n + 1) * SPAN)

        def product(lo, n=n, backward=backward):
            if backward:
                return lax.dot_general(
                    slope[lo : lo + rows, :], flat_buf[...], NT, preferred_element_type=F32
                )
            return jnp.dot(active[lo : lo + rows, :], thin_buf[...], preferred_element_type=F32)

        buf[:rows, cols] = product(rows).astype(BF)
        own = product(0)
        if n == 0:
            pl.semaphore_wait(ready_second if backward else ready_low, 1)
        copy = remote(
            buf.at[:rows, cols], buf.at[rows:, cols],
            swap_send.at[2 + step], swap_recv.at[2 + step], sibling,
        )
        sent.append(copy)
        if step >= 2:
            writes[step - 2].wait()
        stage[step % 2] = own
        if pending:
            finish(*pending.pop())
        pending.append((step, buf, out, n, copy))
        for event, item, stage_no in events.get(step, ()):
            event(item, stage_no)
    finish(*pending.pop())
    views = (
        (down_part.at[:, mine["x"], mine["y"], :, :DOWN_CUT], down_ab),
        (down_part.at[mine["z"], mine["x"], :, :, DOWN_CUT:], down_c),
        (up_part.at[:3, :, mine["z"]], up_z),
        (up_part.at[3:, :, :, :, mine["y"]], up_y),
    )
    ends = [
        pltpu.make_async_copy(src, dst, end_sem.at[i]) for i, (src, dst) in enumerate(views)
    ]
    for copy in ends:
        copy.start()
    writes[2 * spans - 2].wait()
    writes[2 * spans - 1].wait()
    for copy in ends:
        copy.wait()
    for copy in sent:
        copy.wait_send()


def feed_forward_sum(second, low, up, down):
    rows, width = second.shape
    units = up.shape[1] // 2
    tiles = units // TILE
    two = 2 * rows
    anywhere = pl.BlockSpec(memory_space=pl.ANY)
    recv = []
    for lo, hi, _ in DOWN_ITEMS:
        recv += [
            pltpu.VMEM((2, 2, 320, hi - lo), BF),
            pltpu.VMEM((2, 320, hi - lo), BF),
        ]
    recv += [pltpu.VMEM((tiles, 2, 2, 2, 80, TILE), BF)]
    dma = pltpu.SemaphoreType.DMA
    return pl.pallas_call(
        feed_sum_kernel,
        in_specs=[anywhere] * 4,
        out_specs=[anywhere] * 6,
        out_shape=[
            jax.ShapeDtypeStruct((rows, width), F32),
            jax.ShapeDtypeStruct((rows, width), F32),
            jax.ShapeDtypeStruct((2, 320, DOWN_CUT), BF),
            jax.ShapeDtypeStruct((2, 320, width - DOWN_CUT), BF),
            jax.ShapeDtypeStruct((3, 2, 2, 2, 80, TILE), BF),
            jax.ShapeDtypeStruct((tiles - 3, 2, 2, 2, 80, TILE), BF),
        ],
        scratch_shapes=[
            pltpu.VMEM((two, width), BF),
            pltpu.VMEM((two, width), BF),
            pltpu.VMEM((width, two), BF),
            pltpu.VMEM((two, units), BF),
            pltpu.VMEM((two, units), BF),
            pltpu.VMEM((2, 2, 2, 320, width), BF),
            pltpu.VMEM((tiles, 2, 2, 2, 2, 80, TILE), BF),
            pltpu.VMEM((2, width, TILE), BF),
            pltpu.VMEM((2, TILE, width), BF),
            pltpu.VMEM((SPAN, units), BF),
            pltpu.VMEM((units, SPAN), BF),
            pltpu.VMEM((2, rows, SPAN), F32),
        ]
        + recv
        + [
            dma((2,)), dma((6,)), dma((2,)), dma((4,)), dma((12,)), dma((12,)), dma((14,)), dma((14,)),
            pltpu.SemaphoreType.REGULAR, pltpu.SemaphoreType.REGULAR,
        ],
        compiler_params=pltpu.CompilerParams(
            vmem_limit_bytes=VMEM_TOP, collective_id=0, has_side_effects=True
        ),
        cost_estimate=cost(2 * 6 * two * width * units, 6e7),
        name="feed_sum",
    )(second, low, up, down)


def one_hot_rows(lens, c, block, part, rows, along):
    per = rows // block
    at = 0
    ranks = []
    for b in range((part + 1) * per):
        if b >= part * per:
            slot = lax.broadcasted_iota(jnp.int32, (1, block) if along else (block, 1), along)
            ranks.append(jnp.where(slot < lens[c, b], slot + at, -1))
        at = at + lens[c, b]
    rank = jnp.concatenate(ranks, axis=along)
    line = lax.broadcasted_iota(jnp.int32, (FILLED, rows) if along else (rows, FILLED), 1 - along)
    return jnp.where(line == rank, 1.0, 0.0).astype(BF)


def normed_rows(values, gain, shift):
    center = values - jnp.mean(values, axis=1, keepdims=True)
    inverse = lax.rsqrt(jnp.mean(center * center, axis=1, keepdims=True) + EPS)
    return center * inverse * gain + shift


def attend_gather_kernel(
    block, heads,
    lens, tokens_in, weight, output_in, norms,
    first_out, kept_out, mixed_out, middle_out, second_out,
    tok, first, weights, outputs, qkv, packed, mixed, mixed_got, middle, second,
    load_sem, send_sem, recv_sem, turn_send, turn_recv, out_sem,
):
    cells, rows, width = tok.shape
    wide = heads * HEAD_DIM
    cell = lax.axis_index("cells")
    place = lax.axis_index("chrom")
    core = place % 2

    def chrom_near(r):
        return (cell, (place // 2 + r // 2) % 2 * 2 + (core + r % 2) % 2)

    barrier = pltpu.get_barrier_semaphore()
    for r in range(1, 4):
        pl.semaphore_signal(barrier, inc=1, device_id=chrom_near(r), device_id_type=MESH)

    def load(src, dst, sem):
        copy = pltpu.make_async_copy(src, dst, sem)
        copy.start()
        return copy

    loads = [
        load(tokens_in.at[0], tok.at[0], load_sem.at[0]),
        load(tokens_in.at[1], tok.at[1], load_sem.at[1]),
        load(tokens_in.at[2], tok.at[2], load_sem.at[2]),
        load(weight, weights, load_sem.at[3]),
        load(output_in, outputs, load_sem.at[4]),
    ]
    sent, writes = [], []

    def remote(src, dst, send, recv, r):
        copy = pltpu.make_async_remote_copy(
            src_ref=src, dst_ref=dst, send_sem=send, recv_sem=recv,
            device_id=chrom_near(r), device_id_type=MESH,
        )
        copy.start()
        sent.append(copy)
        return copy

    def part_rows(r):
        return slice(r * rows, (r + 1) * rows)

    near, over, across = {}, {}, {}

    def send_over(c):
        over[c] = remote(
            first.at[c, part_rows(0)], first.at[c, part_rows(2)], send_sem.at[3 * c], recv_sem.at[3 * c], 2
        )

    for c in range(cells):
        loads[c].wait()

        def some(i, carry, c=c):
            here = pl.ds(pl.multiple_of(i * 64, 64), 64)
            first[c, here, :] = normed_rows(tok[c, here, :].astype(F32), norms[0:1, :], norms[1:2, :]).astype(BF)
            return carry

        lax.fori_loop(0, rows // 64, some, 0)
        if c == 0:
            pl.semaphore_wait(barrier, 3)
            send_over(0)
        near[c] = remote(
            first.at[c, part_rows(0)], first.at[c, part_rows(1)],
            send_sem.at[3 * c + 1], recv_sem.at[3 * c + 1], 1,
        )
    loads[3].wait()

    def project(c, r):
        qkv[c, part_rows(r), :] = jnp.dot(
            first[c, part_rows(r), :], weights[...], preferred_element_type=F32
        ).astype(BF)

    for c in range(cells):
        project(c, 0)
    for c in range(cells):
        near[c].wait_recv()
        project(c, 1)
    loads[4].wait()

    turns = {}

    def finish(c):
        for copy in turns[c]:
            copy.wait_recv()
        writes.append(load(mixed_got.at[c], mixed_out.at[c], out_sem.at[5 * c]))
        total = tok[c].astype(F32)
        for r in range(4):
            total = total + jnp.dot(
                mixed_got[c, r], outputs[r * wide : (r + 1) * wide, :], preferred_element_type=F32
            )
        middle[c] = total

        def some(i, carry):
            here = pl.ds(pl.multiple_of(i * 64, 64), 64)
            second[c, here, :] = normed_rows(middle[c, here, :], norms[2:3, :], norms[3:4, :]).astype(BF)
            return carry

        lax.fori_loop(0, rows // 64, some, 0)
        writes.append(load(middle.at[c], middle_out.at[c], out_sem.at[5 * c + 1]))
        writes.append(load(second.at[c], second_out.at[c], out_sem.at[5 * c + 2]))

    scale = LOG2E / math.sqrt(HEAD_DIM)
    ones = jnp.ones((FILLED, HEAD_DIM), BF)
    for c in range(cells):
        over[c].wait_recv()
        across[c] = remote(
            first.at[c, part_rows(2)], first.at[c, part_rows(3)],
            send_sem.at[3 * c + 2], recv_sem.at[3 * c + 2], 1,
        )
        if c + 1 < cells:
            send_over(c + 1)
        project(c, 2)
        across[c].wait_recv()
        project(c, 3)
        writes.append(load(first.at[c], first_out.at[c], out_sem.at[5 * c + 3]))
        total = None
        for r in range(4):
            part = jnp.dot(
                one_hot_rows(lens, c, block, r, rows, 1), qkv[c, part_rows(r), :], preferred_element_type=F32
            )
            total = part if total is None else total + part
        packed[c] = total.astype(BF)
        writes.append(load(packed.at[c], kept_out.at[c], out_sem.at[5 * c + 4]))
        turns[c] = []
        for r in (2, 3, 1, 0):
            for h in range(heads):
                lo = h * HEAD_DIM
                q = qkv[c, part_rows(r), lo : lo + HEAD_DIM]
                k = packed[c, :, wide + lo : wide + lo + HEAD_DIM]
                v = packed[c, :, 2 * wide + lo : 2 * wide + lo + HEAD_DIM]
                s = lax.dot_general(q, k, NT, preferred_element_type=F32)
                top = jnp.max(s, axis=1, keepdims=True) * scale
                e = jnp.exp2(s * scale - top).astype(BF)
                o = jnp.dot(e, jnp.concatenate([v, ones], axis=1), preferred_element_type=F32)
                o = (o[:, :HEAD_DIM] / o[:, HEAD_DIM:]).astype(BF)
                if r:
                    mixed[c, r, :, lo : lo + HEAD_DIM] = o
                else:
                    mixed_got[c, 0, :, lo : lo + HEAD_DIM] = o
            if r:
                n = 3 * c + r - 1
                turns[c].append(
                    remote(mixed.at[c, r], mixed_got.at[c, r], turn_send.at[n], turn_recv.at[n], r)
                )
        if c:
            finish(c - 1)
    finish(cells - 1)
    for copy in writes:
        copy.wait()
    for copy in sent:
        copy.wait_send()


def attend_gather(lens, tokens, weight, output, norms, block):
    cells, rows, width = tokens.shape
    wide = weight.shape[1] // 3
    heads = wide // HEAD_DIM
    anywhere = pl.BlockSpec(memory_space=pl.ANY)
    local = pl.BlockSpec(memory_space=pltpu.VMEM)
    dma = pltpu.SemaphoreType.DMA
    shapes = [
        jax.ShapeDtypeStruct((cells, 4 * rows, width), BF),
        jax.ShapeDtypeStruct((cells, FILLED, 3 * wide), BF),
        jax.ShapeDtypeStruct((cells, 4, rows, wide), BF),
        jax.ShapeDtypeStruct((cells, rows, width), F32),
        jax.ShapeDtypeStruct((cells, rows, width), BF),
    ]
    return pl.pallas_call(
        functools.partial(attend_gather_kernel, block, heads),
        in_specs=[smem()] + [anywhere] * 3 + [local],
        out_specs=[anywhere] * 5,
        out_shape=shapes,
        scratch_shapes=[
            pltpu.VMEM((cells, rows, width), BF),
            pltpu.VMEM((cells, 4 * rows, width), BF),
            pltpu.VMEM((width, 3 * wide), BF),
            pltpu.VMEM((width, width), BF),
            pltpu.VMEM((cells, 4 * rows, 3 * wide), BF),
            pltpu.VMEM((cells, FILLED, 3 * wide), BF),
            pltpu.VMEM((cells, 4, rows, wide), BF),
            pltpu.VMEM((cells, 4, rows, wide), BF),
            pltpu.VMEM((cells, rows, width), F32),
            pltpu.VMEM((cells, rows, width), BF),
            dma((5,)), dma((9,)), dma((9,)), dma((9,)), dma((9,)), dma((5 * cells,)),
        ],
        compiler_params=pltpu.CompilerParams(
            vmem_limit_bytes=VMEM_MAX, collective_id=2, has_side_effects=True
        ),
        cost_estimate=cost(6e10, 6e7),
        name="attend_gather",
    )(lens, tokens, weight, output, norms)


def middle_kernel(
    middle, back, part, cotangent, scale, mixed, output, gain,
    layer_out, low_out, g0, g1, g2, g3, output_part, sums, total,
):
    step = pl.program_id(0)
    rows = middle.shape[1]
    wide = mixed.shape[3]
    half = middle.shape[2] // 2
    place = lax.axis_index("chrom")

    @pl.when(step == 0)
    def _():
        sums[...] = jnp.zeros_like(sums)
        total[...] = jnp.zeros_like(total)

    def some(i, carry):
        here = pl.ds(pl.multiple_of(i * 64, 64), 64)
        values = middle[0, here, :]
        layer_out[0, here, :] = (values + part[0, here, :]).astype(BF)
        center = values - jnp.mean(values, axis=1, keepdims=True)
        inverse = lax.rsqrt(jnp.mean(center * center, axis=1, keepdims=True) + EPS)
        normed = center * inverse
        grad = back[0, here, :]
        sums[2:3, :] += jnp.sum(grad * normed, axis=0, keepdims=True)
        sums[3:4, :] += jnp.sum(grad, axis=0, keepdims=True)
        scaled = grad * gain[...]
        through = inverse * (
            scaled
            - jnp.mean(scaled, axis=1, keepdims=True)
            - normed * jnp.mean(scaled * normed, axis=1, keepdims=True)
        )
        low_out[0, here, :] = (cotangent[0, here, :].astype(F32) * scale[0, here, :] + through).astype(BF)
        return carry

    lax.fori_loop(0, rows // 64, some, 0)
    head = jnp.where(place == 0, middle[0, :1, :] + part[0, :1, :], 0.0)
    sums[0:1, :] += head
    sums[1:2, :] += head * head
    for r, out in enumerate((g0, g1, g2, g3)):
        out[0] = lax.dot_general(
            low_out[0], output[r * wide : (r + 1) * wide, :], NT, preferred_element_type=F32
        ).astype(BF)
        total[r] += lax.dot_general(mixed[0, r], low_out[0], TN, preferred_element_type=F32)

    @pl.when(step == pl.num_programs(0) - 1)
    def _():
        for j in range(4):
            r = (place // 2 + j // 2) % 2 * 2 + (place % 2 + j % 2) % 2
            values = total[r].astype(BF)
            for s in range(4):
                k = 4 * j + s
                at = (k // 8, (k // 4) % 2, (k // 2) % 2, k % 2)
                for c in range(2):
                    output_part[(c,) + at] = values[s * 80 : (s + 1) * 80, c * half : (c + 1) * half]


def middle_step(middle, back, part, cotangent, scale, mixed, output, gain):
    cells, rows, width = middle.shape
    wide = mixed.shape[3]
    one = lambda *shape: pl.BlockSpec((1,) + shape, lambda c: (c,) + (0,) * len(shape))
    parted = (2, 2, 2, 2, 2, 80, width // 2)
    return pl.pallas_call(
        middle_kernel,
        grid=(cells,),
        in_specs=[
            one(rows, width), one(rows, width), one(rows, width), one(rows, width), one(rows, 1),
            one(4, rows, wide), whole(output.shape), whole(gain.shape),
        ],
        out_specs=[one(rows, width), one(rows, width)] + [one(rows, wide)] * 4 + [whole(parted), whole((8, width))],
        out_shape=[jax.ShapeDtypeStruct(middle.shape, BF)] * 2
        + [jax.ShapeDtypeStruct((cells, rows, wide), BF)] * 4
        + [jax.ShapeDtypeStruct(parted, BF), jax.ShapeDtypeStruct((8, width), F32)],
        scratch_shapes=[pltpu.VMEM((4, wide, width), F32)],
        compiler_params=pltpu.CompilerParams(vmem_limit_bytes=VMEM_MAX),
        cost_estimate=cost(8 * cells * rows * width * wide * 2, 3e7),
        name="middle_step",
    )(middle, back, part, cotangent, scale, mixed, output, gain)


QUERY_ITEMS = ((0, 512, "xzh"), (512, 960, "zxh"))


def row_dot(left, right, exact_left):
    wide = right if exact_left else left
    high = wide.astype(BF)
    low = (wide - high.astype(F32)).astype(BF)
    pairs = ((left, high), (left, low)) if exact_left else ((high, right), (low, right))
    return sum(lax.dot_general(a, b, NT, preferred_element_type=F32) for a, b in pairs)


def attend_sum_kernel(
    block, heads,
    lens, g0, g1, g2, g3, kept, first_in, *refs
):
    (
        weight, up_z_in, up_y_in, out_in, down_ab_in, down_c_in, early_in, tokens_in, through_in, gain,
        tokens_out, query_out, up_z_out, up_y_out, out_out, down_out, early_out, late_out,
        grads, qkv_c, first, weights, back, moved, total, query_part,
        up_z, up_y, out_part, down_ab, down_c, down_part, got_ab, got_c,
        keep_back, got_near, got_far, got_over,
        qa1, qa2, qa3, qb1, qb2, qb3, query_last, query_got,
        uz1, uz2, uz3, up_z_last, up_z_got, uy1, uy2, uy3, up_y_last, up_y_got,
        oc1, oc2, oc3, oc4, oc5, out_last, out_got, down_got, down_last, early, early_got, late, late_got, column_sum, norm_in,
        load_sem, first_sem, turn_send, turn_recv, back_send, back_recv, sum_send, sum_recv, end_sem, norm_sem,
    ) = refs
    sources = (g0, g1, g2, g3)
    cells = kept.shape[0]
    rows = g0.shape[1]
    wide = heads * HEAD_DIM
    cell = lax.axis_index("cells")
    place = lax.axis_index("chrom")
    core = place % 2
    mine = {"c": core, "y": place // 2, "x": cell % 2, "z": (cell // 2) % 2, "h": cell // 4}

    def chrom_near(r):
        return (place // 2 + r // 2) % 2 * 2 + (core + r % 2) % 2

    near = {
        "c": (cell, chrom_near(1)),
        "y": (cell, chrom_near(2)),
        "x": (cell + 1 - 2 * mine["x"], place),
        "z": (cell + 2 - 4 * mine["z"], place),
        "h": (cell + 4 - 8 * mine["h"], place),
    }
    far = (cell, chrom_near(3))
    by_part = (None, near["c"], near["y"], far)

    barrier = pltpu.get_barrier_semaphore()
    for other in (*near.values(), far):
        pl.semaphore_signal(barrier, inc=1, device_id=other, device_id_type=MESH)

    def load(src, dst, sem):
        copy = pltpu.make_async_copy(src, dst, sem)
        copy.start()
        return copy

    def load_own(c):
        return [
            load(g0.at[c], grads.at[c, 0], load_sem.at[2 * c]),
            load(kept.at[c], qkv_c.at[c % 2], load_sem.at[2 * c + 1]),
        ]

    own_loads = {c: load_own(c) for c in range(2)}
    extra = [
        load(down_ab_in, down_ab, load_sem.at[6]),
        load(down_c_in, down_c, load_sem.at[11]),
        load(up_z_in, up_z, load_sem.at[7]),
        load(up_y_in, up_y, load_sem.at[8]),
        load(out_in, out_part, load_sem.at[9]),
        load(weight, weights, load_sem.at[10]),
    ]

    def load_first(c):
        return [load(first_in.at[c], first.at[c % 2], first_sem.at[c])]

    first_loads = {c: load_first(c) for c in range(2)}
    early_load = load(early_in, early.at[0], load_sem.at[12])
    pl.semaphore_wait(barrier, 6)

    def remote(src, dst, send, recv, device, start=True):
        copy = pltpu.make_async_remote_copy(
            src_ref=src, dst_ref=dst, send_sem=send, recv_sem=recv,
            device_id=device, device_id_type=MESH,
        )
        if start:
            copy.start()
        return copy

    sent = []

    def turn(c):
        line = []
        for r in (2, 3, 1):
            n = 3 * c + r - 1
            line.append(
                remote(sources[r].at[c], grads.at[c, r], turn_send.at[n], turn_recv.at[n], by_part[r])
            )
        sent.extend(line)
        return line

    turns = {0: turn(0)}

    sems = iter(range(64))
    items = {}

    def item(name, part, dims, stages, recvs, cols=slice(None)):
        items[name] = (part, dims, stages, recvs, cols, [next(sems) for _ in stages], {})

    item("uz", up_z, "*hxy", "xyh", (uz1, uz2, uz3))
    item("uy", up_y, "*hzx", "zxh", (uy1, uy2, uy3))
    item("o", out_part, "chzxy", "cyxzh", (oc1, oc2, oc3, oc4, oc5))
    item("da", down_ab, "z", "z", (got_ab,))
    item("dc", down_c, "y", "y", (got_c,))
    for n, (lo, hi, stages) in enumerate(QUERY_ITEMS):
        item("q%d" % n, query_part, "hzx", stages, ((qa1, qa2, qa3), (qb1, qb2, qb3))[n], slice(lo, hi))

    def view(name, s, other):
        _, dims, stages, _, cols, _, _ = items[name]
        index = [slice(None)] * len(dims)
        for t, axis in enumerate(stages[: s + 1]):
            index[dims.index(axis)] = 1 - mine[axis] if (t == s and other) else mine[axis]
        return tuple(index) + (slice(None), cols)

    def go(name, s):
        part, _, stages, recvs, _, ids, flight = items[name]
        copy = remote(
            part.at[view(name, s, True)], recvs[s],
            sum_send.at[ids[s]], sum_recv.at[ids[s]], near[stages[s]],
        )
        flight[s] = copy
        sent.append(copy)

    def end(name, s):
        part, _, stages, recvs, _, _, flight = items[name]
        flight[s].wait_recv()
        add_pieces(part, view(name, s, False), recvs[s])
        if s + 1 < len(stages):
            go(name, s + 1)

    lasts = {
        "uz": (up_z, up_z_last, up_z_got, next(sems)),
        "uy": (up_y, up_y_last, up_y_got, next(sems)),
        "o": (out_part, out_last, out_got, next(sems)),
    }

    def swap_last(name, _):
        part, last, got, sem = lasts[name]
        at = view(name, len(items[name][2]) - 1, False)
        half = part.shape[-2] // 2
        tiles = part.shape[0] if name != "o" else 1
        for t in range(tiles):
            here = (t,) + at[1:] if name != "o" else at
            values = part[here]
            for k in range(2):
                last[k, t] = values[k * half : (k + 1) * half]
        copy = remote(last.at[1 - core], got, sum_send.at[sem], sum_recv.at[sem], near["c"])
        sent.append(copy)
        items[name][6]["last"] = copy

    down_sems = (next(sems), next(sems))

    def down_far():
        return remote(
            down_part, down_got, sum_send.at[down_sems[0]], sum_recv.at[down_sems[0]], near["h"], False
        )

    def down_near():
        return remote(
            down_part.at[1 - core], down_last, sum_send.at[down_sems[1]], sum_recv.at[down_sems[1]],
            near["c"], False,
        )

    def down_start(*_):
        for k in range(2):
            half = slice(k * 160, (k + 1) * 160)
            down_part[k, :, :DOWN_CUT] = down_ab[mine["z"], half, :]
            down_part[k, :, DOWN_CUT:] = down_c[mine["y"], half, :]

        @pl.when(core != mine["h"])
        def _():
            down_far().start()

    def down_add(*_):
        @pl.when(core == mine["h"])
        def _():
            down_far().wait_recv()
            for k in range(2):
                down_part[k] = (down_part[k].astype(F32) + down_got[k].astype(F32)).astype(BF)
            down_near().start()
            down_last[...] = down_part[core]

    def down_end(*_):
        @pl.when(core != mine["h"])
        def _():
            down_far().wait_send()
            down_near().wait_recv()

        @pl.when(core == mine["h"])
        def _():
            down_near().wait_send()

    vectors = {"early": (early, early_got, 26), "late": (late, late_got, 31)}

    def vector_go(name, s):
        stack, got, sem = vectors[name]
        copy = remote(
            stack.at[s], got.at[s], sum_send.at[sem + s], sum_recv.at[sem + s], near["cyxzh"[s]]
        )
        flights[name, s] = copy
        sent.append(copy)

    def vector_end(name, s):
        stack, got, _ = vectors[name]
        flights[name, s].wait_recv()
        stack[s + 1] = stack[s] + got[s]
        if s < 4:
            vector_go(name, s + 1)

    flights = {}

    for copy in extra:
        copy.wait()
    go("uz", 0)
    go("uy", 0)
    go("o", 0)
    early_load.wait()
    vector_go("early", 0)

    near_copies, over_copies, norm_loads = {}, {}, {}

    def back_sum(c, _):
        near_copies[c][1].wait_recv()
        mid = slice(512, 768)
        first[c % 2, mid] = (first[c % 2, mid].astype(F32) + got_far[c].astype(F32)).astype(BF)
        over_copies[c] = remote(
            first.at[c % 2, mid], got_over.at[c], back_send.at[3 * c + 2], back_recv.at[3 * c + 2], near["y"]
        )
        sent.append(over_copies[c])
        norm_loads[c] = [
            load(tokens_in.at[c], norm_in, norm_sem.at[2 * c]),
            load(through_in.at[c], got_far.at[c], norm_sem.at[2 * c + 1]),
        ]

    def back_end(c, _):
        near_copies[c][0].wait_recv()
        over_copies[c].wait_recv()
        for copy in norm_loads[c]:
            copy.wait()

        def some(i, carry):
            here = pl.ds(pl.multiple_of(i * 64, 64), 64)
            values = norm_in[here, :].astype(F32)
            center = values - jnp.mean(values, axis=1, keepdims=True)
            inverse = lax.rsqrt(jnp.mean(center * center, axis=1, keepdims=True) + EPS)
            normed = center * inverse
            scaled = keep_back[c, here, :] + got_near[c, here, :].astype(F32)
            scaled = (scaled + got_over[c, here, :].astype(F32)) * gain[0:1, :]
            keep_back[c, here, :] = got_far[c, here, :].astype(F32) + inverse * (
                scaled
                - jnp.mean(scaled, axis=1, keepdims=True)
                - normed * jnp.mean(scaled * normed, axis=1, keepdims=True)
            )
            return carry

        lax.fori_loop(0, rows // 64, some, 0)
        ends.append(load(keep_back.at[c], tokens_out.at[c], end_sem.at[c]))
        if c + 2 < cells:
            for copy in (*near_copies[c], over_copies[c]):
                copy.wait_send()
                sent[:] = [other for other in sent if other is not copy]
            first_loads[c + 2] = load_first(c + 2)

    ends = []
    events = {
        (0, 0): [(end, "o", 0), (vector_end, "early", 0)],
        (0, 2): [(end, "uy", 0)],
        (0, 3): [(end, "uz", 0), (end, "dc", 0), (vector_end, "early", 1)],
        (0, 5): [(end, "da", 0), (down_start, 0, 0), (end, "uy", 1), (vector_end, "early", 2)],
        (1, 0): [(vector_end, "early", 3)],
        (1, 1): [(back_sum, 0, 0)],
        (1, 3): [(vector_end, "early", 4)],
        (1, 4): [(end, "uy", 2), (swap_last, "uy", 0), (end, "uz", 1)],
        (1, 5): [(end, "o", 1)],
        (2, 0): [(down_add, 0, 0), (back_end, 0, 0), (back_sum, 1, 0)],
        (2, 1): [(end, "uz", 2), (swap_last, "uz", 0), (end, "o", 2), (down_end, 0, 0)],
        (2, 4): [(end, "o", 3)],
        (2, 5): [(back_end, 1, 0)],
        (2, 6): [(vector_end, "late", 0), (end, "o", 4), (swap_last, "o", 0)],
    }

    def run(key):
        for event, a, b in events.get(key, ()):
            event(a, b)

    scale = LOG2E / math.sqrt(HEAD_DIM)
    inv_root = 1.0 / math.sqrt(HEAD_DIM)
    chunk = 256
    for c in range(cells):
        own_loads[c][0].wait()
        own_loads[c][1].wait()
        for copy in turns[c]:
            copy.wait_recv()
        if c == 0:
            go("da", 0)
            go("dc", 0)
        if c + 1 < cells:
            turns[c + 1] = turn(c + 1)
        packed = jnp.zeros((wide, FILLED), F32)
        for r in range(4):
            move = one_hot_rows(lens, c, block, r, rows, 1)
            grad = grads[c, r].astype(F32).T.astype(BF)
            packed = packed + lax.dot_general(grad, move, NT, preferred_element_type=F32)
        query_t = qkv_c[c % 2, :, :wide].astype(F32).T.astype(BF)
        key_t = qkv_c[c % 2, :, wide : 2 * wide].astype(F32).T.astype(BF)
        for h in range(heads):
            lo = h * HEAD_DIM
            k = qkv_c[c % 2, :, wide + lo : wide + lo + HEAD_DIM]
            v = qkv_c[c % 2, :, 2 * wide + lo : 2 * wide + lo + HEAD_DIM]
            kt = key_t[lo : lo + HEAD_DIM, :]
            dv = jnp.zeros((FILLED, HEAD_DIM), F32)
            dk = jnp.zeros((FILLED, HEAD_DIM), F32)
            for w in range(0, FILLED, chunk):
                qt = query_t[lo : lo + HEAD_DIM, w : w + chunk]
                s = jnp.dot(k, qt, preferred_element_type=F32)
                top = jnp.max(s, axis=0, keepdims=True) * scale
                e = jnp.exp2(s * scale - top)
                inv = 1.0 / jnp.sum(e, axis=0, keepdims=True)
                gt = (packed[lo : lo + HEAD_DIM, w : w + chunk] * inv).astype(BF)
                dp = jnp.dot(v, gt, preferred_element_type=F32)
                inner = jnp.sum(e * dp, axis=0, keepdims=True) * inv
                ds = (e * (dp - inner)).astype(BF)
                dv = dv + lax.dot_general(e.astype(BF), gt, NT, preferred_element_type=F32)
                dk = dk + lax.dot_general(ds, qt, NT, preferred_element_type=F32)
                dqt = jnp.dot(kt, ds, preferred_element_type=F32)
                back[w : w + chunk, lo : lo + HEAD_DIM] = (dqt.T * inv_root).astype(BF)
            back[:, wide + lo : wide + lo + HEAD_DIM] = (dk * inv_root).astype(BF)
            back[:, 2 * wide + lo : 2 * wide + lo + HEAD_DIM] = dv.astype(BF)
            run((c, h))
        if c + 2 < cells:
            own_loads[c + 2] = load_own(c + 2)
        for r in range(4):
            move = one_hot_rows(lens, c, block, r, rows, 0)
            moved[r * rows : (r + 1) * rows, :] = jnp.dot(
                move, back[...], preferred_element_type=F32
            ).astype(BF)
        for copy in first_loads[c]:
            copy.wait()
        ones = jnp.ones((8, 4 * rows), BF)
        part = jnp.dot(ones, moved[...], preferred_element_type=F32)
        column_sum[...] = part + column_sum[...] if c else part
        for m in range(first.shape[2] // CHUNK):
            cols = slice(m * CHUNK, (m + 1) * CHUNK)
            part = jnp.dot(first[c % 2, :, cols].T, moved[...], preferred_element_type=F32)
            if c:
                part = part + total[cols, :]
            if c < cells - 1:
                total[cols, :] = part
            else:
                product = part * weights[cols, :].astype(F32)
                late[0, :, cols] = row_dot(ones[:, : 3 * wide], product, True)
                low = part.astype(BF)
                for s in range(0, CHUNK, 32):
                    row = m * CHUNK + s
                    n = row // 160
                    query_part[n // 4, (n // 2) % 2, n % 2, row % 160 : row % 160 + 32, :] = low[s : s + 32, :]
        if c == cells - 1:
            go("q0", 0)
            go("q1", 0)
            line = lax.broadcasted_iota(jnp.int32, late.shape[1:], 0)
            late[0] = jnp.where(line == 0, late[0], row_dot(column_sum[...], weights[...], False))
            vector_go("late", 0)
        run((c, 5))
        lines = []
        for r in (3, 1, 2, 0):
            part = lax.dot_general(
                moved[r * rows : (r + 1) * rows, :], weights[...], NT, preferred_element_type=F32
            )
            if r == 0:
                keep_back[c] = part
                continue
            spot = {1: slice(0, 256), 2: slice(512, 768), 3: slice(256, 512)}[r]
            first[c % 2, spot] = part.astype(BF)
            if r != 2:
                n = 3 * c + (1 if r == 3 else 0)
                copy = remote(
                    first.at[c % 2, spot], (got_far if r == 3 else got_near).at[c],
                    back_send.at[n], back_recv.at[n], near["c"],
                )
                lines.insert(0, copy)
                sent.append(copy)
        near_copies[c] = lines
        run((c, 6))
    vector_end("late", 1)
    back_sum(cells - 1, 0)
    vector_end("late", 2)
    end("q1", 0)
    vector_end("late", 3)
    end("q0", 0)
    vector_end("late", 4)
    end("q1", 1)
    back_end(cells - 1, 0)
    end("q0", 1)
    end("q1", 2)
    end("q0", 2)
    values = query_part[mine["h"], mine["z"], mine["x"]]
    for j in range(4):
        query_last[j] = values[j * 40 : (j + 1) * 40]
    last_query = []
    for r in range(1, 4):
        sem = next(sems)
        copy = remote(
            query_last.at[chrom_near(r)], query_got.at[r], sum_send.at[sem], sum_recv.at[sem], by_part[r]
        )
        last_query.append(copy)
        sent.append(copy)
    query_got[0] = query_last[place]
    n = cells
    for name, out in (("uz", up_z_out), ("uy", up_y_out), ("o", out_out)):
        _, last, got, _ = lasts[name]
        items[name][6]["last"].wait_recv()
        ends.append(load(last.at[core], out.at[0], end_sem.at[n]))
        ends.append(load(got, out.at[1], end_sem.at[n + 1]))
        n += 2
    ends.append(load(down_last, down_out, end_sem.at[n]))
    ends.append(load(early.at[5], early_out, end_sem.at[n + 2]))
    ends.append(load(late.at[5], late_out, end_sem.at[n + 3]))
    for copy in last_query:
        copy.wait_recv()
    ends.append(load(query_got, query_out, end_sem.at[n + 1]))
    for copy in ends:
        copy.wait()
    for copy in sent:
        copy.wait_send()


def attend_sum(
    lens, grads, kept, first, weight, up_z, up_y, out_part, down_ab, down_c, early, tokens, through, gain, block
):
    cells, rows, wide = grads[0].shape
    width = first.shape[2]
    heads = wide // HEAD_DIM
    seq = 4 * rows
    anywhere = pl.BlockSpec(memory_space=pl.ANY)
    dma = pltpu.SemaphoreType.DMA
    vmem = lambda *shape: pltpu.VMEM(shape, BF)
    qa, qb = [hi - lo for lo, hi, _ in QUERY_ITEMS]
    return pl.pallas_call(
        functools.partial(attend_sum_kernel, block, heads),
        in_specs=[smem()] + [anywhere] * 15 + [pl.BlockSpec(memory_space=pltpu.VMEM)],
        out_specs=[anywhere] * 8,
        out_shape=[
            jax.ShapeDtypeStruct((cells, rows, width), F32),
            jax.ShapeDtypeStruct((4, 40, 3 * wide), BF),
            jax.ShapeDtypeStruct((2, 3, 40, TILE), BF),
            jax.ShapeDtypeStruct((2, 2, 40, TILE), BF),
            jax.ShapeDtypeStruct((2, 1, 40, width // 2), BF),
            jax.ShapeDtypeStruct((160, width), BF),
            jax.ShapeDtypeStruct((8, width), F32),
            jax.ShapeDtypeStruct((8, width), F32),
        ],
        scratch_shapes=[
            vmem(cells, 4, rows, wide),
            vmem(2, FILLED, 3 * wide),
            vmem(2, seq, width),
            vmem(width, 3 * wide),
            vmem(FILLED, 3 * wide),
            vmem(seq, 3 * wide),
            pltpu.VMEM((width, 3 * wide), F32),
            vmem(2, 2, 2, 160, 3 * wide),
            vmem(*up_z.shape), vmem(*up_y.shape), vmem(*out_part.shape), vmem(*down_ab.shape), vmem(*down_c.shape),
            vmem(2, 160, width), vmem(*down_ab.shape[1:]), vmem(*down_c.shape[1:]),
            pltpu.VMEM((cells, rows, width), F32),
            vmem(cells, rows, width), vmem(cells, rows, width), vmem(cells, rows, width),
            vmem(2, 2, 160, qa), vmem(2, 160, qa), vmem(160, qa),
            vmem(2, 2, 160, qb), vmem(2, 160, qb), vmem(160, qb),
            vmem(4, 40, 3 * wide), vmem(4, 40, 3 * wide),
            vmem(3, 2, 2, 80, TILE), vmem(3, 2, 80, TILE), vmem(3, 80, TILE),
            vmem(2, 3, 40, TILE), vmem(3, 40, TILE),
            vmem(2, 2, 2, 80, TILE), vmem(2, 2, 80, TILE), vmem(2, 80, TILE),
            vmem(2, 2, 40, TILE), vmem(2, 40, TILE),
            vmem(2, 2, 2, 2, 80, width // 2), vmem(2, 2, 2, 80, width // 2), vmem(2, 2, 80, width // 2),
            vmem(2, 80, width // 2), vmem(80, width // 2),
            vmem(2, 1, 40, width // 2), vmem(1, 40, width // 2),
            vmem(2, 160, width), vmem(160, width),
            pltpu.VMEM((6, 8, width), F32), pltpu.VMEM((5, 8, width), F32),
            pltpu.VMEM((6, 8, width), F32), pltpu.VMEM((5, 8, width), F32),
            pltpu.VMEM((8, 3 * wide), F32), vmem(rows, width),
            dma((13,)), dma((3,)), dma((9,)), dma((9,)), dma((9,)), dma((9,)), dma((36,)), dma((36,)),
            dma((16,)), dma((2 * cells,)),
        ],
        compiler_params=pltpu.CompilerParams(
            vmem_limit_bytes=VMEM_TOP, collective_id=1, has_side_effects=True
        ),
        cost_estimate=cost(8e10, 6e7),
        name="attend_sum",
    )(
        lens, *grads, kept, first, weight, up_z, up_y, out_part, down_ab, down_c, early, tokens, through, gain
    )


def swap(x, axis, mask):
    size = lax.axis_size(axis)
    return lax.ppermute(x, axis, [(i, i ^ mask) for i in range(size)])


def halve(x, dim, axis, bit):
    mine = (lax.axis_index(axis) >> bit) & 1
    send = lax.dynamic_index_in_dim(x, 1 - mine, dim, keepdims=False)
    keep = lax.dynamic_index_in_dim(x, mine, dim, keepdims=False)
    got = swap(send, axis, 1 << bit)
    return keep.astype(F32) + got.astype(F32)


def log2(n):
    return n.bit_length() - 1


def scatter_rows(x, order, names):
    names = list(names)
    for i, name in enumerate(order):
        x = halve(x.astype(BF), names.index(name), name[0], name[1])
        names.remove(name)
    return x


def sum_all(x):
    for bit in range(log2(lax.axis_size("chrom"))):
        x = x + swap(x, "chrom", 1 << bit)
    for bit in range(log2(lax.axis_size("cells"))):
        x = x + swap(x, "cells", 1 << bit)
    return x


def scatter_columns_split(x, order):
    cell_bits = log2(lax.axis_size("cells"))
    width = x.shape[1]
    names = [("cells", b) for b in reversed(range(cell_bits))] + [("chrom", 1)]
    x = x.reshape((2,) * (cell_bits + 1) + (-1, width))
    return place_columns(scatter_rows(x, order, names))


def place_columns(x):
    core = lax.axis_index("chrom") & 1
    x = x.reshape(2, -1, x.shape[-1])
    keep = lax.dynamic_index_in_dim(x, core, 0, keepdims=False)
    got = swap(lax.dynamic_index_in_dim(x, 1 - core, 0, keepdims=False).astype(BF), "chrom", 1).astype(F32)
    left = jnp.where(core == 0, keep, got)
    right = jnp.where(core == 0, got, keep)
    return jnp.concatenate([left, right], axis=1)


def scatter_rows_split(x, order):
    cell_bits = log2(lax.axis_size("cells"))
    width = x.shape[1]
    names = [("cells", b) for b in reversed(range(cell_bits - 1))] + [("chrom", 1)]
    x = x.reshape((2,) * cell_bits + (-1, width))
    return place_rows(scatter_rows(x, order, names))


def place_rows(x):
    cells = lax.axis_size("cells")
    chrom = lax.axis_size("chrom")
    core = lax.axis_index("chrom") & 1
    top = cells // 2
    high = lax.axis_index("cells") // top
    width = x.shape[1]
    pairs = []
    for cell in range(cells):
        for place in range(chrom):
            if (cell // top) != (place & 1):
                pairs.append((cell * chrom + place, (cell ^ top) * chrom + place))
    got = lax.ppermute(x.astype(BF), ("cells", "chrom"), pairs)
    x = (x.astype(F32) + got.astype(F32)).reshape(2, -1, width)
    keep = lax.dynamic_index_in_dim(x, core, 0, keepdims=False)
    send = lax.dynamic_index_in_dim(x, 1 - core, 0, keepdims=False).astype(BF)
    back = []
    for cell in range(cells):
        for place in range(chrom):
            if (cell // top) == (place & 1):
                back.append((cell * chrom + place, cell * chrom + (place ^ 1)))
    got = lax.ppermute(send, ("cells", "chrom"), back)
    return jnp.where(core == high, keep, got.astype(F32))


def feed_forward_plain(second_low, down_low, up_weight, down_weight):
    cell_bits = log2(lax.axis_size("cells"))
    core = lax.axis_index("chrom") & 1
    result_part, result_send, back_part, back_send, down_grad, up_grad = feed_forward(
        core[None].astype(jnp.int32),
        second_low,
        swap(second_low, "chrom", 1),
        down_low,
        swap(down_low, "chrom", 1),
        up_weight,
        down_weight,
    )
    second_back = back_part + swap(back_send, "chrom", 1).astype(F32)
    result_part = result_part + swap(result_send, "chrom", 1).astype(F32)
    low_bits = [("cells", b) for b in range(cell_bits - 1)]
    down_out = scatter_rows_split(down_grad, low_bits + [("chrom", 1)])
    up_out = scatter_columns_split(
        up_grad, [("chrom", 1)] + low_bits[::-1] + [("cells", cell_bits - 1)]
    )
    return second_back, result_part, down_out, up_out


def norm_rows(values, gain, shift):
    center = values - jnp.mean(values, axis=-1, keepdims=True)
    inverse = lax.rsqrt(jnp.mean(center * center, axis=-1, keepdims=True) + EPS)
    normed = center * inverse
    return (normed * gain + shift, normed, inverse)


def norm_back(grad_out, normed, inverse, gain):
    scaled = grad_out * gain
    grad_in = inverse * (
        scaled
        - jnp.mean(scaled, axis=-1, keepdims=True)
        - normed * jnp.mean(scaled * normed, axis=-1, keepdims=True)
    )
    return (grad_in, jnp.sum(grad_out * normed, axis=0), jnp.sum(grad_out, axis=0))


def contract(left, right):
    return lax.dot_general(left, right, TN, preferred_element_type=F32)


def back_through(grad, weight):
    return lax.dot_general(grad, weight, NT, preferred_element_type=F32)


def per_device(
    tokens,
    cotangent,
    block_lengths,
    group_ids,
    group_weights,
    first_gain,
    first_shift,
    query_weight,
    key_weight,
    value_weight,
    output_weight,
    second_gain,
    second_shift,
    up_weight,
    down_weight,
):
    cells_here, seq_here, width = tokens.shape
    rows = cells_here * seq_here
    parts = lax.axis_size("chrom")
    cell_bits = log2(lax.axis_size("cells"))
    seq_full = seq_here * parts
    nblocks = block_lengths.shape[1]
    block = seq_full // nblocks
    per = nblocks // parts
    wide = width // parts
    place = lax.axis_index("chrom")
    core = place & 1
    near = [place ^ r for r in range(parts)]

    valid = (jnp.arange(block)[None, None, :] < block_lengths[:, :, None]).reshape(
        cells_here, seq_full
    )
    local_valid = lax.dynamic_slice_in_dim(valid, place * seq_here, seq_here, 1)
    lens = jnp.concatenate(
        [lax.dynamic_slice_in_dim(block_lengths, n * per, per, 1) for n in near], axis=1
    )
    n_groups = group_weights.shape[0]
    cell_scale = jnp.sum(
        jnp.where(group_ids[:, None] == jnp.arange(n_groups)[None, :], group_weights[None, :], 0.0),
        axis=1,
    )

    def my_heads(weight):
        return lax.dynamic_slice_in_dim(weight, place * wide, wide, 1)

    qkv_weight = jnp.concatenate(
        [my_heads(query_weight), my_heads(key_weight), my_heads(value_weight)], axis=1
    )
    output_near = jnp.concatenate(
        [lax.dynamic_slice_in_dim(output_weight, n * wide, wide, 0) for n in near], axis=0
    )

    fused = lax.axis_size("cells") == 8 and parts == 4
    if fused:
        norms = jnp.stack([first_gain, first_shift, second_gain, second_shift])
        first_all, kept, mixed_near, middle, second_low = attend_gather(
            lens,
            tokens,
            qkv_weight,
            output_near,
            norms,
            block,
        )
        second_low = second_low.reshape(rows, width)
    else:
        flat = tokens.reshape(rows, width).astype(F32)
        first_out, first_norm, first_inv = norm_rows(flat, first_gain, first_shift)
        first_low = first_out.astype(BF).reshape(cells_here, seq_here, width)
        first_all, mixed_near, kept = [], [], []
        for c in range(cells_here):
            mine = first_low[c]
            over = swap(mine, "chrom", 2)
            first_all.append([mine, swap(mine, "chrom", 1), over, swap(over, "chrom", 1)])
        for c in range(cells_here):
            mixed, qkv_c = attend(first_all[c], lens[c], qkv_weight, block)
            kept.append(qkv_c)
            mixed_near.append(
                jnp.concatenate([mixed[0]] + [swap(mixed[r], "chrom", r) for r in range(1, parts)], axis=1)
            )
        mixed_flat = jnp.concatenate(mixed_near, axis=0)

        middle = flat + jnp.dot(mixed_flat, output_near, preferred_element_type=F32)
        second_out, second_norm, second_inv = norm_rows(middle, second_gain, second_shift)
        second_low = second_out.astype(BF)
    result_back = (
        cotangent.astype(F32)
        * cell_scale[:, None, None]
        * local_valid.astype(F32)[:, :, None]
    ).reshape(rows, width)
    down_low = result_back.astype(BF)
    low_bits = [("cells", b) for b in range(cell_bits - 1)]
    if fused:
        second_back, result_part, down_ab, down_c, up_z, up_y = feed_forward_sum(
            second_low, down_low, up_weight, down_weight
        )
    else:
        second_back, result_part, down_out, up_out = feed_forward_plain(
            second_low, down_low, up_weight, down_weight
        )
    if fused:
        cells_shape = (cells_here, seq_here, width)
        layer_out, attend_low, *rest = middle_step(
            middle,
            second_back.reshape(cells_shape),
            result_part.reshape(cells_shape),
            cotangent,
            cell_scale[:, None, None] * local_valid.astype(F32)[:, :, None],
            mixed_near,
            output_near,
            second_gain.reshape(1, width),
        )
        grads_near, output_part, early = rest[:4], rest[4], rest[5]
    else:
        result = middle + result_part
        result_cells = result.reshape(cells_here, seq_here, width)
        layer_out = result_cells.astype(BF)

        cls_rows = jnp.where(place == 0, result_cells[:, 0, :], 0.0)
        cls_total = jnp.sum(cls_rows, axis=0)
        cls_square = jnp.sum(cls_rows * cls_rows, axis=0)

        middle_ln, second_gain_grad, second_shift_grad = norm_back(
            second_back, second_norm, second_inv, second_gain
        )
        middle_back = result_back + middle_ln
        attend_low = middle_back.astype(BF)
        output_grad = contract(mixed_flat, attend_low).reshape(parts, wide, width)
        output_grad = jnp.concatenate(
            [lax.dynamic_index_in_dim(output_grad, place ^ j, 0, keepdims=False) for j in range(parts)],
            axis=0,
        )
        early = jnp.stack([cls_total, cls_square, second_gain_grad, second_shift_grad])


    if fused:
        tokens_grad, qkv_got, up_z, up_y, out_two, down_grad, early, late = attend_sum(
            lens,
            grads_near,
            kept,
            first_all,
            qkv_weight,
            up_z,
            up_y,
            output_part,
            down_ab,
            down_c,
            early,
            tokens,
            attend_low,
            norms,
            block,
        )
        late = jnp.stack([(late[0] - first_shift * late[1]) / first_gain, late[1]])
        down_out = down_grad.astype(F32)

        def both_cores(two):
            two = two.transpose(0, 2, 1, 3).reshape(2, two.shape[2], -1)
            swapped = jnp.where(core == 0, two, two[::-1])
            return jnp.concatenate([swapped[0], swapped[1]], axis=1).astype(F32)

        up_two = jnp.stack([up_z[:, 0], up_z[:, 1], up_y[:, 0], up_z[:, 2], up_y[:, 1]], axis=1)
        up_out = both_cores(up_two)
        output_out = both_cores(out_two)
        pieces = [
            lax.dynamic_index_in_dim(qkv_got, place ^ j, 0, keepdims=False).astype(F32)
            for j in range(parts)
        ]
    else:
        half_width = width // 2
        output_half = lax.dynamic_slice_in_dim(output_grad, core * half_width, half_width, 1) + swap(
            lax.dynamic_slice_in_dim(output_grad, (1 - core) * half_width, half_width, 1).astype(BF),
            "chrom",
            1,
        ).astype(F32)
        output_out = scatter_columns_split(
            output_half.astype(BF), low_bits + [("cells", cell_bits - 1), ("chrom", 1)]
        )
        mixed_back = back_through(attend_low, output_near).astype(BF)
        mixed_back = mixed_back.reshape(cells_here, seq_here, width)
        heads_back = []
        for c in range(cells_here):
            pieces = [mixed_back[c, :, r * wide : (r + 1) * wide] for r in range(parts)]
            heads_back.append(
                [pieces[0]] + [swap(pieces[r], "chrom", r) for r in range(1, parts)]
            )
        qkv_grad = None
        first_back = []
        for c in range(cells_here):
            qkv_back = attend_back(heads_back[c], lens[c], kept[c], block)
            pieces = [back_through(g, qkv_weight) for g in qkv_back]
            sent = swap(jnp.stack([pieces[1].astype(BF), pieces[3].astype(BF)]), "chrom", 1).astype(F32)
            over = swap((pieces[2] + sent[1]).astype(BF), "chrom", 2)
            first_back.append(pieces[0] + sent[0] + over.astype(F32))
            part = contract(
                jnp.concatenate(first_all[c], axis=0), jnp.concatenate(qkv_back, axis=0)
            )
            qkv_grad = part if qkv_grad is None else qkv_grad + part
        first_back = jnp.concatenate(first_back, axis=0)

        names = [("cells", b) for b in reversed(range(cell_bits))]
        qkv_sum = scatter_rows(
            qkv_grad.reshape((2,) * cell_bits + (-1, 3 * wide)),
            [("cells", b) for b in range(cell_bits)],
            names,
        ).reshape(parts, -1, 3 * wide)
        pieces = [lax.dynamic_index_in_dim(qkv_sum, near[0], 0, keepdims=False)]
        for r in range(1, parts):
            piece = lax.dynamic_index_in_dim(qkv_sum, near[r], 0, keepdims=False).astype(BF)
            pieces.append(swap(piece, "chrom", r).astype(F32))
        pieces = jnp.stack(pieces)
        pieces = [lax.dynamic_index_in_dim(pieces, place ^ j, 0, keepdims=False) for j in range(parts)]
        first_ln, first_gain_grad, first_shift_grad = norm_back(
            first_back, first_norm, first_inv, first_gain
        )
        tokens_grad = (middle_back + first_ln).reshape(cells_here, seq_here, width)
        early = sum_all(early)
        late = sum_all(jnp.stack([first_gain_grad, first_shift_grad]))
    query_out, key_out, value_out = [
        jnp.concatenate([p[:, i * wide : (i + 1) * wide] for p in pieces], axis=1) for i in range(3)
    ]

    count_cells = cells_here * lax.axis_size("cells")
    cls_mean = early[0] / count_cells
    cls_var = early[1] / count_cells - cls_mean * cls_mean
    share = width // (parts * lax.axis_size("cells"))
    start = (lax.axis_index("cells") * parts + place) * share

    def mine(vector):
        return lax.dynamic_slice_in_dim(vector, start, share, 0)

    return (
        layer_out,
        tokens_grad,
        mine(late[0]),
        mine(late[1]),
        query_out,
        key_out,
        value_out,
        output_out,
        mine(early[2]),
        mine(early[3]),
        up_out,
        down_out,
        cls_mean,
        cls_var,
    )


def solution(mesh):
    rows = P("cells", "chrom", None)
    both = ("cells", "chrom")
    in_specs = (rows, rows, P("cells", None), P("cells")) + (P(),) * 11
    out_specs = (
        (rows, rows)
        + (P(both), P(both))
        + (P(both, None),) * 4
        + (P(both), P(both))
        + (P(both, None), P(both, None))
        + (P(), P())
    )
    return jax.shard_map(
        per_device, mesh=mesh, in_specs=in_specs, out_specs=out_specs, check_vma=False
    )
```

```python
import functools
import itertools
import math

import jax
import jax.numpy as jnp
from jax import lax
from jax.experimental import pallas as pl
from jax.experimental.pallas import tpu as pltpu
from jax.sharding import PartitionSpec as P

HEAD_DIM = 64
FILLED = 768
EPS = 1e-05
ROOT_HALF = 0.7071067811865476
DENSITY_SCALE = 0.3989422804014327
LOG2E = 1.4426950408889634
BF = jnp.bfloat16
F32 = jnp.float32
NT = (((1,), (1,)), ((), ()))
TN = (((0,), (0,)), ((), ()))
VMEM_MAX = 60 * 2**20
VMEM_TOP = 63 * 2**20


def whole(shape):
    return pl.BlockSpec(shape, lambda *_: (0,) * len(shape), pipeline_mode=pl.Buffered(1))


def smem():
    return pl.BlockSpec(memory_space=pltpu.SMEM)


def cost(flops, moved, exps=0):
    return pl.CostEstimate(flops=int(flops), bytes_accessed=int(moved), transcendentals=int(exps))


def shift_rows(shape, dim, shift, length):
    slot = lax.broadcasted_iota(jnp.int32, shape, dim)
    row = lax.broadcasted_iota(jnp.int32, shape, 1 - dim)
    return jnp.where((row == slot + shift) & (slot < length), 1.0, 0.0).astype(BF)


def pack(packed, values, lens, part, block, at):
    per = values.shape[0] // block
    for b in range(per):
        here = lens[part * per + b]
        rows = values[b * block : (b + 1) * block, :]
        shift = at % 8
        base = pl.multiple_of(at - shift, 8) if part + b else 0
        move = shift_rows((block + 8, block), 1, shift, here)
        moved = jnp.dot(move, rows, preferred_element_type=F32)
        if part + b:
            packed[pl.ds(base, 8), :] += moved[:8, :]
            packed[pl.ds(pl.multiple_of(base + 8, 8), block), :] = moved[8:, :]
        else:
            packed[: block + 8, :] = moved
        at = at + here
    return at


def unpack(packed, out, lens, part, block, at):
    per = out.shape[0] // block
    for b in range(per):
        here = lens[part * per + b]
        shift = at % 8
        base = pl.multiple_of(at - shift, 8) if part + b else 0
        rows = packed[pl.ds(base, block + 8), :].astype(BF)
        move = shift_rows((block, block + 8), 0, shift, here)
        out[b * block : (b + 1) * block, :] = jnp.dot(
            move, rows, preferred_element_type=F32
        ).astype(BF)
        at = at + here
    return at


def attend_kernel(block, heads, lens, *refs):
    parts = 4
    firsts, weight = refs[:parts], refs[parts]
    mixed = refs[parts + 1 : 2 * parts + 1]
    qkv_c = refs[2 * parts + 1]
    query, packed = refs[2 * parts + 2 :]
    rows = firsts[0].shape[0]
    wide = heads * HEAD_DIM
    at = 0
    for r in range(parts):
        qkv = jnp.dot(firsts[r][...], weight[...], preferred_element_type=F32)
        query[r * rows : (r + 1) * rows, :] = qkv[:, :wide].astype(BF)
        at = pack(packed, qkv.astype(BF), lens, r, block, at)
    qkv_c[...] = packed[:FILLED, :].astype(BF)
    scale = LOG2E / math.sqrt(HEAD_DIM)
    ones = jnp.ones((FILLED, HEAD_DIM), BF)
    for r in range(parts):
        for h in range(heads):
            lo = h * HEAD_DIM
            q = query[r * rows : (r + 1) * rows, lo : lo + HEAD_DIM]
            k = qkv_c[:, wide + lo : wide + lo + HEAD_DIM]
            v = qkv_c[:, 2 * wide + lo : 2 * wide + lo + HEAD_DIM]
            s = lax.dot_general(q, k, NT, preferred_element_type=F32)
            top = jnp.max(s, axis=1, keepdims=True) * scale
            e = jnp.exp2(s * scale - top).astype(BF)
            o = jnp.dot(e, jnp.concatenate([v, ones], axis=1), preferred_element_type=F32)
            o = o[:, :HEAD_DIM] / o[:, HEAD_DIM:]
            mixed[r][:, lo : lo + HEAD_DIM] = o.astype(BF)


def attend(firsts, lens, weight, block):
    rows, width = firsts[0].shape
    wide3 = weight.shape[1]
    wide = wide3 // 3
    heads = wide // HEAD_DIM
    out = pl.pallas_call(
        functools.partial(attend_kernel, block, heads),
        in_specs=[smem()] + [whole((rows, width))] * 4 + [whole(weight.shape)],
        out_specs=[whole((rows, wide))] * 4 + [whole((FILLED, wide3))],
        out_shape=[jax.ShapeDtypeStruct((rows, wide), BF)] * 4
        + [jax.ShapeDtypeStruct((FILLED, wide3), BF)],
        scratch_shapes=[pltpu.VMEM((4 * rows, wide), BF), pltpu.VMEM((FILLED + block, wide3), F32)],
        compiler_params=pltpu.CompilerParams(vmem_limit_bytes=VMEM_MAX),
        cost_estimate=cost(2 * 4 * rows * width * wide3 + 4 * 4 * rows * FILLED * 256 * heads, 8e6),
        grid=(1,),
        name="attend",
    )(lens, *firsts, weight)
    return out[:4], out[4]


def attend_back_kernel(block, heads, lens, *refs):
    parts = 4
    grads, qkv_c = refs[:parts], refs[parts]
    outs = refs[parts + 1 : 2 * parts + 1]
    packed, back = refs[2 * parts + 1 :]
    wide = heads * HEAD_DIM
    at = 0
    for r in range(parts):
        at = pack(packed, grads[r][...], lens, r, block, at)
    scale = LOG2E / math.sqrt(HEAD_DIM)
    inv_root = 1.0 / math.sqrt(HEAD_DIM)
    chunk = 256
    back[FILLED:, :] = jnp.zeros((block, 3 * wide), F32)
    grad_t = packed[:FILLED, :].T
    query_t = qkv_c[:, :wide].astype(F32).T.astype(BF)
    key_t = qkv_c[:, wide : 2 * wide].astype(F32).T.astype(BF)
    for h in range(heads):
        lo = h * HEAD_DIM
        k = qkv_c[:, wide + lo : wide + lo + HEAD_DIM]
        v = qkv_c[:, 2 * wide + lo : 2 * wide + lo + HEAD_DIM]
        kt = key_t[lo : lo + HEAD_DIM, :]
        dv = jnp.zeros((FILLED, HEAD_DIM), F32)
        dk = jnp.zeros((FILLED, HEAD_DIM), F32)
        for c in range(0, FILLED, chunk):
            qt = query_t[lo : lo + HEAD_DIM, c : c + chunk]
            s = jnp.dot(k, qt, preferred_element_type=F32)
            top = jnp.max(s, axis=0, keepdims=True) * scale
            e = jnp.exp2(s * scale - top)
            inv = 1.0 / jnp.sum(e, axis=0, keepdims=True)
            gt = (grad_t[lo : lo + HEAD_DIM, c : c + chunk] * inv).astype(BF)
            dp = jnp.dot(v, gt, preferred_element_type=F32)
            inner = jnp.sum(e * dp, axis=0, keepdims=True) * inv
            ds = (e * (dp - inner)).astype(BF)
            dv = dv + lax.dot_general(e.astype(BF), gt, NT, preferred_element_type=F32)
            dk = dk + lax.dot_general(ds, qt, NT, preferred_element_type=F32)
            dqt = jnp.dot(kt, ds, preferred_element_type=F32)
            back[c : c + chunk, lo : lo + HEAD_DIM] = dqt.T * inv_root
        back[:FILLED, wide + lo : wide + lo + HEAD_DIM] = dk * inv_root
        back[:FILLED, 2 * wide + lo : 2 * wide + lo + HEAD_DIM] = dv
    at = 0
    for r in range(parts):
        at = unpack(back, outs[r], lens, r, block, at)


def attend_back(grads, lens, qkv_c, block):
    rows, wide = grads[0].shape
    heads = wide // HEAD_DIM
    return pl.pallas_call(
        functools.partial(attend_back_kernel, block, heads),
        in_specs=[smem()] + [whole((rows, wide))] * 4 + [whole(qkv_c.shape)],
        out_specs=[whole((rows, 3 * wide))] * 4,
        out_shape=[jax.ShapeDtypeStruct((rows, 3 * wide), BF)] * 4,
        scratch_shapes=[
            pltpu.VMEM((FILLED + block, wide), F32),
            pltpu.VMEM((FILLED + block, 3 * wide), F32),
        ],
        compiler_params=pltpu.CompilerParams(vmem_limit_bytes=VMEM_MAX),
        cost_estimate=cost(2 * 5 * FILLED * FILLED * 256 * heads, 6e6),
        grid=(1,),
        name="attend_back",
    )(lens, *grads, qkv_c)


FF_TILE = 512
FF_ROWS = 256
FF_GRAD = 256


def feed_kernel(half, second_a, second_b, low_a, low_b, up, down, *refs):
    result, send_result, back, send_back, down_grad, up_grad = refs[:6]
    second_t, active, upper_back, acc_result, acc_back = refs[6:]
    rows, width = second_a.shape
    tile = up.shape[1]
    step = pl.program_id(0)

    @pl.when(step == 0)
    def _():
        result[...] = jnp.zeros_like(result)
        back[...] = jnp.zeros_like(back)
        acc_result[...] = jnp.zeros_like(acc_result)
        acc_back[...] = jnp.zeros_like(acc_back)
        for part, ref in enumerate((second_a, second_b)):
            for lo in range(0, rows, FF_ROWS):
                at = part * rows + lo
                second_t[:, at : at + FF_ROWS] = ref[lo : lo + FF_ROWS, :].astype(F32).T.astype(BF)

    for part, (second, low, to_result, to_back) in enumerate(
        ((second_a, low_a, result, back), (second_b, low_b, acc_result, acc_back))
    ):

        def chunk(i, carry):
            here = pl.ds(pl.multiple_of(i * FF_ROWS, FF_ROWS), FF_ROWS)
            there = pl.ds(pl.multiple_of(part * rows + i * FF_ROWS, FF_ROWS), FF_ROWS)
            upper = jnp.dot(second[here, :], up[...], preferred_element_type=F32)
            grad = lax.dot_general(low[here, :], down[...], NT, preferred_element_type=F32)
            below = 0.5 * (1.0 + lax.erf(upper * ROOT_HALF))
            density = jnp.exp(-0.5 * upper * upper) * DENSITY_SCALE
            act = (upper * below).astype(BF)
            ub = (grad * (below + upper * density)).astype(BF)
            active[there, :] = act
            upper_back[there, :] = ub
            to_result[here, :] += jnp.dot(act, down[...], preferred_element_type=F32)
            to_back[here, :] += lax.dot_general(ub, up[...], NT, preferred_element_type=F32)
            return carry

        lax.fori_loop(0, rows // FF_ROWS, chunk, 0)

    def one_down(i, carry):
        here = pl.ds(pl.multiple_of(i * FF_GRAD, FF_GRAD), FF_GRAD)
        act = active[:, here].astype(F32).T.astype(BF)
        down_grad[here, :] = (
            jnp.dot(act[:, :rows], low_a[...], preferred_element_type=F32)
            + jnp.dot(act[:, rows:], low_b[...], preferred_element_type=F32)
        ).astype(BF)
        return carry

    lax.fori_loop(0, tile // FF_GRAD, one_down, 0)

    def one_up(i, carry):
        here = pl.ds(pl.multiple_of(i * FF_GRAD, FF_GRAD), FF_GRAD)
        up_grad[here, :] = jnp.dot(
            second_t[here, :], upper_back[...], preferred_element_type=F32
        ).astype(BF)
        return carry

    lax.fori_loop(0, width // FF_GRAD, one_up, 0)

    @pl.when(step == pl.num_programs(0) - 1)
    def _():
        send_result[...] = acc_result[...].astype(BF)
        send_back[...] = acc_back[...].astype(BF)


def feed_forward(half, second_a, second_b, low_a, low_b, up, down):
    rows, width = second_a.shape
    units = up.shape[1] // 2
    tiles = units // FF_TILE
    two = 2 * rows
    return pl.pallas_call(
        feed_kernel,
        grid_spec=pltpu.PrefetchScalarGridSpec(
            num_scalar_prefetch=1,
            grid=(tiles,),
            in_specs=[whole((rows, width))] * 4
            + [
                pl.BlockSpec((width, FF_TILE), lambda j, half: (0, half[0] * tiles + j)),
                pl.BlockSpec((FF_TILE, width), lambda j, half: (half[0] * tiles + j, 0)),
            ],
            out_specs=[whole((rows, width))] * 4
            + [
                pl.BlockSpec((FF_TILE, width), lambda j, half: (j, 0)),
                pl.BlockSpec((width, FF_TILE), lambda j, half: (0, j)),
            ],
            scratch_shapes=[
                pltpu.VMEM((width, two), BF),
                pltpu.VMEM((two, FF_TILE), BF),
                pltpu.VMEM((two, FF_TILE), BF),
                pltpu.VMEM((rows, width), F32),
                pltpu.VMEM((rows, width), F32),
            ],
        ),
        out_shape=[
            jax.ShapeDtypeStruct((rows, width), F32),
            jax.ShapeDtypeStruct((rows, width), BF),
            jax.ShapeDtypeStruct((rows, width), F32),
            jax.ShapeDtypeStruct((rows, width), BF),
            jax.ShapeDtypeStruct((units, width), BF),
            jax.ShapeDtypeStruct((width, units), BF),
        ],
        compiler_params=pltpu.CompilerParams(vmem_limit_bytes=VMEM_MAX),
        cost_estimate=cost(2 * 6 * two * width * units, 6e7),
        name="feed_forward",
    )(half, second_a, second_b, low_a, low_b, up, down)


MESH = pl.DeviceIdType.MESH
TILE = 512
SPAN = 256
CHUNK = 256
DOWN_ITEMS = ((0, 512, "xyz"), (512, 1024, "yxz"), (1024, 1280, "zxy"))
DOWN_CUT = 1024
UP_ORDERS = ("zxy", "zxy", "yxz", "zxy", "yxz")
UP_SLOT = (0, 1, 3, 2, 4)


def add_pieces(total, view, got):
    lead = len(total.shape) - 2
    tail = tuple(view[lead:]) + (slice(None),) * (len(total.shape) - max(len(view), lead))
    free = [i for i in range(lead) if isinstance(view[i], slice)]
    for pick in itertools.product(*[range(total.shape[i]) for i in free]):
        index = list(view[:lead])
        for i, n in zip(free, pick):
            index[i] = n
        here = tuple(index) + tail
        add = got[pick] if pick else got[...]
        total[here] = (total[here].astype(F32) + add.astype(F32)).astype(BF)


def feed_sum_kernel(
    second_in, low_in, up, down,
    back_out, result_out, down_ab, down_c, up_z, up_y,
    second, low, second_t, active, slope, down_part, up_part,
    wide_buf, tall_buf, flat_buf, thin_buf, stage,
    ra1, ra2, rb1, rb2, rc1, rc2, up_recv,
    load_sem, weight_sem, out_sem, end_sem, swap_send, swap_recv, sum_send, sum_recv,
    ready_second, ready_low,
):
    rows = low_in.shape[0]
    width = low_in.shape[1]
    two = 2 * rows
    units = active.shape[1]
    tiles = units // TILE
    spans = width // SPAN
    cell = lax.axis_index("cells")
    place = lax.axis_index("chrom")
    core = place % 2
    mine = {"y": place // 2, "x": cell % 2, "z": (cell // 2) % 2}
    sibling = (cell, place + 1 - 2 * core)
    near = {
        "y": (cell, place + 2 - 4 * mine["y"]),
        "x": (cell + 1 - 2 * mine["x"], place),
        "z": (cell + 2 - 4 * mine["z"], place),
    }

    barrier = pltpu.get_barrier_semaphore()
    for other in (sibling, near["x"], near["y"], near["z"]):
        pl.semaphore_signal(barrier, inc=1, device_id=other, device_id_type=MESH)
    loads = [
        pltpu.make_async_copy(second_in, second.at[:rows], load_sem.at[0]),
        pltpu.make_async_copy(low_in, low.at[:rows], load_sem.at[1]),
    ]
    for copy in loads:
        copy.start()
    base = core * units

    def weight_copy(kind, j, slot):
        if kind == "wide":
            src = up.at[:, pl.ds(pl.multiple_of(base + j * TILE, 128), TILE)]
            return pltpu.make_async_copy(src, wide_buf.at[slot], weight_sem.at[slot])
        if kind == "tall":
            src = down.at[pl.ds(pl.multiple_of(base + j * TILE, 128), TILE), :]
            return pltpu.make_async_copy(src, tall_buf.at[slot], weight_sem.at[2 + slot])
        if kind == "flat":
            src = up.at[j * SPAN : (j + 1) * SPAN, pl.ds(pl.multiple_of(base, 128), units)]
            return pltpu.make_async_copy(src, flat_buf, weight_sem.at[4])
        src = down.at[pl.ds(pl.multiple_of(base, 128), units), j * SPAN : (j + 1) * SPAN]
        return pltpu.make_async_copy(src, thin_buf, weight_sem.at[5])

    plan = (
        [("wide", j) for j in range(tiles)]
        + [("tall", j) for j in range(tiles)]
        + [(kind, j) for j in range(spans) for kind in ("flat", "thin")]
    )
    copies = {}

    def fetch(i):
        if i < len(plan):
            kind, j = plan[i]
            copies[i] = weight_copy(kind, j, j % 2)
            copies[i].start()

    fetch(0)
    pl.semaphore_wait(barrier, 4)

    def remote(src, dst, send, recv, device):
        copy = pltpu.make_async_remote_copy(
            src_ref=src, dst_ref=dst, send_sem=send, recv_sem=recv,
            device_id=device, device_id_type=MESH,
        )
        copy.start()
        return copy

    sent = []
    swaps = [
        remote(second_in, second.at[rows:], swap_send.at[0], swap_recv.at[0], sibling),
        remote(low_in, low.at[rows:], swap_send.at[1], swap_recv.at[1], sibling),
    ]
    sent += swaps

    flight = {}

    def down_view(order, stage_no, lo, hi, other, fix_z=None):
        index = {"z": slice(None), "x": slice(None), "y": slice(None)}
        for s, axis in enumerate(order[: stage_no + 1]):
            index[axis] = 1 - mine[axis] if (s == stage_no and other) else mine[axis]
        if fix_z is not None:
            index["z"] = fix_z
        return (index["z"], index["x"], index["y"], slice(None), slice(lo, hi))

    def up_view(order, stage_no, other):
        index = {"z": slice(None), "x": slice(None), "y": slice(None)}
        for s, axis in enumerate(order[: stage_no + 1]):
            index[axis] = 1 - mine[axis] if (s == stage_no and other) else mine[axis]
        return (slice(None), index["z"], index["x"], index["y"])

    down_recv = ((ra1, ra2), (rb1, rb2), (rc1, rc2))

    def go_down(item, stage_no, fix_z=None):
        lo, hi, order = DOWN_ITEMS[item]
        src = down_part.at[down_view(order, stage_no, lo, hi, True, fix_z)]
        dst = down_recv[item][stage_no]
        sem = item * 3 + stage_no
        if fix_z is not None:
            dst = dst.at[fix_z]
            sem = item * 3 + (2 if fix_z else 0)
        copy = remote(src, dst, sum_send.at[sem], sum_recv.at[sem], near[order[stage_no]])
        flight.setdefault(("d", item, stage_no), []).append(copy)
        sent.append(copy)

    def end_down(item, stage_no):
        lo, hi, order = DOWN_ITEMS[item]
        for copy in flight[("d", item, stage_no)]:
            copy.wait_recv()
        add_pieces(down_part, down_view(order, stage_no, lo, hi, False), down_recv[item][stage_no])
        if stage_no < 1:
            go_down(item, stage_no + 1)

    def go_up(j):
        order = UP_ORDERS[j]
        slot = UP_SLOT[j]
        copy = remote(
            up_part.at[slot].at[up_view(order, 0, True)], up_recv.at[slot],
            sum_send.at[9 + j], sum_recv.at[9 + j], near[order[0]],
        )
        flight[("u", j)] = copy
        sent.append(copy)

    def end_up(j, _):
        flight[("u", j)].wait_recv()
        slot = UP_SLOT[j]
        add_pieces(up_part, (slot,) + up_view(UP_ORDERS[j], 0, False), up_recv.at[slot])

    def down_rows(row):
        block = row // 320
        return (block // 4, (block // 2) % 2, block % 2, row % 320)

    def transpose_rows(at):
        second_t[:, at : at + CHUNK] = second[at : at + CHUNK, :].T

    def hidden(j, lo):
        here, cols = slice(lo, lo + rows), slice(j * TILE, (j + 1) * TILE)
        upper = jnp.dot(second[here, :], wide_buf[j % 2], preferred_element_type=F32)
        below = 0.5 * (1.0 + lax.erf(upper * ROOT_HALF))
        density = jnp.exp(-0.5 * upper * upper) * DENSITY_SCALE
        active[here, cols] = (upper * below).astype(BF)
        slope[here, cols] = (below + upper * density).astype(BF)

    def down_grad(lo):
        act = active[:, lo : lo + CHUNK].T
        grad = jnp.dot(act, low[...], preferred_element_type=F32).astype(BF)
        for s in range(0, CHUNK, 64):
            z, x, y, row = down_rows(lo + s)
            down_part[z, x, y, row : row + 64, :] = grad[s : s + 64, :]

    loads[0].wait()
    for j in range(tiles + 1):
        if j < tiles:
            fetch(j + 1)
            copies[j].wait()
        for part in range(2):
            if j < tiles:
                hidden(j, part * rows)
            if j:
                down_grad((j - 1) * TILE + part * CHUNK)
            if j == 0 and part == 0:
                loads[1].wait()
                for copy in swaps:
                    copy.wait_recv()
        if j < tiles:
            transpose_rows(j * CHUNK)
        else:
            transpose_rows(two - CHUNK)
        if j == 3:
            go_down(0, 0, 0)
            go_down(1, 0, 0)
    go_down(0, 0, 1)
    go_down(1, 0, 1)
    go_down(2, 0)
    for copy in swaps:
        copy.wait_send()
        sent[:] = [other for other in sent if other is not copy]
    pl.semaphore_signal(ready_second, inc=1, device_id=sibling, device_id_type=MESH)

    for j in range(tiles):
        fetch(tiles + j + 1)
        copies[tiles + j].wait()
        cols = slice(j * TILE, (j + 1) * TILE)

        def hidden_back(i, carry, j=j, cols=cols):
            here = pl.ds(pl.multiple_of(i * CHUNK, CHUNK), CHUNK)
            grad = lax.dot_general(low[here, :], tall_buf[j % 2], NT, preferred_element_type=F32)
            slope[here, cols] = (grad * slope[here, cols].astype(F32)).astype(BF)
            return carry

        lax.fori_loop(0, two // CHUNK, hidden_back, 0)
        for m in range(4):
            grad = jnp.dot(
                second_t[m * 320 : (m + 1) * 320, :], slope[:, cols], preferred_element_type=F32
            ).astype(BF)
            for s in range(4):
                k = 4 * m + s
                up_part[UP_SLOT[j], k // 8, (k // 4) % 2, (k // 2) % 2, k % 2] = grad[s * 80 : (s + 1) * 80]
        go_up(j)
    end_down(0, 0)
    pl.semaphore_signal(ready_low, inc=1, device_id=sibling, device_id_type=MESH)

    events = {
        0: [(end_down, 1, 0)],
        2: [(end_down, 2, 0)],
        8: [(end_up, 0, 0)],
        9: [
            (end_up, 2, 0), (end_down, 1, 1), (end_down, 2, 1), (end_up, 1, 0), (end_up, 3, 0),
            (end_up, 4, 0), (end_down, 0, 1),
        ],
    }
    pending = []
    writes = {}

    def finish(step, buf, out, n, copy):
        copy.wait_recv()
        cols = slice(n * SPAN, (n + 1) * SPAN)
        stage[step % 2] = stage[step % 2] + buf[rows:, cols].astype(F32)
        writes[step] = pltpu.make_async_copy(stage.at[step % 2], out.at[:, cols], out_sem.at[step % 2])
        writes[step].start()

    for step in range(2 * spans):
        n = step // 2
        backward = step % 2 == 0
        buf, out = (second, back_out) if backward else (low, result_out)
        fetch(2 * tiles + step + 1)
        copies[2 * tiles + step].wait()
        cols = slice(n * SPAN, (n + 1) * SPAN)

        def product(lo, n=n, backward=backward):
            if backward:
                return lax.dot_general(
                    slope[lo : lo + rows, :], flat_buf[...], NT, preferred_element_type=F32
                )
            return jnp.dot(active[lo : lo + rows, :], thin_buf[...], preferred_element_type=F32)

        buf[:rows, cols] = product(rows).astype(BF)
        own = product(0)
        if n == 0:
            pl.semaphore_wait(ready_second if backward else ready_low, 1)
        copy = remote(
            buf.at[:rows, cols], buf.at[rows:, cols],
            swap_send.at[2 + step], swap_recv.at[2 + step], sibling,
        )
        sent.append(copy)
        if step >= 2:
            writes[step - 2].wait()
        stage[step % 2] = own
        if pending:
            finish(*pending.pop())
        pending.append((step, buf, out, n, copy))
        for event, item, stage_no in events.get(step, ()):
            event(item, stage_no)
    finish(*pending.pop())
    views = (
        (down_part.at[:, mine["x"], mine["y"], :, :DOWN_CUT], down_ab),
        (down_part.at[mine["z"], mine["x"], :, :, DOWN_CUT:], down_c),
        (up_part.at[:3, :, mine["z"]], up_z),
        (up_part.at[3:, :, :, :, mine["y"]], up_y),
    )
    ends = [
        pltpu.make_async_copy(src, dst, end_sem.at[i]) for i, (src, dst) in enumerate(views)
    ]
    for copy in ends:
        copy.start()
    writes[2 * spans - 2].wait()
    writes[2 * spans - 1].wait()
    for copy in ends:
        copy.wait()
    for copy in sent:
        copy.wait_send()


def feed_forward_sum(second, low, up, down):
    rows, width = second.shape
    units = up.shape[1] // 2
    tiles = units // TILE
    two = 2 * rows
    anywhere = pl.BlockSpec(memory_space=pl.ANY)
    recv = []
    for lo, hi, _ in DOWN_ITEMS:
        recv += [
            pltpu.VMEM((2, 2, 320, hi - lo), BF),
            pltpu.VMEM((2, 320, hi - lo), BF),
        ]
    recv += [pltpu.VMEM((tiles, 2, 2, 2, 80, TILE), BF)]
    dma = pltpu.SemaphoreType.DMA
    return pl.pallas_call(
        feed_sum_kernel,
        in_specs=[anywhere] * 4,
        out_specs=[anywhere] * 6,
        out_shape=[
            jax.ShapeDtypeStruct((rows, width), F32),
            jax.ShapeDtypeStruct((rows, width), F32),
            jax.ShapeDtypeStruct((2, 320, DOWN_CUT), BF),
            jax.ShapeDtypeStruct((2, 320, width - DOWN_CUT), BF),
            jax.ShapeDtypeStruct((3, 2, 2, 2, 80, TILE), BF),
            jax.ShapeDtypeStruct((tiles - 3, 2, 2, 2, 80, TILE), BF),
        ],
        scratch_shapes=[
            pltpu.VMEM((two, width), BF),
            pltpu.VMEM((two, width), BF),
            pltpu.VMEM((width, two), BF),
            pltpu.VMEM((two, units), BF),
            pltpu.VMEM((two, units), BF),
            pltpu.VMEM((2, 2, 2, 320, width), BF),
            pltpu.VMEM((tiles, 2, 2, 2, 2, 80, TILE), BF),
            pltpu.VMEM((2, width, TILE), BF),
            pltpu.VMEM((2, TILE, width), BF),
            pltpu.VMEM((SPAN, units), BF),
            pltpu.VMEM((units, SPAN), BF),
            pltpu.VMEM((2, rows, SPAN), F32),
        ]
        + recv
        + [
            dma((2,)), dma((6,)), dma((2,)), dma((4,)), dma((12,)), dma((12,)), dma((14,)), dma((14,)),
            pltpu.SemaphoreType.REGULAR, pltpu.SemaphoreType.REGULAR,
        ],
        compiler_params=pltpu.CompilerParams(
            vmem_limit_bytes=VMEM_TOP, collective_id=0, has_side_effects=True
        ),
        cost_estimate=cost(2 * 6 * two * width * units, 6e7),
        name="feed_sum",
    )(second, low, up, down)


def one_hot_rows(lens, c, block, part, rows, along):
    per = rows // block
    at = 0
    ranks = []
    for b in range((part + 1) * per):
        if b >= part * per:
            slot = lax.broadcasted_iota(jnp.int32, (1, block) if along else (block, 1), along)
            ranks.append(jnp.where(slot < lens[c, b], slot + at, -1))
        at = at + lens[c, b]
    rank = jnp.concatenate(ranks, axis=along)
    line = lax.broadcasted_iota(jnp.int32, (FILLED, rows) if along else (rows, FILLED), 1 - along)
    return jnp.where(line == rank, 1.0, 0.0).astype(BF)


def normed_rows(values, gain, shift):
    center = values - jnp.mean(values, axis=1, keepdims=True)
    inverse = lax.rsqrt(jnp.mean(center * center, axis=1, keepdims=True) + EPS)
    return center * inverse * gain + shift


def attend_gather_kernel(
    block, heads,
    lens, tokens_in, weight, output_in, norms,
    first_out, kept_out, mixed_out, middle_out, second_out,
    tok, first, weights, outputs, qkv, packed, mixed, mixed_got, middle, second,
    load_sem, send_sem, recv_sem, turn_send, turn_recv, out_sem,
):
    cells, rows, width = tok.shape
    wide = heads * HEAD_DIM
    cell = lax.axis_index("cells")
    place = lax.axis_index("chrom")
    core = place % 2

    def chrom_near(r):
        return (cell, (place // 2 + r // 2) % 2 * 2 + (core + r % 2) % 2)

    barrier = pltpu.get_barrier_semaphore()
    for r in range(1, 4):
        pl.semaphore_signal(barrier, inc=1, device_id=chrom_near(r), device_id_type=MESH)

    def load(src, dst, sem):
        copy = pltpu.make_async_copy(src, dst, sem)
        copy.start()
        return copy

    loads = [
        load(tokens_in.at[0], tok.at[0], load_sem.at[0]),
        load(tokens_in.at[1], tok.at[1], load_sem.at[1]),
        load(tokens_in.at[2], tok.at[2], load_sem.at[2]),
        load(weight, weights, load_sem.at[3]),
        load(output_in, outputs, load_sem.at[4]),
    ]
    sent, writes = [], []

    def remote(src, dst, send, recv, r):
        copy = pltpu.make_async_remote_copy(
            src_ref=src, dst_ref=dst, send_sem=send, recv_sem=recv,
            device_id=chrom_near(r), device_id_type=MESH,
        )
        copy.start()
        sent.append(copy)
        return copy

    def part_rows(r):
        return slice(r * rows, (r + 1) * rows)

    near, over, across = {}, {}, {}

    def send_over(c):
        over[c] = remote(
            first.at[c, part_rows(0)], first.at[c, part_rows(2)], send_sem.at[3 * c], recv_sem.at[3 * c], 2
        )

    for c in range(cells):
        loads[c].wait()

        def some(i, carry, c=c):
            here = pl.ds(pl.multiple_of(i * 64, 64), 64)
            first[c, here, :] = normed_rows(tok[c, here, :].astype(F32), norms[0:1, :], norms[1:2, :]).astype(BF)
            return carry

        lax.fori_loop(0, rows // 64, some, 0)
        if c == 0:
            pl.semaphore_wait(barrier, 3)
            send_over(0)
        near[c] = remote(
            first.at[c, part_rows(0)], first.at[c, part_rows(1)],
            send_sem.at[3 * c + 1], recv_sem.at[3 * c + 1], 1,
        )
    loads[3].wait()

    def project(c, r):
        qkv[c, part_rows(r), :] = jnp.dot(
            first[c, part_rows(r), :], weights[...], preferred_element_type=F32
        ).astype(BF)

    for c in range(cells):
        project(c, 0)
    for c in range(cells):
        near[c].wait_recv()
        project(c, 1)
    loads[4].wait()

    turns = {}

    def finish(c):
        for copy in turns[c]:
            copy.wait_recv()
        writes.append(load(mixed_got.at[c], mixed_out.at[c], out_sem.at[5 * c]))
        total = tok[c].astype(F32)
        for r in range(4):
            total = total + jnp.dot(
                mixed_got[c, r], outputs[r * wide : (r + 1) * wide, :], preferred_element_type=F32
            )
        middle[c] = total

        def some(i, carry):
            here = pl.ds(pl.multiple_of(i * 64, 64), 64)
            second[c, here, :] = normed_rows(middle[c, here, :], norms[2:3, :], norms[3:4, :]).astype(BF)
            return carry

        lax.fori_loop(0, rows // 64, some, 0)
        writes.append(load(middle.at[c], middle_out.at[c], out_sem.at[5 * c + 1]))
        writes.append(load(second.at[c], second_out.at[c], out_sem.at[5 * c + 2]))

    scale = LOG2E / math.sqrt(HEAD_DIM)
    ones = jnp.ones((FILLED, HEAD_DIM), BF)
    for c in range(cells):
        over[c].wait_recv()
        across[c] = remote(
            first.at[c, part_rows(2)], first.at[c, part_rows(3)],
            send_sem.at[3 * c + 2], recv_sem.at[3 * c + 2], 1,
        )
        if c + 1 < cells:
            send_over(c + 1)
        project(c, 2)
        across[c].wait_recv()
        project(c, 3)
        writes.append(load(first.at[c], first_out.at[c], out_sem.at[5 * c + 3]))
        total = None
        for r in range(4):
            part = jnp.dot(
                one_hot_rows(lens, c, block, r, rows, 1), qkv[c, part_rows(r), :], preferred_element_type=F32
            )
            total = part if total is None else total + part
        packed[c] = total.astype(BF)
        writes.append(load(packed.at[c], kept_out.at[c], out_sem.at[5 * c + 4]))
        turns[c] = []
        for r in (2, 3, 1, 0):
            for h in range(heads):
                lo = h * HEAD_DIM
                q = qkv[c, part_rows(r), lo : lo + HEAD_DIM]
                k = packed[c, :, wide + lo : wide + lo + HEAD_DIM]
                v = packed[c, :, 2 * wide + lo : 2 * wide + lo + HEAD_DIM]
                s = lax.dot_general(q, k, NT, preferred_element_type=F32)
                top = jnp.max(s, axis=1, keepdims=True) * scale
                e = jnp.exp2(s * scale - top).astype(BF)
                o = jnp.dot(e, jnp.concatenate([v, ones], axis=1), preferred_element_type=F32)
                o = (o[:, :HEAD_DIM] / o[:, HEAD_DIM:]).astype(BF)
                if r:
                    mixed[c, r, :, lo : lo + HEAD_DIM] = o
                else:
                    mixed_got[c, 0, :, lo : lo + HEAD_DIM] = o
            if r:
                n = 3 * c + r - 1
                turns[c].append(
                    remote(mixed.at[c, r], mixed_got.at[c, r], turn_send.at[n], turn_recv.at[n], r)
                )
        if c:
            finish(c - 1)
    finish(cells - 1)
    for copy in writes:
        copy.wait()
    for copy in sent:
        copy.wait_send()


def attend_gather(lens, tokens, weight, output, norms, block):
    cells, rows, width = tokens.shape
    wide = weight.shape[1] // 3
    heads = wide // HEAD_DIM
    anywhere = pl.BlockSpec(memory_space=pl.ANY)
    local = pl.BlockSpec(memory_space=pltpu.VMEM)
    dma = pltpu.SemaphoreType.DMA
    shapes = [
        jax.ShapeDtypeStruct((cells, 4 * rows, width), BF),
        jax.ShapeDtypeStruct((cells, FILLED, 3 * wide), BF),
        jax.ShapeDtypeStruct((cells, 4, rows, wide), BF),
        jax.ShapeDtypeStruct((cells, rows, width), F32),
        jax.ShapeDtypeStruct((cells, rows, width), BF),
    ]
    return pl.pallas_call(
        functools.partial(attend_gather_kernel, block, heads),
        in_specs=[smem()] + [anywhere] * 3 + [local],
        out_specs=[anywhere] * 5,
        out_shape=shapes,
        scratch_shapes=[
            pltpu.VMEM((cells, rows, width), BF),
            pltpu.VMEM((cells, 4 * rows, width), BF),
            pltpu.VMEM((width, 3 * wide), BF),
            pltpu.VMEM((width, width), BF),
            pltpu.VMEM((cells, 4 * rows, 3 * wide), BF),
            pltpu.VMEM((cells, FILLED, 3 * wide), BF),
            pltpu.VMEM((cells, 4, rows, wide), BF),
            pltpu.VMEM((cells, 4, rows, wide), BF),
            pltpu.VMEM((cells, rows, width), F32),
            pltpu.VMEM((cells, rows, width), BF),
            dma((5,)), dma((9,)), dma((9,)), dma((9,)), dma((9,)), dma((5 * cells,)),
        ],
        compiler_params=pltpu.CompilerParams(
            vmem_limit_bytes=VMEM_MAX, collective_id=2, has_side_effects=True
        ),
        cost_estimate=cost(6e10, 6e7),
        name="attend_gather",
    )(lens, tokens, weight, output, norms)


MIDDLE_CUT = 1


def middle_kernel(
    middle, back, part, cotangent, scale, mixed, output, gain,
    layer_out, low_out, g0, g1, g2, g3, output_part, sums, low_all, mixed_all,
):
    step = pl.program_id(0)
    rows = middle.shape[1]
    wide = mixed.shape[3]
    half = middle.shape[2] // 2
    place = lax.axis_index("chrom")

    @pl.when(step == 0)
    def _():
        sums[...] = jnp.zeros_like(sums)

    def some(i, carry):
        here = pl.ds(pl.multiple_of(i * 64, 64), 64)
        values = middle[0, here, :]
        layer_out[0, here, :] = (values + part[0, here, :]).astype(BF)
        center = values - jnp.mean(values, axis=1, keepdims=True)
        inverse = lax.rsqrt(jnp.mean(center * center, axis=1, keepdims=True) + EPS)
        normed = center * inverse
        grad = back[0, here, :]
        sums[2:3, :] += jnp.sum(grad * normed, axis=0, keepdims=True)
        sums[3:4, :] += jnp.sum(grad, axis=0, keepdims=True)
        scaled = grad * gain[...]
        through = inverse * (
            scaled
            - jnp.mean(scaled, axis=1, keepdims=True)
            - normed * jnp.mean(scaled * normed, axis=1, keepdims=True)
        )
        low_out[0, here, :] = (cotangent[0, here, :].astype(F32) * scale[0, here, :] + through).astype(BF)
        return carry

    lax.fori_loop(0, rows // 64, some, 0)
    spot = pl.ds(pl.multiple_of(step * rows, rows), rows)
    starts = jnp.logical_and(place == 0, step % MIDDLE_CUT == 0)
    head = jnp.where(starts, middle[0, :1, :] + part[0, :1, :], 0.0)
    sums[0:1, :] += head
    sums[1:2, :] += head * head
    for r, out in enumerate((g0, g1, g2, g3)):
        out[0] = lax.dot_general(
            low_out[0], output[r * wide : (r + 1) * wide, :], NT, preferred_element_type=F32
        ).astype(BF)
        mixed_all[r, spot, :] = mixed[0, r]
    low_all[spot, :] = low_out[0]

    @pl.when(step == pl.num_programs(0) - 1)
    def _():
        for j in range(4):
            r = (place // 2 + j // 2) % 2 * 2 + (place % 2 + j % 2) % 2
            values = lax.dot_general(
                mixed_all[r], low_all[...], TN, preferred_element_type=F32
            ).astype(BF)
            for s in range(4):
                k = 4 * j + s
                at = (k // 8, (k // 4) % 2, (k // 2) % 2, k % 2)
                for c in range(2):
                    output_part[(c,) + at] = values[s * 80 : (s + 1) * 80, c * half : (c + 1) * half]


def middle_step(middle, back, part, cotangent, scale, mixed, output, gain):
    cells, rows, width = middle.shape
    wide = mixed.shape[3]
    cut = MIDDLE_CUT
    some = rows // cut

    def one(last):
        return pl.BlockSpec((1, some, last), lambda s: (s // cut, s % cut, 0))

    heads = pl.BlockSpec((1, 4, some, wide), lambda s: (s // cut, 0, s % cut, 0))
    parted = (2, 2, 2, 2, 2, 80, width // 2)
    return pl.pallas_call(
        middle_kernel,
        grid=(cells * cut,),
        in_specs=[one(width)] * 4 + [one(1), heads, whole(output.shape), whole(gain.shape)],
        out_specs=[one(width)] * 2 + [one(wide)] * 4 + [whole(parted), whole((8, width))],
        out_shape=[jax.ShapeDtypeStruct(middle.shape, BF)] * 2
        + [jax.ShapeDtypeStruct((cells, rows, wide), BF)] * 4
        + [jax.ShapeDtypeStruct(parted, BF), jax.ShapeDtypeStruct((8, width), F32)],
        scratch_shapes=[
            pltpu.VMEM((cells * rows, width), BF),
            pltpu.VMEM((4, cells * rows, wide), BF),
        ],
        compiler_params=pltpu.CompilerParams(vmem_limit_bytes=VMEM_MAX),
        cost_estimate=cost(8 * cells * rows * width * wide * 2, 3e7),
        name="middle_step",
    )(middle, back, part, cotangent, scale, mixed, output, gain)


QUERY_ITEMS = ((0, 512, "xzh"), (512, 960, "zxh"))


def row_dot(left, right, exact_left):
    wide = right if exact_left else left
    high = wide.astype(BF)
    low = (wide - high.astype(F32)).astype(BF)
    pairs = ((left, high), (left, low)) if exact_left else ((high, right), (low, right))
    return sum(lax.dot_general(a, b, NT, preferred_element_type=F32) for a, b in pairs)


def attend_sum_kernel(
    block, heads,
    lens, g0, g1, g2, g3, kept, first_in, *refs
):
    (
        weight, up_z_in, up_y_in, out_in, down_ab_in, down_c_in, early_in, tokens_in, through_in, gain,
        tokens_out, query_out, up_z_out, up_y_out, out_out, down_out, early_out, late_out,
        grads, qkv_c, first, weights, back, moved, total, query_part,
        up_z, up_y, out_part, down_ab, down_c, down_part, got_ab, got_c,
        keep_back, got_near, got_far, got_over,
        qa1, qa2, qa3, qb1, qb2, qb3, query_last, query_got,
        uz1, uz2, uz3, up_z_last, up_z_got, uy1, uy2, uy3, up_y_last, up_y_got,
        oc1, oc2, oc3, oc4, oc5, out_last, out_got, down_got, down_last, early, early_got, late, late_got, column_sum, norm_in,
        load_sem, first_sem, turn_send, turn_recv, back_send, back_recv, sum_send, sum_recv, end_sem, norm_sem,
    ) = refs
    sources = (g0, g1, g2, g3)
    cells = kept.shape[0]
    rows = g0.shape[1]
    wide = heads * HEAD_DIM
    cell = lax.axis_index("cells")
    place = lax.axis_index("chrom")
    core = place % 2
    mine = {"c": core, "y": place // 2, "x": cell % 2, "z": (cell // 2) % 2, "h": cell // 4}

    def chrom_near(r):
        return (place // 2 + r // 2) % 2 * 2 + (core + r % 2) % 2

    near = {
        "c": (cell, chrom_near(1)),
        "y": (cell, chrom_near(2)),
        "x": (cell + 1 - 2 * mine["x"], place),
        "z": (cell + 2 - 4 * mine["z"], place),
        "h": (cell + 4 - 8 * mine["h"], place),
    }
    far = (cell, chrom_near(3))
    by_part = (None, near["c"], near["y"], far)

    barrier = pltpu.get_barrier_semaphore()
    for other in (*near.values(), far):
        pl.semaphore_signal(barrier, inc=1, device_id=other, device_id_type=MESH)

    def load(src, dst, sem):
        copy = pltpu.make_async_copy(src, dst, sem)
        copy.start()
        return copy

    def load_own(c):
        return [
            load(g0.at[c], grads.at[c, 0], load_sem.at[2 * c]),
            load(kept.at[c], qkv_c.at[c % 2], load_sem.at[2 * c + 1]),
        ]

    own_loads = {c: load_own(c) for c in range(2)}
    extra = [
        load(down_ab_in, down_ab, load_sem.at[6]),
        load(down_c_in, down_c, load_sem.at[11]),
        load(up_z_in, up_z, load_sem.at[7]),
        load(up_y_in, up_y, load_sem.at[8]),
        load(out_in, out_part, load_sem.at[9]),
        load(weight, weights, load_sem.at[10]),
    ]

    def load_first(c):
        return [load(first_in.at[c], first.at[c % 2], first_sem.at[c])]

    first_loads = {c: load_first(c) for c in range(2)}
    early_load = load(early_in, early.at[0], load_sem.at[12])
    pl.semaphore_wait(barrier, 6)

    def remote(src, dst, send, recv, device, start=True):
        copy = pltpu.make_async_remote_copy(
            src_ref=src, dst_ref=dst, send_sem=send, recv_sem=recv,
            device_id=device, device_id_type=MESH,
        )
        if start:
            copy.start()
        return copy

    sent = []

    def turn(c):
        line = []
        for r in (2, 3, 1):
            n = 3 * c + r - 1
            line.append(
                remote(sources[r].at[c], grads.at[c, r], turn_send.at[n], turn_recv.at[n], by_part[r])
            )
        sent.extend(line)
        return line

    turns = {0: turn(0)}

    sems = iter(range(64))
    items = {}

    def item(name, part, dims, stages, recvs, cols=slice(None)):
        items[name] = (part, dims, stages, recvs, cols, [next(sems) for _ in stages], {})

    item("uz", up_z, "*hxy", "xyh", (uz1, uz2, uz3))
    item("uy", up_y, "*hzx", "xzh", (uy1, uy2, uy3))
    item("o", out_part, "chzxy", "cxyzh", (oc1, oc2, oc3, oc4, oc5))
    item("da", down_ab, "z", "z", (got_ab,))
    item("dc", down_c, "y", "y", (got_c,))
    for n, (lo, hi, stages) in enumerate(QUERY_ITEMS):
        item("q%d" % n, query_part, "hzx", stages, ((qa1, qa2, qa3), (qb1, qb2, qb3))[n], slice(lo, hi))

    def view(name, s, other):
        _, dims, stages, _, cols, _, _ = items[name]
        index = [slice(None)] * len(dims)
        for t, axis in enumerate(stages[: s + 1]):
            index[dims.index(axis)] = 1 - mine[axis] if (t == s and other) else mine[axis]
        return tuple(index) + (slice(None), cols)

    def go(name, s):
        part, _, stages, recvs, _, ids, flight = items[name]
        copy = remote(
            part.at[view(name, s, True)], recvs[s],
            sum_send.at[ids[s]], sum_recv.at[ids[s]], near[stages[s]],
        )
        flight[s] = copy
        sent.append(copy)

    def end(name, s):
        part, _, stages, recvs, _, _, flight = items[name]
        flight[s].wait_recv()
        add_pieces(part, view(name, s, False), recvs[s])
        if s + 1 < len(stages):
            go(name, s + 1)

    lasts = {
        "uz": (up_z, up_z_last, up_z_got, next(sems)),
        "uy": (up_y, up_y_last, up_y_got, next(sems)),
        "o": (out_part, out_last, out_got, next(sems)),
    }

    def swap_last(name, _):
        part, last, got, sem = lasts[name]
        at = view(name, len(items[name][2]) - 1, False)
        half = part.shape[-2] // 2
        tiles = part.shape[0] if name != "o" else 1
        for t in range(tiles):
            here = (t,) + at[1:] if name != "o" else at
            values = part[here]
            for k in range(2):
                last[k, t] = values[k * half : (k + 1) * half]
        copy = remote(last.at[1 - core], got, sum_send.at[sem], sum_recv.at[sem], near["c"])
        sent.append(copy)
        items[name][6]["last"] = copy

    down_sems = (next(sems), next(sems))

    def down_far():
        return remote(
            down_part, down_got, sum_send.at[down_sems[0]], sum_recv.at[down_sems[0]], near["h"], False
        )

    def down_near():
        return remote(
            down_part.at[1 - core], down_last, sum_send.at[down_sems[1]], sum_recv.at[down_sems[1]],
            near["c"], False,
        )

    def down_start(*_):
        for k in range(2):
            half = slice(k * 160, (k + 1) * 160)
            down_part[k, :, :DOWN_CUT] = down_ab[mine["z"], half, :]
            down_part[k, :, DOWN_CUT:] = down_c[mine["y"], half, :]

        @pl.when(core != mine["h"])
        def _():
            down_far().start()

    def down_add(*_):
        @pl.when(core == mine["h"])
        def _():
            down_far().wait_recv()
            for k in range(2):
                down_part[k] = (down_part[k].astype(F32) + down_got[k].astype(F32)).astype(BF)
            down_near().start()
            down_last[...] = down_part[core]

    def down_end(*_):
        @pl.when(core != mine["h"])
        def _():
            down_far().wait_send()
            down_near().wait_recv()

        @pl.when(core == mine["h"])
        def _():
            down_near().wait_send()

    vectors = {"early": (early, early_got, 26), "late": (late, late_got, 31)}

    def vector_go(name, s):
        stack, got, sem = vectors[name]
        copy = remote(
            stack.at[s], got.at[s], sum_send.at[sem + s], sum_recv.at[sem + s], near["cyxzh"[s]]
        )
        flights[name, s] = copy
        sent.append(copy)

    def vector_end(name, s):
        stack, got, _ = vectors[name]
        flights[name, s].wait_recv()
        stack[s + 1] = stack[s] + got[s]
        if s < 4:
            vector_go(name, s + 1)

    flights = {}

    for copy in extra:
        copy.wait()
    go("uz", 0)
    go("uy", 0)
    go("o", 0)
    early_load.wait()
    vector_go("early", 0)

    near_copies, over_copies, norm_loads = {}, {}, {}

    def back_sum(c, _):
        near_copies[c][1].wait_recv()
        mid = slice(512, 768)
        first[c % 2, mid] = (first[c % 2, mid].astype(F32) + got_far[c].astype(F32)).astype(BF)
        over_copies[c] = remote(
            first.at[c % 2, mid], got_over.at[c], back_send.at[3 * c + 2], back_recv.at[3 * c + 2], near["y"]
        )
        sent.append(over_copies[c])
        norm_loads[c] = [
            load(tokens_in.at[c], norm_in, norm_sem.at[2 * c]),
            load(through_in.at[c], got_far.at[c], norm_sem.at[2 * c + 1]),
        ]

    def back_end(c, _):
        near_copies[c][0].wait_recv()
        over_copies[c].wait_recv()
        for copy in norm_loads[c]:
            copy.wait()

        def some(i, carry):
            here = pl.ds(pl.multiple_of(i * 64, 64), 64)
            values = norm_in[here, :].astype(F32)
            center = values - jnp.mean(values, axis=1, keepdims=True)
            inverse = lax.rsqrt(jnp.mean(center * center, axis=1, keepdims=True) + EPS)
            normed = center * inverse
            scaled = keep_back[c, here, :] + got_near[c, here, :].astype(F32)
            scaled = (scaled + got_over[c, here, :].astype(F32)) * gain[0:1, :]
            keep_back[c, here, :] = got_far[c, here, :].astype(F32) + inverse * (
                scaled
                - jnp.mean(scaled, axis=1, keepdims=True)
                - normed * jnp.mean(scaled * normed, axis=1, keepdims=True)
            )
            return carry

        lax.fori_loop(0, rows // 64, some, 0)
        ends.append(load(keep_back.at[c], tokens_out.at[c], end_sem.at[c]))
        if c + 2 < cells:
            for copy in (*near_copies[c], over_copies[c]):
                copy.wait_send()
                sent[:] = [other for other in sent if other is not copy]
            first_loads[c + 2] = load_first(c + 2)

    ends = []
    events = {
        (0, 0): [(end, "o", 0), (vector_end, "early", 0)],
        (0, 3): [(end, "dc", 0), (vector_end, "early", 1)],
        (0, 4): [(end, "da", 0), (down_start, 0, 0)],
        (0, 6): [(end, "uy", 0), (vector_end, "early", 2)],
        (1, 1): [(back_sum, 0, 0), (vector_end, "early", 3)],
        (1, 3): [(end, "uz", 0), (end, "uy", 1), (down_add, 0, 0)],
        (1, 5): [(end, "o", 1), (end, "uy", 2), (swap_last, "uy", 0), (vector_end, "early", 4)],
        (2, 1): [(back_end, 0, 0), (back_sum, 1, 0), (down_end, 0, 0)],
        (2, 4): [(end, "uz", 1), (end, "o", 2)],
        (2, 5): [(back_end, 1, 0)],
        (2, 6): [(back_sum, 2, 0), (vector_end, "late", 0), (end, "o", 3)],
    }

    def run(key):
        for event, a, b in events.get(key, ()):
            event(a, b)

    scale = LOG2E / math.sqrt(HEAD_DIM)
    inv_root = 1.0 / math.sqrt(HEAD_DIM)
    chunk = 256
    for c in range(cells):
        own_loads[c][0].wait()
        own_loads[c][1].wait()
        for copy in turns[c]:
            copy.wait_recv()
        if c == 0:
            go("da", 0)
            go("dc", 0)
        if c + 1 < cells:
            turns[c + 1] = turn(c + 1)
        packed = jnp.zeros((wide, FILLED), F32)
        for r in range(4):
            move = one_hot_rows(lens, c, block, r, rows, 1)
            grad = grads[c, r].astype(F32).T.astype(BF)
            packed = packed + lax.dot_general(grad, move, NT, preferred_element_type=F32)
        query_t = qkv_c[c % 2, :, :wide].astype(F32).T.astype(BF)
        key_t = qkv_c[c % 2, :, wide : 2 * wide].astype(F32).T.astype(BF)
        for h in range(heads):
            lo = h * HEAD_DIM
            k = qkv_c[c % 2, :, wide + lo : wide + lo + HEAD_DIM]
            v = qkv_c[c % 2, :, 2 * wide + lo : 2 * wide + lo + HEAD_DIM]
            kt = key_t[lo : lo + HEAD_DIM, :]
            dv = jnp.zeros((FILLED, HEAD_DIM), F32)
            dk = jnp.zeros((FILLED, HEAD_DIM), F32)
            for w in range(0, FILLED, chunk):
                qt = query_t[lo : lo + HEAD_DIM, w : w + chunk]
                s = jnp.dot(k, qt, preferred_element_type=F32)
                top = jnp.max(s, axis=0, keepdims=True) * scale
                e = jnp.exp2(s * scale - top)
                inv = 1.0 / jnp.sum(e, axis=0, keepdims=True)
                gt = (packed[lo : lo + HEAD_DIM, w : w + chunk] * inv).astype(BF)
                dp = jnp.dot(v, gt, preferred_element_type=F32)
                inner = jnp.sum(e * dp, axis=0, keepdims=True) * inv
                ds = (e * (dp - inner)).astype(BF)
                dv = dv + lax.dot_general(e.astype(BF), gt, NT, preferred_element_type=F32)
                dk = dk + lax.dot_general(ds, qt, NT, preferred_element_type=F32)
                dqt = jnp.dot(kt, ds, preferred_element_type=F32)
                back[w : w + chunk, lo : lo + HEAD_DIM] = (dqt.T * inv_root).astype(BF)
            back[:, wide + lo : wide + lo + HEAD_DIM] = (dk * inv_root).astype(BF)
            back[:, 2 * wide + lo : 2 * wide + lo + HEAD_DIM] = dv.astype(BF)
            run((c, h))
        if c + 2 < cells:
            own_loads[c + 2] = load_own(c + 2)
        for r in range(4):
            move = one_hot_rows(lens, c, block, r, rows, 0)
            moved[r * rows : (r + 1) * rows, :] = jnp.dot(
                move, back[...], preferred_element_type=F32
            ).astype(BF)
        for copy in first_loads[c]:
            copy.wait()
        ones = jnp.ones((8, 4 * rows), BF)
        part = jnp.dot(ones, moved[...], preferred_element_type=F32)
        column_sum[...] = part + column_sum[...] if c else part
        for m in range(first.shape[2] // CHUNK):
            cols = slice(m * CHUNK, (m + 1) * CHUNK)
            part = jnp.dot(first[c % 2, :, cols].T, moved[...], preferred_element_type=F32)
            if c:
                part = part + total[cols, :]
            if c < cells - 1:
                total[cols, :] = part
            else:
                product = part * weights[cols, :].astype(F32)
                late[0, :, cols] = row_dot(ones[:, : 3 * wide], product, True)
                low = part.astype(BF)
                for s in range(0, CHUNK, 32):
                    row = m * CHUNK + s
                    n = row // 160
                    query_part[n // 4, (n // 2) % 2, n % 2, row % 160 : row % 160 + 32, :] = low[s : s + 32, :]
        if c == cells - 1:
            go("q0", 0)
            go("q1", 0)
            line = lax.broadcasted_iota(jnp.int32, late.shape[1:], 0)
            late[0] = jnp.where(line == 0, late[0], row_dot(column_sum[...], weights[...], False))
            vector_go("late", 0)
        run((c, 5))
        lines = []
        for r in (3, 1, 2, 0):
            part = lax.dot_general(
                moved[r * rows : (r + 1) * rows, :], weights[...], NT, preferred_element_type=F32
            )
            if r == 0:
                keep_back[c] = part
                continue
            spot = {1: slice(0, 256), 2: slice(512, 768), 3: slice(256, 512)}[r]
            first[c % 2, spot] = part.astype(BF)
            if r != 2:
                n = 3 * c + (1 if r == 3 else 0)
                copy = remote(
                    first.at[c % 2, spot], (got_far if r == 3 else got_near).at[c],
                    back_send.at[n], back_recv.at[n], near["c"],
                )
                lines.insert(0, copy)
                sent.append(copy)
        near_copies[c] = lines
        run((c, 6))
    vector_end("late", 1)
    end("uz", 2)
    swap_last("uz", 0)
    end("q1", 0)
    end("q0", 0)
    vector_end("late", 2)
    end("o", 4)
    swap_last("o", 0)
    end("q1", 1)
    back_end(cells - 1, 0)
    end("q0", 1)
    vector_end("late", 3)
    end("q1", 2)
    end("q0", 2)
    vector_end("late", 4)
    values = query_part[mine["h"], mine["z"], mine["x"]]
    for j in range(4):
        query_last[j] = values[j * 40 : (j + 1) * 40]
    last_query = []
    for r in range(1, 4):
        sem = next(sems)
        copy = remote(
            query_last.at[chrom_near(r)], query_got.at[r], sum_send.at[sem], sum_recv.at[sem], by_part[r]
        )
        last_query.append(copy)
        sent.append(copy)
    query_got[0] = query_last[place]
    n = cells
    for name, out in (("uz", up_z_out), ("uy", up_y_out), ("o", out_out)):
        _, last, got, _ = lasts[name]
        items[name][6]["last"].wait_recv()
        ends.append(load(last.at[core], out.at[0], end_sem.at[n]))
        ends.append(load(got, out.at[1], end_sem.at[n + 1]))
        n += 2
    ends.append(load(down_last, down_out, end_sem.at[n]))
    ends.append(load(early.at[5], early_out, end_sem.at[n + 2]))
    ends.append(load(late.at[5], late_out, end_sem.at[n + 3]))
    for copy in last_query:
        copy.wait_recv()
    ends.append(load(query_got, query_out, end_sem.at[n + 1]))
    for copy in ends:
        copy.wait()
    for copy in sent:
        copy.wait_send()


def attend_sum(
    lens, grads, kept, first, weight, up_z, up_y, out_part, down_ab, down_c, early, tokens, through, gain, block
):
    cells, rows, wide = grads[0].shape
    width = first.shape[2]
    heads = wide // HEAD_DIM
    seq = 4 * rows
    anywhere = pl.BlockSpec(memory_space=pl.ANY)
    dma = pltpu.SemaphoreType.DMA
    vmem = lambda *shape: pltpu.VMEM(shape, BF)
    qa, qb = [hi - lo for lo, hi, _ in QUERY_ITEMS]
    return pl.pallas_call(
        functools.partial(attend_sum_kernel, block, heads),
        in_specs=[smem()] + [anywhere] * 15 + [pl.BlockSpec(memory_space=pltpu.VMEM)],
        out_specs=[anywhere] * 8,
        out_shape=[
            jax.ShapeDtypeStruct((cells, rows, width), F32),
            jax.ShapeDtypeStruct((4, 40, 3 * wide), BF),
            jax.ShapeDtypeStruct((2, 3, 40, TILE), BF),
            jax.ShapeDtypeStruct((2, 2, 40, TILE), BF),
            jax.ShapeDtypeStruct((2, 1, 40, width // 2), BF),
            jax.ShapeDtypeStruct((160, width), BF),
            jax.ShapeDtypeStruct((8, width), F32),
            jax.ShapeDtypeStruct((8, width), F32),
        ],
        scratch_shapes=[
            vmem(cells, 4, rows, wide),
            vmem(2, FILLED, 3 * wide),
            vmem(2, seq, width),
            vmem(width, 3 * wide),
            vmem(FILLED, 3 * wide),
            vmem(seq, 3 * wide),
            pltpu.VMEM((width, 3 * wide), F32),
            vmem(2, 2, 2, 160, 3 * wide),
            vmem(*up_z.shape), vmem(*up_y.shape), vmem(*out_part.shape), vmem(*down_ab.shape), vmem(*down_c.shape),
            vmem(2, 160, width), vmem(*down_ab.shape[1:]), vmem(*down_c.shape[1:]),
            pltpu.VMEM((cells, rows, width), F32),
            vmem(cells, rows, width), vmem(cells, rows, width), vmem(cells, rows, width),
            vmem(2, 2, 160, qa), vmem(2, 160, qa), vmem(160, qa),
            vmem(2, 2, 160, qb), vmem(2, 160, qb), vmem(160, qb),
            vmem(4, 40, 3 * wide), vmem(4, 40, 3 * wide),
            vmem(3, 2, 2, 80, TILE), vmem(3, 2, 80, TILE), vmem(3, 80, TILE),
            vmem(2, 3, 40, TILE), vmem(3, 40, TILE),
            vmem(2, 2, 2, 80, TILE), vmem(2, 2, 80, TILE), vmem(2, 80, TILE),
            vmem(2, 2, 40, TILE), vmem(2, 40, TILE),
            vmem(2, 2, 2, 2, 80, width // 2), vmem(2, 2, 2, 80, width // 2), vmem(2, 2, 80, width // 2),
            vmem(2, 80, width // 2), vmem(80, width // 2),
            vmem(2, 1, 40, width // 2), vmem(1, 40, width // 2),
            vmem(2, 160, width), vmem(160, width),
            pltpu.VMEM((6, 8, width), F32), pltpu.VMEM((5, 8, width), F32),
            pltpu.VMEM((6, 8, width), F32), pltpu.VMEM((5, 8, width), F32),
            pltpu.VMEM((8, 3 * wide), F32), vmem(rows, width),
            dma((13,)), dma((3,)), dma((9,)), dma((9,)), dma((9,)), dma((9,)), dma((36,)), dma((36,)),
            dma((16,)), dma((2 * cells,)),
        ],
        compiler_params=pltpu.CompilerParams(
            vmem_limit_bytes=VMEM_TOP, collective_id=1, has_side_effects=True
        ),
        cost_estimate=cost(8e10, 6e7),
        name="attend_sum",
    )(
        lens, *grads, kept, first, weight, up_z, up_y, out_part, down_ab, down_c, early, tokens, through, gain
    )


def swap(x, axis, mask):
    size = lax.axis_size(axis)
    return lax.ppermute(x, axis, [(i, i ^ mask) for i in range(size)])


def halve(x, dim, axis, bit):
    mine = (lax.axis_index(axis) >> bit) & 1
    send = lax.dynamic_index_in_dim(x, 1 - mine, dim, keepdims=False)
    keep = lax.dynamic_index_in_dim(x, mine, dim, keepdims=False)
    got = swap(send, axis, 1 << bit)
    return keep.astype(F32) + got.astype(F32)


def log2(n):
    return n.bit_length() - 1


def scatter_rows(x, order, names):
    names = list(names)
    for i, name in enumerate(order):
        x = halve(x.astype(BF), names.index(name), name[0], name[1])
        names.remove(name)
    return x


def sum_all(x):
    for bit in range(log2(lax.axis_size("chrom"))):
        x = x + swap(x, "chrom", 1 << bit)
    for bit in range(log2(lax.axis_size("cells"))):
        x = x + swap(x, "cells", 1 << bit)
    return x


def scatter_columns_split(x, order):
    cell_bits = log2(lax.axis_size("cells"))
    width = x.shape[1]
    names = [("cells", b) for b in reversed(range(cell_bits))] + [("chrom", 1)]
    x = x.reshape((2,) * (cell_bits + 1) + (-1, width))
    return place_columns(scatter_rows(x, order, names))


def place_columns(x):
    core = lax.axis_index("chrom") & 1
    x = x.reshape(2, -1, x.shape[-1])
    keep = lax.dynamic_index_in_dim(x, core, 0, keepdims=False)
    got = swap(lax.dynamic_index_in_dim(x, 1 - core, 0, keepdims=False).astype(BF), "chrom", 1).astype(F32)
    left = jnp.where(core == 0, keep, got)
    right = jnp.where(core == 0, got, keep)
    return jnp.concatenate([left, right], axis=1)


def scatter_rows_split(x, order):
    cell_bits = log2(lax.axis_size("cells"))
    width = x.shape[1]
    names = [("cells", b) for b in reversed(range(cell_bits - 1))] + [("chrom", 1)]
    x = x.reshape((2,) * cell_bits + (-1, width))
    return place_rows(scatter_rows(x, order, names))


def place_rows(x):
    cells = lax.axis_size("cells")
    chrom = lax.axis_size("chrom")
    core = lax.axis_index("chrom") & 1
    top = cells // 2
    high = lax.axis_index("cells") // top
    width = x.shape[1]
    pairs = []
    for cell in range(cells):
        for place in range(chrom):
            if (cell // top) != (place & 1):
                pairs.append((cell * chrom + place, (cell ^ top) * chrom + place))
    got = lax.ppermute(x.astype(BF), ("cells", "chrom"), pairs)
    x = (x.astype(F32) + got.astype(F32)).reshape(2, -1, width)
    keep = lax.dynamic_index_in_dim(x, core, 0, keepdims=False)
    send = lax.dynamic_index_in_dim(x, 1 - core, 0, keepdims=False).astype(BF)
    back = []
    for cell in range(cells):
        for place in range(chrom):
            if (cell // top) == (place & 1):
                back.append((cell * chrom + place, cell * chrom + (place ^ 1)))
    got = lax.ppermute(send, ("cells", "chrom"), back)
    return jnp.where(core == high, keep, got.astype(F32))


def feed_forward_plain(second_low, down_low, up_weight, down_weight):
    cell_bits = log2(lax.axis_size("cells"))
    core = lax.axis_index("chrom") & 1
    result_part, result_send, back_part, back_send, down_grad, up_grad = feed_forward(
        core[None].astype(jnp.int32),
        second_low,
        swap(second_low, "chrom", 1),
        down_low,
        swap(down_low, "chrom", 1),
        up_weight,
        down_weight,
    )
    second_back = back_part + swap(back_send, "chrom", 1).astype(F32)
    result_part = result_part + swap(result_send, "chrom", 1).astype(F32)
    low_bits = [("cells", b) for b in range(cell_bits - 1)]
    down_out = scatter_rows_split(down_grad, low_bits + [("chrom", 1)])
    up_out = scatter_columns_split(
        up_grad, [("chrom", 1)] + low_bits[::-1] + [("cells", cell_bits - 1)]
    )
    return second_back, result_part, down_out, up_out


def norm_rows(values, gain, shift):
    center = values - jnp.mean(values, axis=-1, keepdims=True)
    inverse = lax.rsqrt(jnp.mean(center * center, axis=-1, keepdims=True) + EPS)
    normed = center * inverse
    return (normed * gain + shift, normed, inverse)


def norm_back(grad_out, normed, inverse, gain):
    scaled = grad_out * gain
    grad_in = inverse * (
        scaled
        - jnp.mean(scaled, axis=-1, keepdims=True)
        - normed * jnp.mean(scaled * normed, axis=-1, keepdims=True)
    )
    return (grad_in, jnp.sum(grad_out * normed, axis=0), jnp.sum(grad_out, axis=0))


def contract(left, right):
    return lax.dot_general(left, right, TN, preferred_element_type=F32)


def back_through(grad, weight):
    return lax.dot_general(grad, weight, NT, preferred_element_type=F32)


def per_device(
    tokens,
    cotangent,
    block_lengths,
    group_ids,
    group_weights,
    first_gain,
    first_shift,
    query_weight,
    key_weight,
    value_weight,
    output_weight,
    second_gain,
    second_shift,
    up_weight,
    down_weight,
):
    cells_here, seq_here, width = tokens.shape
    rows = cells_here * seq_here
    parts = lax.axis_size("chrom")
    cell_bits = log2(lax.axis_size("cells"))
    seq_full = seq_here * parts
    nblocks = block_lengths.shape[1]
    block = seq_full // nblocks
    per = nblocks // parts
    wide = width // parts
    place = lax.axis_index("chrom")
    core = place & 1
    near = [place ^ r for r in range(parts)]

    valid = (jnp.arange(block)[None, None, :] < block_lengths[:, :, None]).reshape(
        cells_here, seq_full
    )
    local_valid = lax.dynamic_slice_in_dim(valid, place * seq_here, seq_here, 1)
    lens = jnp.concatenate(
        [lax.dynamic_slice_in_dim(block_lengths, n * per, per, 1) for n in near], axis=1
    )
    n_groups = group_weights.shape[0]
    cell_scale = jnp.sum(
        jnp.where(group_ids[:, None] == jnp.arange(n_groups)[None, :], group_weights[None, :], 0.0),
        axis=1,
    )

    def my_heads(weight):
        return lax.dynamic_slice_in_dim(weight, place * wide, wide, 1)

    qkv_weight = jnp.concatenate(
        [my_heads(query_weight), my_heads(key_weight), my_heads(value_weight)], axis=1
    )
    output_near = jnp.concatenate(
        [lax.dynamic_slice_in_dim(output_weight, n * wide, wide, 0) for n in near], axis=0
    )

    fused = lax.axis_size("cells") == 8 and parts == 4
    if fused:
        norms = jnp.stack([first_gain, first_shift, second_gain, second_shift])
        first_all, kept, mixed_near, middle, second_low = attend_gather(
            lens,
            tokens,
            qkv_weight,
            output_near,
            norms,
            block,
        )
        second_low = second_low.reshape(rows, width)
    else:
        flat = tokens.reshape(rows, width).astype(F32)
        first_out, first_norm, first_inv = norm_rows(flat, first_gain, first_shift)
        first_low = first_out.astype(BF).reshape(cells_here, seq_here, width)
        first_all, mixed_near, kept = [], [], []
        for c in range(cells_here):
            mine = first_low[c]
            over = swap(mine, "chrom", 2)
            first_all.append([mine, swap(mine, "chrom", 1), over, swap(over, "chrom", 1)])
        for c in range(cells_here):
            mixed, qkv_c = attend(first_all[c], lens[c], qkv_weight, block)
            kept.append(qkv_c)
            mixed_near.append(
                jnp.concatenate([mixed[0]] + [swap(mixed[r], "chrom", r) for r in range(1, parts)], axis=1)
            )
        mixed_flat = jnp.concatenate(mixed_near, axis=0)

        middle = flat + jnp.dot(mixed_flat, output_near, preferred_element_type=F32)
        second_out, second_norm, second_inv = norm_rows(middle, second_gain, second_shift)
        second_low = second_out.astype(BF)
    result_back = (
        cotangent.astype(F32)
        * cell_scale[:, None, None]
        * local_valid.astype(F32)[:, :, None]
    ).reshape(rows, width)
    down_low = result_back.astype(BF)
    low_bits = [("cells", b) for b in range(cell_bits - 1)]
    if fused:
        second_back, result_part, down_ab, down_c, up_z, up_y = feed_forward_sum(
            second_low, down_low, up_weight, down_weight
        )
    else:
        second_back, result_part, down_out, up_out = feed_forward_plain(
            second_low, down_low, up_weight, down_weight
        )
    if fused:
        cells_shape = (cells_here, seq_here, width)
        layer_out, attend_low, *rest = middle_step(
            middle,
            second_back.reshape(cells_shape),
            result_part.reshape(cells_shape),
            cotangent,
            cell_scale[:, None, None] * local_valid.astype(F32)[:, :, None],
            mixed_near,
            output_near,
            second_gain.reshape(1, width),
        )
        grads_near, output_part, early = rest[:4], rest[4], rest[5]
    else:
        result = middle + result_part
        result_cells = result.reshape(cells_here, seq_here, width)
        layer_out = result_cells.astype(BF)

        cls_rows = jnp.where(place == 0, result_cells[:, 0, :], 0.0)
        cls_total = jnp.sum(cls_rows, axis=0)
        cls_square = jnp.sum(cls_rows * cls_rows, axis=0)

        middle_ln, second_gain_grad, second_shift_grad = norm_back(
            second_back, second_norm, second_inv, second_gain
        )
        middle_back = result_back + middle_ln
        attend_low = middle_back.astype(BF)
        output_grad = contract(mixed_flat, attend_low).reshape(parts, wide, width)
        output_grad = jnp.concatenate(
            [lax.dynamic_index_in_dim(output_grad, place ^ j, 0, keepdims=False) for j in range(parts)],
            axis=0,
        )
        early = jnp.stack([cls_total, cls_square, second_gain_grad, second_shift_grad])


    if fused:
        tokens_grad, qkv_got, up_z, up_y, out_two, down_grad, early, late = attend_sum(
            lens,
            grads_near,
            kept,
            first_all,
            qkv_weight,
            up_z,
            up_y,
            output_part,
            down_ab,
            down_c,
            early,
            tokens,
            attend_low,
            norms,
            block,
        )
        late = jnp.stack([(late[0] - first_shift * late[1]) / first_gain, late[1]])
        down_out = down_grad.astype(F32)

        def both_cores(two):
            two = two.transpose(0, 2, 1, 3).reshape(2, two.shape[2], -1)
            swapped = jnp.where(core == 0, two, two[::-1])
            return jnp.concatenate([swapped[0], swapped[1]], axis=1).astype(F32)

        up_two = jnp.stack([up_z[:, 0], up_z[:, 1], up_y[:, 0], up_z[:, 2], up_y[:, 1]], axis=1)
        up_out = both_cores(up_two)
        output_out = both_cores(out_two)
        pieces = [
            lax.dynamic_index_in_dim(qkv_got, place ^ j, 0, keepdims=False).astype(F32)
            for j in range(parts)
        ]
    else:
        half_width = width // 2
        output_half = lax.dynamic_slice_in_dim(output_grad, core * half_width, half_width, 1) + swap(
            lax.dynamic_slice_in_dim(output_grad, (1 - core) * half_width, half_width, 1).astype(BF),
            "chrom",
            1,
        ).astype(F32)
        output_out = scatter_columns_split(
            output_half.astype(BF), low_bits + [("cells", cell_bits - 1), ("chrom", 1)]
        )
        mixed_back = back_through(attend_low, output_near).astype(BF)
        mixed_back = mixed_back.reshape(cells_here, seq_here, width)
        heads_back = []
        for c in range(cells_here):
            pieces = [mixed_back[c, :, r * wide : (r + 1) * wide] for r in range(parts)]
            heads_back.append(
                [pieces[0]] + [swap(pieces[r], "chrom", r) for r in range(1, parts)]
            )
        qkv_grad = None
        first_back = []
        for c in range(cells_here):
            qkv_back = attend_back(heads_back[c], lens[c], kept[c], block)
            pieces = [back_through(g, qkv_weight) for g in qkv_back]
            sent = swap(jnp.stack([pieces[1].astype(BF), pieces[3].astype(BF)]), "chrom", 1).astype(F32)
            over = swap((pieces[2] + sent[1]).astype(BF), "chrom", 2)
            first_back.append(pieces[0] + sent[0] + over.astype(F32))
            part = contract(
                jnp.concatenate(first_all[c], axis=0), jnp.concatenate(qkv_back, axis=0)
            )
            qkv_grad = part if qkv_grad is None else qkv_grad + part
        first_back = jnp.concatenate(first_back, axis=0)

        names = [("cells", b) for b in reversed(range(cell_bits))]
        qkv_sum = scatter_rows(
            qkv_grad.reshape((2,) * cell_bits + (-1, 3 * wide)),
            [("cells", b) for b in range(cell_bits)],
            names,
        ).reshape(parts, -1, 3 * wide)
        pieces = [lax.dynamic_index_in_dim(qkv_sum, near[0], 0, keepdims=False)]
        for r in range(1, parts):
            piece = lax.dynamic_index_in_dim(qkv_sum, near[r], 0, keepdims=False).astype(BF)
            pieces.append(swap(piece, "chrom", r).astype(F32))
        pieces = jnp.stack(pieces)
        pieces = [lax.dynamic_index_in_dim(pieces, place ^ j, 0, keepdims=False) for j in range(parts)]
        first_ln, first_gain_grad, first_shift_grad = norm_back(
            first_back, first_norm, first_inv, first_gain
        )
        tokens_grad = (middle_back + first_ln).reshape(cells_here, seq_here, width)
        early = sum_all(early)
        late = sum_all(jnp.stack([first_gain_grad, first_shift_grad]))
    query_out, key_out, value_out = [
        jnp.concatenate([p[:, i * wide : (i + 1) * wide] for p in pieces], axis=1) for i in range(3)
    ]

    count_cells = cells_here * lax.axis_size("cells")
    cls_mean = early[0] / count_cells
    cls_var = early[1] / count_cells - cls_mean * cls_mean
    share = width // (parts * lax.axis_size("cells"))
    start = (lax.axis_index("cells") * parts + place) * share

    def mine(vector):
        return lax.dynamic_slice_in_dim(vector, start, share, 0)

    return (
        layer_out,
        tokens_grad,
        mine(late[0]),
        mine(late[1]),
        query_out,
        key_out,
        value_out,
        output_out,
        mine(early[2]),
        mine(early[3]),
        up_out,
        down_out,
        cls_mean,
        cls_var,
    )


def solution(mesh):
    rows = P("cells", "chrom", None)
    both = ("cells", "chrom")
    in_specs = (rows, rows, P("cells", None), P("cells")) + (P(),) * 11
    out_specs = (
        (rows, rows)
        + (P(both), P(both))
        + (P(both, None),) * 4
        + (P(both), P(both))
        + (P(both, None), P(both, None))
        + (P(), P())
    )
    return jax.shard_map(
        per_device, mesh=mesh, in_specs=in_specs, out_specs=out_specs, check_vma=False
    )
```
